32 devices in a mesh: dp: 8 (over y, x, core), mp: 4 (over z).
Axes of the slice: x: 2, y: 2, z: 4, core: 2. Of those that a mesh axis runs over, the one named last changes fastest.
Arguments:
- lengths: int32 [4, 8], P(None, 'dp'), may hold values from 2 to 1024, as said below
- owners: int32 [4, 8, 1024, 1], P(None, 'dp'), may hold values from 0 to 31; in each aligned block of 256 rows (0 to 255, 256 to 511, ..., all dimensions but the last counted through in order) at most 16 rows name the same one
- item_rows: int32 [4, 8, 1024], P(None, 'dp'), may hold values from 0 to 783
- buckets: int32 [4, 8, 1024], P(None, 'dp'), may hold values from 0 to 127
- negatives: int32 [4, 512], replicated, may hold values from 0 to 25087
- table: float32 [25088, 512], P(('dp', 'mp')), may hold values from -6 to 6
- table_m: float32 [25088, 512], P(('dp', 'mp')), may hold values from -0.00030517578 to 0.00030517578
- table_v: float32 [25088, 512], P(('dp', 'mp')), may hold values from 2.0065307e-09 to 8.010864e-09
- w_f1: float32 [512, 2048], P(None, 'mp'), may hold values from -0.25 to 0.25
- f1_m: float32 [512, 2048], P(None, 'mp'), may hold values from -0.0009765625 to 0.0009765625
- f1_v: float32 [512, 2048], P(None, 'mp'), may hold values from 2.0065308e-08 to 8.010864e-08
- w_f2: float32 [512, 512], P('mp'), may hold values from -0.25 to 0.25
- f2_m: float32 [512, 512], P('mp'), may hold values from -0.0009765625 to 0.0009765625
- f2_v: float32 [512, 512], P('mp'), may hold values from 2.0065308e-08 to 8.010864e-08
- gains: float32 [3, 512], replicated, may hold values from 0.5 to 1.5
- gains_m: float32 [3, 512], replicated, may hold values from -0.0034179688 to 0.0034179688
- gains_v: float32 [3, 512], replicated, may hold values from 2.0065308e-07 to 8.010864e-07
- bias: float32 [8, 128], P('mp'), may hold values from -6 to 6
- bias_m: float32 [8, 128], P('mp'), may hold values from -0.0034179688 to 0.0034179688
- bias_v: float32 [8, 128], P('mp'), may hold values from 2.0065308e-07 to 8.010864e-07
Outputs:
- loss_sum: float32 [], replicated
- loss_count: float32 [], replicated
- grad_norm: float32 [], replicated
- table_new: float32 [25088, 512], P(('dp', 'mp'))
- table_m_new: float32 [25088, 512], P(('dp', 'mp'))
- table_v_new: float32 [25088, 512], P(('dp', 'mp'))
- table_low: bfloat16 [25088, 512], P(('dp', 'mp'))
- f1_new: float32 [512, 2048], P(None, 'mp')
- f1_m_new: float32 [512, 2048], P(None, 'mp')
- f1_v_new: float32 [512, 2048], P(None, 'mp')
- f1_low: bfloat16 [512, 2048], P(None, 'mp')
- f2_new: float32 [512, 512], P('mp')
- f2_m_new: float32 [512, 512], P('mp')
- f2_v_new: float32 [512, 512], P('mp')
- f2_low: bfloat16 [512, 512], P('mp')
- gains_new: float32 [3, 512], replicated
- gains_m_new: float32 [3, 512], replicated
- gains_v_new: float32 [3, 512], replicated
- bias_new: float32 [8, 128], P('mp')
- bias_m_new: float32 [8, 128], P('mp')
- bias_v_new: float32 [8, 128], P('mp')
The draws below stay inside these ranges and needn't reach their ends.
Inputs may be any that keep to these rules, and one draw needn't show every extreme that they name: `lengths`: in each micro-batch one history has exactly 1024 events. `owners`: counting the rows in order over all leading dimensions, in each aligned block of 256 rows (the lookups of one device) no owner appears more than 16 times; some owner appears exactly 16 times in some blocks.
All inputs are finite; a program needn't handle non-finite values.
Results may differ from the reference program's by a relative error of at most 0.0035.
The reference program's roundings to bfloat16 on the way count: a program that leaves them out, or rounds other values in their place, can miss the bound.
Values may be sent and summed in bfloat16 or wider, within the bound.
A program may use at most 320 MiB of HBM per device.

```python
import math
from functools import partial
import jax
import jax.numpy as jnp
import numpy as np
from jax import lax

H = 8
DH = 64
D = 512
NB = 128
NEG = 512
ROWS_DEV = 784
LEN = 1024
MB = 4
STEP = 10
HISTS = 8
ITEMS = 25088
LOOK_DEV = 256
CAP = 16
DEVICES = 32


def draw_lengths(key, part):
    first_key = jax.random.fold_in(key, 11)
    second_key = jax.random.fold_in(key, 12)
    spread = jax.random.randint(first_key, (MB, HISTS), 75, 101)
    index = jnp.arange(HISTS)[None, :]
    base = LEN * (HISTS + 2 * index) * spread // (3 * HISTS * 100)
    base = jnp.maximum(base, 2)
    chosen = jax.random.randint(second_key, (MB, 1), 0, HISTS)
    return jnp.where(index == chosen, LEN, base).astype(jnp.int32)


def plant(entries, own_key, least, largest):
    spot = [jax.random.randint(jax.random.fold_in(own_key, axis), (), 0, length) for axis, length in enumerate(entries.shape)]
    longest = entries.shape.index(max(entries.shape))
    beside = spot[:longest] + [(spot[longest] + 1) % entries.shape[longest]] + spot[longest + 1:]
    return entries.at[tuple(spot)].set(least).at[tuple(beside)].set(largest)


def shard_levels(key, dims, cuts, smallest, top_value):
    level = 1.0
    for dim, shards_of in cuts:
        steps = jax.random.uniform(jax.random.fold_in(jax.random.fold_in(key, 6), dim), (shards_of,), jnp.float32, smallest / len(cuts), top_value / len(cuts))
        level = level * jnp.repeat(jnp.exp(steps), dims[dim] // shards_of).reshape((-1,) + (1,) * (len(dims) - 1 - dim))
    return level


def assign_block(key, own, number, rows, count, top, bound, slope):
    sequence = jax.random.permutation(key, count)
    packed, usual = load_shares(count, rows * top, bound, slope, True), load_shares(count, rows * top, bound, slope, False)
    places = jnp.arange(count)

    def named(tallies, turn):
        used = int((tallies > 0).sum())
        fixed = max(1, used // 4)
        passed = fixed + (places - fixed + turn * (used - fixed)) % max(1, count - fixed)
        return jnp.zeros((count,), jnp.int32).at[sequence[jnp.where(places < fixed, places, passed)]].set(jnp.asarray(tallies, jnp.int32))

    tallies = jnp.where(number % 4 == 0, named(packed, number // 4), named(usual, number - number // 4 - 1))
    mixed = jax.random.permutation(jax.random.fold_in(own, 3), count)
    donor, taker = mixed[0:count // 2 * 2:2], mixed[1:count // 2 * 2:2]
    room = jnp.minimum(tallies[donor] - 1, bound - tallies[taker]) // 2
    room = jnp.where((donor == sequence[0]) | (taker == sequence[0]) | (tallies[taker] == 0), 0, jnp.maximum(room, 0))
    passed = jax.random.randint(jax.random.fold_in(own, 4), (count // 2,), 0, 1 << 20) % (room + 1)
    tallies = tallies.at[donor].add(-passed).at[taker].add(passed)
    members = jnp.searchsorted(jnp.cumsum(tallies), jnp.arange(rows * top), side="right").astype(jnp.int32)
    table = members.reshape(top, rows).T
    table = table[jax.random.permutation(jax.random.fold_in(own, 1), rows)]
    turn = jax.random.randint(jax.random.fold_in(own, 2), (rows, 1), 0, top)
    return jnp.take_along_axis(table, (jnp.arange(top)[None, :] + turn) % top, axis=1)


def load_shares(number_of, total, most, slope, full):
    weights = [(1 << 20) // math.isqrt(grade ** slope) + 1 for grade in range(1, number_of + 1)]
    largest = most if full else min(most, max(-(-total // number_of), total * weights[0] // sum(weights)))
    least = 1 if total - largest >= number_of - 1 else 0
    counts, rest = [largest] + [least] * (number_of - 1), total - largest - least * (number_of - 1)
    while rest > 0:
        movable = [i for i in range(1, number_of) if counts[i] < largest] or [i for i in range(1, number_of) if counts[i] < most]
        whole, remaining = sum([weights[i] for i in movable]), rest
        for i in movable:
            more = min(most - counts[i], max(1, remaining * weights[i] // whole), rest)
            counts[i] = counts[i] + more
            rest = rest - more
    return np.array(counts)


def normal_values(own_key, dims, scale, bound, split=(), held_as=jnp.bfloat16):
    entries = jax.random.normal(own_key, dims, jnp.float32) * scale
    if len(split) > 0:
        entries = shard_levels(own_key, dims, split, -0.22, 0.18) * entries
    return jnp.clip(entries, min=-bound, max=bound).astype(held_as)


def setup_inputs(seed: int = 0) -> dict:
    splits = jax.random.split(jax.random.key(seed), 21)
    lengths = draw_lengths(jax.random.fold_in(splits[20], 71), 0)
    owners_keys = jax.random.split(jax.random.fold_in(splits[1], 1), MB * HISTS * LEN // LOOK_DEV)
    owners_turns = jax.random.permutation(jax.random.fold_in(splits[1], 3), MB * HISTS * LEN // LOOK_DEV)
    owners = jax.vmap(lambda own, number: assign_block(jax.random.fold_in(splits[1], 2), own, number, LOOK_DEV, DEVICES, 1, CAP, 1))(owners_keys, owners_turns).reshape((MB, HISTS, LEN, 1))
    item_rows = plant(jax.random.randint(splits[2], (MB, HISTS, LEN), 0, ROWS_DEV), jax.random.fold_in(splits[2], 1), 0, ROWS_DEV - 1).astype(jnp.int32)
    buckets = plant(jax.random.randint(splits[3], (MB, HISTS, LEN), 0, NB), jax.random.fold_in(splits[3], 1), 0, NB - 1).astype(jnp.int32)
    negatives = plant(jax.random.randint(splits[4], (MB, NEG), 0, ITEMS), jax.random.fold_in(splits[4], 1), 0, ITEMS - 1).astype(jnp.int32)
    table = normal_values(splits[5], (ITEMS, D), 1.0, 6.0, ((0, 32),), jnp.float32)
    table_m = normal_values(splits[6], (ITEMS, D), (0.111 / (10 * D)), 0.00030517578, ((0, 32),), jnp.float32)
    table_v = jnp.clip(jnp.exp(math.log(8.01086397217432e-09) - 1.3843914 * jax.random.uniform(splits[7], (ITEMS, D), jnp.float32) ** shard_levels(splits[7], (ITEMS, D), ((0, 32),), -0.2, 0.2)), 2.006530719356192e-09, 8.01086397217432e-09)
    w_f1 = normal_values(splits[8], (D, 4 * D), D ** -0.5, 0.25, ((1, 4),), jnp.float32)
    f1_m = normal_values(splits[9], (D, 4 * D), (0.111 / (3.2 * D)), 0.0009765625, ((1, 4),), jnp.float32)
    f1_v = jnp.clip(jnp.exp(math.log(8.010864149810004e-08) - 1.3843914 * jax.random.uniform(splits[10], (D, 4 * D), jnp.float32) ** shard_levels(splits[10], (D, 4 * D), ((1, 4),), -0.2, 0.2)), 2.006530763765113e-08, 8.010864149810004e-08)
    w_f2 = normal_values(splits[11], (D, D), D ** -0.5, 0.25, ((0, 4),), jnp.float32)
    f2_m = normal_values(splits[12], (D, D), (0.111 / (3.2 * D)), 0.0009765625, ((0, 4),), jnp.float32)
    f2_v = jnp.clip(jnp.exp(math.log(8.010864149810004e-08) - 1.3843914 * jax.random.uniform(splits[13], (D, D), jnp.float32) ** shard_levels(splits[13], (D, D), ((0, 4),), -0.2, 0.2)), 2.006530763765113e-08, 8.010864149810004e-08)
    gains = jnp.clip(1.0 + 0.1 * jax.random.normal(splits[14], (3, D), jnp.float32), 0.5, 1.5)
    gains_m = normal_values(splits[15], (3, D), (0.111 / D), 0.0034179688, (), jnp.float32)
    gains_v = jnp.clip(jnp.exp(jax.random.uniform(splits[16], (3, D), jnp.float32, math.log(2.006530763765113e-07), math.log(8.010864007701457e-07))), 2.006530763765113e-07, 8.010864007701457e-07)
    bias = normal_values(splits[17], (H, NB), 1.5, 6.0, ((0, 4),), jnp.float32)
    bias_m = normal_values(splits[18], (H, NB), (0.111 / D), 0.0034179688, ((0, 4),), jnp.float32)
    bias_v = jnp.clip(jnp.exp(math.log(8.010864007701457e-07) - 1.3843914 * jax.random.uniform(splits[19], (H, NB), jnp.float32) ** shard_levels(splits[19], (H, NB), ((0, 4),), -0.2, 0.2)), 2.006530763765113e-07, 8.010864007701457e-07)
    return {"lengths": lengths, "owners": owners, "item_rows": item_rows, "buckets": buckets, "negatives": negatives, "table": table, "table_m": table_m, "table_v": table_v, "w_f1": w_f1, "f1_m": f1_m, "f1_v": f1_v, "w_f2": w_f2, "f2_m": f2_m, "f2_v": f2_v, "gains": gains, "gains_m": gains_m, "gains_v": gains_v, "bias": bias, "bias_m": bias_m, "bias_v": bias_v}


@jax.custom_vjp
def low(v):
    return lax.optimization_barrier(v.astype(jnp.bfloat16)).astype(jnp.float32)

@jax.custom_vjp
def low_back(v):
    return v

def low_keep(v):
    return (low(v), None)

def low_pass(kept, grad):
    return (grad,)

def back_keep(v):
    return (v, None)

def back_low(kept, grad):
    return (low(grad),)
low.defvjp(low_keep, low_pass)
low_back.defvjp(back_keep, back_low)
epsilon = 1e-06
clip_at = 1.0
beta_one = 0.9
beta_two = 0.95
adam_floor = 1e-08
highest = lax.Precision.HIGHEST

def norm_rows(values, gain):
    return values * lax.rsqrt(lax.optimization_barrier(jnp.mean(values * values, -1, keepdims=True)) + epsilon) * gain

def group_loss(table_rows, w1_low, w2_low, gains, bias, item_ids, lens, marks, neg_ids):
    count = item_ids.shape[0]
    inputs = table_rows[item_ids]
    neg_rows = table_rows[neg_ids]
    normed = low(norm_rows(inputs, gains[0]))
    hidden = low_back(jnp.einsum('gtd,df->gtf', normed, w1_low, precision=highest))
    act = jax.nn.silu(hidden).reshape(count, LEN, H, 4, DH)
    upper = act[:, :, :, 0, :].reshape(count, LEN, D)
    values = low(act[:, :, :, 1, :])
    queries = low(act[:, :, :, 2, :])
    key_rows = low(act[:, :, :, 3, :])
    onehot = (marks[..., None] == jnp.arange(NB)).astype(jnp.float32)
    key_bias = jnp.einsum('gkn,hn->ghk', onehot, bias, precision=highest)
    scores = jnp.einsum('gqhd,gkhd->ghqk', queries, key_rows, precision=highest) * DH ** (-0.5)
    scores = low_back(scores + key_bias[:, :, None, :])
    place = jnp.arange(LEN)
    causal = place[None, :] <= place[:, None]
    live = place[None, :] < lens[:, None]
    mask = causal[None, None] & live[:, None, None, :]
    weights = low(jnp.where(mask, jax.nn.silu(scores), 0.0) / (place + 1.0)[:, None])
    attended = low_back(jnp.einsum('ghqk,gkhd->gqhd', weights, values, precision=highest)).reshape(count, LEN, D)
    gated_rows = low(norm_rows(attended, gains[1]) * upper)
    branch = low_back(jnp.einsum('gtf,fd->gtd', gated_rows, w2_low, precision=highest))
    resid = inputs + branch
    output = low(norm_rows(resid, gains[2]))
    target = jnp.concatenate([inputs[:, 1:], jnp.zeros((count, 1, D), jnp.float32)], 1)
    scale = 2.0 * D ** (-0.5)
    neg_logits = low_back(jnp.einsum('gtd,nd->gtn', output, neg_rows, precision=highest) * scale)
    pos_logits = lax.optimization_barrier(jnp.sum(output * target, -1)) * scale
    top = jnp.maximum(lax.optimization_barrier(jnp.max(neg_logits, -1)), pos_logits)
    total = jnp.exp(pos_logits - top) + lax.optimization_barrier(jnp.sum(jnp.exp(neg_logits - top[..., None]), -1))
    per_row = top + jnp.log(total) - pos_logits
    valid = place[None, :] + 1 < lens[:, None]
    return jnp.sum(jnp.where(valid, per_row, 0.0))

def forward(params, item_ids, lens, marks, neg_ids):
    table, w_f1, w_f2, gains, bias = params
    table_rows = low(table)
    w1_low = low(w_f1)
    w2_low = low(w_f2)
    step_fn = jax.checkpoint(partial(group_loss, table_rows, w1_low, w2_low, gains, bias))

    def scan_step(carry, pieces):
        return (carry + step_fn(*pieces), None)
    total, unused = lax.scan(scan_step, jnp.float32(0.0), (item_ids, lens, marks, neg_ids))
    return total

def adam_step(weight, grad, first, second, rate, decay):
    first_new = beta_one * first + (1.0 - beta_one) * grad
    second_new = beta_two * second + (1.0 - beta_two) * grad * grad
    fix_one = 1.0 - beta_one ** STEP
    fix_two = 1.0 - beta_two ** STEP
    move = first_new / fix_one / (jnp.sqrt(second_new / fix_two) + adam_floor) + decay * weight
    return (weight - rate * move, first_new, second_new)

def reference(lengths, owners, item_rows, buckets, negatives, table, table_m, table_v, w_f1, f1_m, f1_v, w_f2, f2_m, f2_v, gains, gains_m, gains_v, bias, bias_m, bias_v):
    groups = MB * HISTS // 4
    item_ids = (owners[..., 0] * ROWS_DEV + item_rows).reshape(groups, 4, LEN).astype(jnp.int32)
    lens = lengths.reshape(groups, 4)
    marks = buckets.reshape(groups, 4, LEN)
    neg_ids = jnp.repeat(negatives, HISTS // 4, 0)
    params = (table, w_f1, w_f2, gains, bias)
    loss_sum, pull = jax.vjp(lambda p: forward(p, item_ids, lens, marks, neg_ids), params)
    grads = pull(jnp.float32(1.0))[0]
    loss_count = jnp.sum((jnp.arange(LEN)[None, None, :] + 1 < lengths[..., None]).astype(jnp.float32))
    squares = sum((jnp.sum(g * g) for g in grads))
    grad_norm = jnp.sqrt(squares)
    factor = jnp.minimum(1.0, clip_at / grad_norm)
    g_table, g_one, g_two, g_gains, g_bias = [g * factor for g in grads]
    t_new, t_m, t_v = adam_step(table, g_table, table_m, table_v, 0.5, 0.1)
    a_new, a_m, a_v = adam_step(w_f1, g_one, f1_m, f1_v, 0.04, 0.1)
    b_new, b_m, b_v = adam_step(w_f2, g_two, f2_m, f2_v, 0.04, 0.1)
    c_new, c_m, c_v = adam_step(gains, g_gains, gains_m, gains_v, 0.5, 0.0)
    e_new, e_m, e_v = adam_step(bias, g_bias, bias_m, bias_v, 1.0, 0.0)
    return (loss_sum, loss_count, grad_norm, t_new, t_m, t_v, t_new.astype(jnp.bfloat16), a_new, a_m, a_v, a_new.astype(jnp.bfloat16), b_new, b_m, b_v, b_new.astype(jnp.bfloat16), c_new, c_m, c_v, e_new, e_m, e_v)
```

```python
import functools

import jax
import jax.numpy as jnp
from jax import lax
from jax.experimental import pallas as pl
from jax.experimental.pallas import tpu as pltpu
from jax.sharding import PartitionSpec as P

DH = 64
D = 512
NB = 128
LEN = 1024
MB = 4
STEP = 10

TB = 256
NT = LEN // TB
HEADS = D // DH
PAIRS = HEADS // 2
WIDE = 2 * DH
CH = 16
LANES = 128
ASK = 4

epsilon = 1e-06
clip_at = 1.0
beta_one = 0.9
beta_two = 0.95
adam_floor = 1e-08
highest = lax.Precision.HIGHEST
f32 = jnp.float32
bf16 = jnp.bfloat16
MESH = pl.DeviceIdType.MESH
VM = pl.BlockSpec(memory_space=pltpu.VMEM)
LIMIT = 60 * 1024 * 1024

NN = (((1,), (0,)), ((), ()))
NT_ = (((1,), (1,)), ((), ()))
TN = (((0,), (0,)), ((), ()))


def mm(a, b, dims=NN):
    return lax.dot_general(a, b, dims, preferred_element_type=f32)


def spot(index, n_model):
    return (index // n_model, lax.rem(index, n_model))


def greet(n_every, n_model, me):
    barrier = pltpu.get_barrier_semaphore()

    def signal(i, carry):
        pl.semaphore_signal(
            barrier, inc=1, device_id=spot(lax.rem(me + i, n_every), n_model), device_id_type=MESH
        )
        return carry

    lax.fori_loop(1, n_every, signal, 0)
    pl.semaphore_wait(barrier, n_every - 1)


def fetch_kernel(
    n_data, n_model, groups, table_ref, req_ref, got_ref, asked_ref, low_ref, send_ref,
    ask_send, ask_recv, row_send, row_recv, own_sem,
):
    n_every = n_data * n_model
    slots = groups * CH
    rows_dev = table_ref.shape[0]
    me = lax.axis_index("dp") * n_model + lax.axis_index("mp")
    greet(n_every, n_model, me)

    def ask(i, carry):
        to = lax.rem(me + i, n_every)
        pltpu.make_async_remote_copy(
            src_ref=req_ref.at[to],
            dst_ref=asked_ref.at[me],
            send_sem=ask_send.at[to],
            recv_sem=ask_recv.at[me],
            device_id=spot(to, n_model),
            device_id_type=MESH,
        ).start()
        return carry

    lax.fori_loop(1, n_every, ask, 0)
    asked_ref[me] = req_ref[me]
    low_ref[...] = table_ref[...].astype(bf16)
    eye = lax.broadcasted_iota(jnp.int32, (LANES, LANES), 0) == lax.broadcasted_iota(
        jnp.int32, (LANES, LANES), 1
    )
    lane = lax.broadcasted_iota(jnp.int32, (ASK * slots, rows_dev), 1).astype(f32)

    def asked_copy(src):
        return pltpu.make_async_remote_copy(
            src_ref=req_ref.at[src],
            dst_ref=asked_ref.at[src],
            send_sem=ask_send.at[src],
            recv_sem=ask_recv.at[src],
            device_id=spot(src, n_model),
            device_id_type=MESH,
        )

    def row_copy(src, dst, to):
        return pltpu.make_async_remote_copy(
            src_ref=send_ref.at[to],
            dst_ref=got_ref.at[:, dst],
            send_sem=row_send.at[to],
            recv_sem=row_recv.at[src],
            device_id=spot(to, n_model),
            device_id_type=MESH,
        )

    def serve(first, own):
        columns = []
        for j in range(ASK):
            src = lax.rem(me + first + j, n_every)
            if not (own and j == 0):
                asked_copy(src).wait_recv()
            wanted = jnp.broadcast_to(asked_ref[src], (LANES, LANES))
            column = jnp.sum(jnp.where(eye, wanted, 0.0), axis=1, keepdims=True)
            columns.append(column[:slots])
        column = jnp.concatenate(columns, axis=0)
        hot = jnp.where(lane == column, 1.0, 0.0).astype(bf16)
        found = mm(hot, low_ref[...]).astype(bf16)
        for j in range(ASK):
            to = lax.rem(me + first + j, n_every)
            piece = found[j * slots : (j + 1) * slots].reshape(groups, CH, D)
            send_ref[to] = piece
            if own and j == 0:
                pltpu.make_async_copy(send_ref.at[to], got_ref.at[:, me], own_sem).start()
            else:
                row_copy(me, me, to).start()

    serve(0, True)

    def more(b, carry):
        serve(b * ASK, False)
        return carry

    lax.fori_loop(1, n_every // ASK, more, 0)

    def finish(i, carry):
        other = lax.rem(me + i, n_every)
        asked_copy(other).wait_send()
        row_copy(other, other, other).wait_send()
        row_copy(other, other, other).wait_recv()
        return carry

    lax.fori_loop(1, n_every, finish, 0)
    pltpu.make_async_copy(send_ref.at[me], got_ref.at[:, me], own_sem).wait()


def fetch(table, req, n_data, n_model, groups):
    n_every = n_data * n_model
    slots = groups * CH
    return pl.pallas_call(
        functools.partial(fetch_kernel, n_data, n_model, groups),
        out_shape=(
            jax.ShapeDtypeStruct((groups, n_every, CH, D), bf16),
            jax.ShapeDtypeStruct((n_every, 1, LANES), f32),
        ),
        in_specs=[VM, VM],
        out_specs=(VM, VM),
        scratch_shapes=[
            pltpu.VMEM(table.shape, bf16),
            pltpu.VMEM((n_every, groups, CH, D), bf16),
            pltpu.SemaphoreType.DMA((n_every,)),
            pltpu.SemaphoreType.DMA((n_every,)),
            pltpu.SemaphoreType.DMA((n_every,)),
            pltpu.SemaphoreType.DMA((n_every,)),
            pltpu.SemaphoreType.DMA,
        ],
        compiler_params=pltpu.CompilerParams(
            collective_id=0, has_side_effects=True, vmem_limit_bytes=LIMIT
        ),
        cost_estimate=pl.CostEstimate(
            flops=2 * n_every * slots * table.shape[0] * D,
            bytes_accessed=8 * n_every * slots * D,
            transcendentals=0,
        ),
    )(table, req)


def give_kernel(
    n_data, n_model, out_ref, pack_ref, got_ref, packs_ref, row_send, row_recv, pack_send, pack_recv, own_sem
):
    n_every = n_data * n_model
    me = lax.axis_index("dp") * n_model + lax.axis_index("mp")
    greet(n_every, n_model, me)

    def row_copy(src, dst, to):
        return pltpu.make_async_remote_copy(
            src_ref=out_ref.at[:, to],
            dst_ref=got_ref.at[dst],
            send_sem=row_send.at[to],
            recv_sem=row_recv.at[src],
            device_id=spot(to, n_model),
            device_id_type=MESH,
        )

    def pack_copy(src, dst, to):
        return pltpu.make_async_remote_copy(
            src_ref=pack_ref,
            dst_ref=packs_ref.at[dst],
            send_sem=pack_send.at[to],
            recv_sem=pack_recv.at[src],
            device_id=spot(to, n_model),
            device_id_type=MESH,
        )

    def start(i, carry):
        to = lax.rem(me + i, n_every)
        row_copy(me, me, to).start()
        pack_copy(me, me, to).start()
        return carry

    lax.fori_loop(1, n_every, start, 0)
    own = pltpu.make_async_copy(out_ref.at[:, me], got_ref.at[me], own_sem)
    own.start()
    packs_ref[me] = pack_ref[...]

    def finish(i, carry):
        other = lax.rem(me + i, n_every)
        row_copy(other, other, other).wait_send()
        row_copy(other, other, other).wait_recv()
        pack_copy(other, other, other).wait_send()
        pack_copy(other, other, other).wait_recv()
        return carry

    lax.fori_loop(1, n_every, finish, 0)
    own.wait()


def give(out, pack, n_data, n_model):
    groups, n_every = out.shape[:2]
    return pl.pallas_call(
        functools.partial(give_kernel, n_data, n_model),
        out_shape=(
            jax.ShapeDtypeStruct((n_every, groups, CH, D), bf16),
            jax.ShapeDtypeStruct((n_every,) + pack.shape, f32),
        ),
        in_specs=[VM, VM],
        out_specs=(VM, VM),
        scratch_shapes=[pltpu.SemaphoreType.DMA((n_every,))] * 4 + [pltpu.SemaphoreType.DMA],
        compiler_params=pltpu.CompilerParams(
            collective_id=1, has_side_effects=True, vmem_limit_bytes=LIMIT
        ),
        cost_estimate=pl.CostEstimate(
            flops=0, bytes_accessed=4 * out.size * 4, transcendentals=0
        ),
    )(out, pack)


def silu_parts(values):
    sigma = 0.5 + 0.5 * jnp.tanh(0.5 * values)
    return sigma, sigma * (1.0 + values * (1.0 - sigma))


def halves(tile):
    low = lax.broadcasted_iota(jnp.int32, tile.shape, 1) < DH
    zero = jnp.zeros_like(tile)
    return jnp.concatenate([jnp.where(low, tile, zero), jnp.where(low, zero, tile)], axis=0)


def beside(tile):
    half = tile.shape[0] // 2
    return jnp.concatenate([tile[:half], tile[half:]], axis=1)


def row_sum(values):
    return jnp.sum(values, axis=0, keepdims=True)


def ahead_kernel(
    group_len, got_ref, slot_ref, w1_ref, w2_ref, kb_ref, neg_ref, gains_ref, live_ref,
    x_ref, n1_ref, q_ref, k_ref, v_ref, do_ref, ghu_ref, gres_ref, gw2_ref, gneg_ref, stat_ref,
    xf_ref, hu_ref, o_ref, carry_ref,
):
    slots = got_ref.shape[1]
    gain_in = gains_ref[0:1, :]
    gain_attn = gains_ref[1:2, :]
    gain_out = gains_ref[2:3, :]

    def inputs(i, carry):
        rows = pl.ds(pl.multiple_of(i * TB, TB), TB)
        group = i * TB // group_len
        hot = (
            lax.broadcasted_iota(jnp.int32, (TB, slots), 1) == slot_ref[rows, :]
        )
        x = mm(jnp.where(hot, 1.0, 0.0).astype(bf16), got_ref[group])
        x_ref[rows, :] = x.astype(bf16)
        xf_ref[rows, :] = x
        factor = lax.rsqrt(jnp.mean(x * x, -1, keepdims=True) + epsilon)
        n1 = (x * factor * gain_in).astype(bf16)
        n1_ref[rows, :] = n1
        hu_ref[rows, :] = mm(n1, w1_ref[0], NT_)
        for c, ref in ((1, v_ref), (2, q_ref), (3, k_ref)):
            hidden = mm(n1, w1_ref[c], NT_)
            act = (hidden * silu_parts(hidden)[0]).astype(bf16)
            if c == 2:
                act = act * jnp.asarray(0.5 * DH ** (-0.5), bf16)
            for p in range(PAIRS):
                ref[p, rows, :] = act[:, p * WIDE : (p + 1) * WIDE]
        return carry

    lax.fori_loop(0, NT, inputs, 0)
    xf_ref[LEN:, :] = jnp.zeros((8, D), f32)
    carry_ref[...] = jnp.zeros_like(carry_ref)
    stat_ref[...] = jnp.zeros_like(stat_ref)
    gw2_ref[...] = jnp.zeros_like(gw2_ref)
    gneg_ref[...] = jnp.zeros_like(gneg_ref)
    scale = 2.0 * D ** (-0.5)
    in_row = lax.broadcasted_iota(jnp.int32, (2 * TB, TB), 0)
    in_col = lax.broadcasted_iota(jnp.int32, (2 * TB, TB), 1)
    causal = in_col <= lax.rem(in_row, TB)
    first_half = in_row < TB

    def block(i, carry):
        rows = pl.ds(pl.multiple_of(i * TB, TB), TB)
        place = lax.broadcasted_iota(jnp.int32, (TB, 1), 0) + i * TB
        inv = 1.0 / (place.astype(f32) + 1.0)
        inv2 = jnp.concatenate([inv, inv], axis=0)
        for p in range(PAIRS):
            q2 = halves(q_ref[p, rows, :])

            def part(j, total, masked, p=p, q2=q2):
                keys = pl.ds(pl.multiple_of(j * TB, TB), TB)
                kb = kb_ref[p, j]
                h = mm(q2, k_ref[p, keys, :], NT_) + jnp.where(first_half, kb[0:1, :], kb[1:2, :])
                w = (h + h * jnp.tanh(h)) * inv2
                if masked:
                    w = jnp.where(causal, w, 0.0)
                return total + mm(beside(w.astype(bf16)), halves(v_ref[p, keys, :]))

            total = lax.fori_loop(
                0, i, functools.partial(part, masked=False), jnp.zeros((TB, WIDE), f32)
            )
            o_ref[p] = part(i, total, True)
        o = jnp.concatenate([o_ref[p] for p in range(PAIRS)], axis=1)
        factor_attn = lax.rsqrt(jnp.mean(o * o, -1, keepdims=True) + epsilon)
        na = o * factor_attn * gain_attn
        hu = hu_ref[rows, :]
        sigma, slope = silu_parts(hu)
        upper = hu * sigma
        gated = (na * upper).astype(bf16)
        y = xf_ref[rows, :] + mm(gated, w2_ref[...])
        factor_out = lax.rsqrt(jnp.mean(y * y, -1, keepdims=True) + epsilon)
        z = (y * factor_out * gain_out).astype(bf16)
        zf = z.astype(f32)
        after = xf_ref[pl.ds(pl.multiple_of(i * TB + TB, 8), 8), :]
        last = lax.broadcasted_iota(jnp.int32, (TB, 1), 0) == TB - 1
        target = jnp.where(last, after[0:1, :], pltpu.roll(xf_ref[rows, :], TB - 1, 0))
        neg_logits = mm(z, neg_ref[...], NT_) * scale
        pos = jnp.sum(zf * target, -1, keepdims=True) * scale
        top = jnp.maximum(jnp.max(neg_logits, -1, keepdims=True), pos)
        neg_exp = jnp.exp(neg_logits - top)
        pos_exp = jnp.exp(pos - top)
        total = pos_exp + jnp.sum(neg_exp, -1, keepdims=True)
        live = live_ref[rows, :]
        per = (top + jnp.log(total) - pos) * live
        gneg = (neg_exp / total * live).astype(bf16)
        gpos = (pos_exp / total - 1.0) * live
        gz = mm(gneg, neg_ref[...]) * scale + gpos * target * scale
        gneg_ref[...] += mm(gneg, z, TN) * scale
        target_grad = gpos * zf * scale
        first = lax.broadcasted_iota(jnp.int32, (TB, 1), 0) == 0
        shifted = jnp.where(first, carry_ref[0:1, :], pltpu.roll(target_grad, 1, 0))
        carry_ref[0:1, :] = target_grad[TB - 1 : TB, :]
        scaled = gz * gain_out
        gy = factor_out * (
            scaled - y * factor_out * factor_out * jnp.mean(y * scaled, -1, keepdims=True)
        )
        gres_ref[rows, :] = gy + shifted
        low = gy.astype(bf16)
        gg = mm(low, w2_ref[...], NT_)
        gw2_ref[...] += mm(gated, low, TN)
        gnorm = gg * upper
        gup = gg * na
        og = gain_attn * gnorm
        inner = jnp.sum(o * og, -1, keepdims=True)
        go = factor_attn * (og - o * factor_attn * factor_attn * (inner / D))
        go = go.astype(bf16)
        for p in range(PAIRS):
            do_ref[p, rows, :] = go[:, p * WIDE : (p + 1) * WIDE]
        ghu_ref[rows, :] = (gup * slope).astype(bf16)
        stat_ref[1:2, :] += row_sum(gnorm * o * factor_attn)
        stat_ref[2:3, :] += row_sum(gz * y * factor_out)
        stat_ref[3:4, :] += jnp.broadcast_to(row_sum(per), (1, D))
        stat_ref[4:5, :] += jnp.broadcast_to(row_sum(live), (1, D))
        return carry

    lax.fori_loop(0, NT, block, 0)


def ahead(got, slot_col, w1, w2, kb, neg, gains, live, group_len):
    sds = jax.ShapeDtypeStruct
    pairs_shape = sds((PAIRS, LEN, WIDE), bf16)
    return pl.pallas_call(
        functools.partial(ahead_kernel, group_len),
        out_shape=(
            sds((LEN, D), bf16), sds((LEN, D), bf16),
            pairs_shape, pairs_shape, pairs_shape, pairs_shape,
            sds((LEN, D), bf16), sds((LEN, D), f32),
            sds((D, D), f32), sds(neg.shape, f32), sds((8, D), f32),
        ),
        in_specs=[VM] * 8,
        out_specs=(VM,) * 11,
        scratch_shapes=[
            pltpu.VMEM((LEN + 8, D), f32),
            pltpu.VMEM((LEN, D), f32),
            pltpu.VMEM((PAIRS, TB, WIDE), f32),
            pltpu.VMEM((8, D), f32),
        ],
        compiler_params=pltpu.CompilerParams(vmem_limit_bytes=LIMIT),
        cost_estimate=pl.CostEstimate(
            flops=60_000_000_000, bytes_accessed=20_000_000, transcendentals=6_000_000
        ),
    )(got, slot_col, w1, w2, kb, neg, gains, live)


def back_kernel(
    group_len, x_ref, n1_ref, q_ref, k_ref, v_ref, do_ref, ghu_ref, gres_ref, kb_ref, w1_ref, gains_ref,
    slot_ref, bucket_ref, out_ref, gw1_ref, stat_ref,
    gh_ref, hid_ref, kt_ref, dq_ref, dk_ref, dv_ref, bs_ref,
):
    groups, slots = out_ref.shape[:2]
    gain_in = gains_ref[0:1, :]

    def inputs(i, carry):
        rows = pl.ds(pl.multiple_of(i * TB, TB), TB)
        for c in (1, 2, 3):
            hid_ref[c - 1, rows, :] = mm(n1_ref[rows, :], w1_ref[c], NT_)
        return carry

    lax.fori_loop(0, NT, inputs, 0)
    bs_ref[...] = jnp.zeros_like(bs_ref)
    in_row = lax.broadcasted_iota(jnp.int32, (2 * TB, TB), 0)
    in_col = lax.broadcasted_iota(jnp.int32, (2 * TB, TB), 1)
    causal = lax.rem(in_row, TB) <= in_col
    ones_lane = lax.broadcasted_iota(jnp.int32, (2 * TB, LANES), 1)
    ones_half = lax.broadcasted_iota(jnp.int32, (2 * TB, LANES), 0) >= TB

    for p in range(PAIRS):
        lanes = slice(p * WIDE, (p + 1) * WIDE)
        dq_ref[...] = jnp.zeros_like(dq_ref)
        mark = jnp.where(
            ones_lane == jnp.where(ones_half, 2 * p + 1, 2 * p), 1.0, 0.0
        ).astype(bf16)

        def keys_step(j, carry, p=p, lanes=lanes, mark=mark):
            keys = pl.ds(pl.multiple_of(j * TB, TB), TB)
            k2 = halves(k_ref[p, keys, :])
            v2 = halves(v_ref[p, keys, :])
            kt = k_ref[p, keys, :].astype(f32).T
            low = lax.broadcasted_iota(jnp.int32, kt.shape, 0) < DH
            kt2 = jnp.concatenate(
                [jnp.where(low, kt, 0.0), jnp.where(low, 0.0, kt)], axis=1
            ).astype(bf16)
            kb = jnp.concatenate(
                [kb_ref[keys, 2 * p : 2 * p + 1], kb_ref[keys, 2 * p + 1 : 2 * p + 2]], axis=0
            )
            dk_ref[...] = jnp.zeros_like(dk_ref)
            dv_ref[...] = jnp.zeros_like(dv_ref)

            def part(i, masked):
                rows = pl.ds(pl.multiple_of(i * TB, TB), TB)
                q = q_ref[p, rows, :]
                do = do_ref[p, rows, :]
                place = lax.broadcasted_iota(jnp.int32, (1, TB), 1) + i * TB
                inv = 1.0 / (place.astype(f32) + 1.0)
                h = mm(k2, q, NT_) + kb
                t = jnp.tanh(h)
                m = h * t
                w = (h + m) * inv
                ds = mm(v2, do, NT_) * ((1.0 + t) * (0.5 * inv)) * (1.0 + h - m)
                if masked:
                    w = jnp.where(causal, w, 0.0)
                    ds = jnp.where(causal, ds, 0.0)
                ds = ds.astype(bf16)
                dv_ref[...] += mm(beside(w.astype(bf16)), halves(do))
                dk_ref[...] += mm(beside(ds), jnp.concatenate([halves(q), mark], axis=1))
                dq_ref[i] += mm(kt2, ds)

            part(j, True)

            def later(i, inner):
                part(i, False)
                return inner

            lax.fori_loop(j + 1, NT, later, 0)
            slope_v = silu_parts(hid_ref[0, keys, lanes])[1]
            slope_k = silu_parts(hid_ref[2, keys, lanes])[1]
            gh_ref[0, keys, lanes] = (dv_ref[...] * slope_v).astype(bf16)
            gh_ref[2, keys, lanes] = (dk_ref[:, :WIDE] * 2.0 * slope_k).astype(bf16)
            bs_ref[keys, :] += dk_ref[:, WIDE:]
            return carry

        lax.fori_loop(0, NT, keys_step, 0)
        for i in range(NT):
            rows = slice(i * TB, (i + 1) * TB)
            slope_q = silu_parts(hid_ref[1, rows, lanes])[1]
            gh_ref[1, rows, lanes] = (dq_ref[i].T * DH ** (-0.5) * slope_q).astype(bf16)

    stat_ref[...] = jnp.zeros_like(stat_ref)
    hot = jnp.where(
        lax.broadcasted_iota(jnp.int32, (LEN, NB), 1) == bucket_ref[...], 1.0, 0.0
    )
    bias_grad = lax.dot_general(bs_ref[...], hot, TN, precision=highest, preferred_element_type=f32)
    stat_ref[8:16, 0:NB] = bias_grad[0:8, :]
    gw1_ref[0] = mm(ghu_ref[...], n1_ref[...], TN)
    for c in (1, 2, 3):
        gw1_ref[c] = mm(gh_ref[c - 1], n1_ref[...], TN)
    per_group = group_len // TB

    def outputs(i, carry):
        rows = pl.ds(pl.multiple_of(i * TB, TB), TB)
        gn = mm(ghu_ref[rows, :], w1_ref[0])
        for c in (1, 2, 3):
            gn += mm(gh_ref[c - 1, rows, :], w1_ref[c])
        x = x_ref[rows, :].astype(f32)
        factor = lax.rsqrt(jnp.mean(x * x, -1, keepdims=True) + epsilon)
        scaled = gn * gain_in
        gx = factor * (scaled - x * factor * factor * jnp.mean(x * scaled, -1, keepdims=True))
        gx = (gx + gres_ref[rows, :]).astype(bf16)
        stat_ref[0:1, :] += row_sum(gn * x * factor)
        group = i // per_group
        hot = lax.broadcasted_iota(jnp.int32, (slots, TB), 0) == slot_ref[i]
        mine = mm(jnp.where(hot, 1.0, 0.0).astype(bf16), gx).astype(bf16)
        if per_group == 1:
            out_ref[group] = mine
        else:
            out_ref[group] = jnp.where(lax.rem(i, per_group) == 0, mine, out_ref[group] + mine)
        return carry

    lax.fori_loop(0, NT, outputs, 0)


def back(x, n1, q, k, v, do, ghu, gres, kb, w1, gains, slot_row, bucket, groups, slots):
    sds = jax.ShapeDtypeStruct
    return pl.pallas_call(
        functools.partial(back_kernel, LEN // groups),
        out_shape=(sds((groups, slots, D), bf16), sds(w1.shape, f32), sds((16, D), f32)),
        in_specs=[VM] * 13,
        out_specs=(VM,) * 3,
        scratch_shapes=[
            pltpu.VMEM((3, LEN, D), bf16),
            pltpu.VMEM((3, LEN, D), f32),
            pltpu.VMEM((8, LANES), f32),
            pltpu.VMEM((NT, WIDE, TB), f32),
            pltpu.VMEM((TB, WIDE + LANES), f32),
            pltpu.VMEM((TB, WIDE), f32),
            pltpu.VMEM((LEN, LANES), f32),
        ],
        compiler_params=pltpu.CompilerParams(vmem_limit_bytes=LIMIT),
        cost_estimate=pl.CostEstimate(
            flops=60_000_000_000, bytes_accessed=20_000_000, transcendentals=6_000_000
        ),
    )(x, n1, q, k, v, do, ghu, gres, kb, w1, gains, slot_row, bucket)


def adam_step(weight, grad, first, second, rate, decay):
    first_new = beta_one * first + (1.0 - beta_one) * grad
    second_new = beta_two * second + (1.0 - beta_two) * grad * grad
    fix_one = 1.0 - beta_one**STEP
    fix_two = 1.0 - beta_two**STEP
    move = first_new / fix_one / (jnp.sqrt(second_new / fix_two) + adam_floor) + decay * weight
    return (weight - rate * move, first_new, second_new)


def pick(array, index):
    return lax.dynamic_index_in_dim(array, index, 0, keepdims=False)


def per_device(
    lengths, owners, item_rows, buckets, negatives, table, table_m, table_v, w_f1, f1_m, f1_v,
    w_f2, f2_m, f2_v, gains, gains_m, gains_v, bias, bias_m, bias_v,
):
    n_model = lax.axis_size("mp")
    n_data = lax.axis_size("dp")
    n_every = n_model * n_data
    device_at = lax.axis_index(("dp", "mp"))
    model_at = lax.axis_index("mp")
    rows_dev = table.shape[0]
    copies = n_model // MB
    micro = model_at // copies
    lead = (lax.rem(model_at, copies) == 0).astype(f32)
    look = LEN // n_model
    cap = max(2, 2 * look // n_every)
    group_len = look * max(1, CH // cap)
    groups = LEN // group_len
    slots = n_every * CH
    heads_dev = bias.shape[0]
    fw = heads_dev * DH

    owner = pick(owners, micro).reshape(groups, group_len)
    local = pick(item_rows, micro).reshape(groups, group_len)
    bucket = pick(buckets, micro).reshape(LEN)
    length = pick(lengths, micro)[0]
    owner_hot = (owner[..., None] == jnp.arange(n_every)).astype(bf16)
    spots = jnp.arange(group_len)
    earlier = (spots[None, :] < spots[:, None]).astype(bf16)
    before = jnp.einsum("ij,gjn->gin", earlier, owner_hot, preferred_element_type=f32)
    rank = jnp.sum(before * owner_hot.astype(f32), -1)
    slot = owner * CH + rank.astype(jnp.int32)
    slot_hot = (slot[:, None, :] == jnp.arange(slots)[None, :, None]).astype(bf16)
    marked = local + 1
    digits = jnp.stack([marked // 32, marked % 32], -1).astype(bf16)
    found = jnp.einsum("gse,gev->gsv", slot_hot, digits, preferred_element_type=f32)
    want = (found[..., 0] * 32.0 + found[..., 1] - 1.0).reshape(groups, n_every, CH)
    want = want.transpose(1, 0, 2).reshape(n_every, 1, groups * CH)
    want = jnp.pad(want, ((0, 0), (0, 0), (0, LANES - groups * CH)), constant_values=-1.0)

    w1_mine = w_f1.astype(bf16).T
    weights = jnp.concatenate([w1_mine, w_f2.astype(bf16)], 0)
    every = lax.all_gather(weights, "mp", axis=0)
    w1 = every[:, : 4 * fw].reshape(n_model, heads_dev, 4, DH, D)
    w1 = w1.transpose(2, 0, 1, 3, 4).reshape(4, D, D)
    w2 = every[:, 4 * fw :].reshape(D, D)
    bias_all = lax.all_gather(bias, "mp", axis=0, tiled=True)
    bucket_hot = (bucket[:, None] == jnp.arange(NB)).astype(f32)
    key_bias = jnp.einsum("kn,hn->kh", bucket_hot, bias_all, precision=highest)
    in_length = jnp.arange(LEN) < length
    key_bias = jnp.where(in_length[:, None], 0.5 * key_bias, -1e30)
    kb_col = key_bias
    kb_row = key_bias.reshape(NT, TB, PAIRS, 2).transpose(2, 0, 3, 1)
    live = ((jnp.arange(LEN) + 1 < length).astype(f32) * lead)[:, None]

    neg_ids = negatives.reshape(-1)
    neg_mine = neg_ids // rows_dev == device_at
    neg_local = jnp.where(neg_mine, neg_ids % rows_dev, -1)
    neg_hot = (neg_local[:, None] == jnp.arange(rows_dev)).astype(bf16)
    neg_term = jnp.dot(neg_hot, table.astype(bf16), preferred_element_type=f32).astype(bf16)
    neg_all = lax.psum(neg_term, ("dp", "mp"))
    neg = pick(neg_all.reshape(MB, -1, D), micro)

    got, asked = fetch(table, want, n_data, n_model, groups)
    got = got.reshape(groups, slots, D)

    x, n1, q, k, v, do, ghu, gres, gw2, gneg, stat_a = ahead(
        got, slot.reshape(LEN, 1), w1, w2, kb_row, neg, gains, live, group_len
    )
    out, gw1, stat_b = back(
        x, n1, q, k, v, do, ghu, gres, kb_col, w1, gains,
        slot.reshape(NT, 1, TB), bucket.reshape(LEN, 1), groups, slots,
    )
    pack = jnp.concatenate([stat_b[0:1], stat_a[1:5], stat_b[8:16]], 0)
    pack = jnp.pad(pack, ((0, 3), (0, 0)))
    incoming, packs = give(out.reshape(groups, n_every, CH, D), pack, n_data, n_model)

    gneg_sum = lax.psum_scatter(gneg, "dp", scatter_dimension=0, tiled=True)
    gneg_all = lax.all_gather(gneg_sum.astype(bf16), ("dp", "mp"), axis=0)
    rows_neg = gneg.shape[0] // n_data
    gneg_all = gneg_all.reshape(n_data, MB, copies, rows_neg, D)[:, :, 0]
    gneg_all = gneg_all.transpose(1, 0, 2, 3).reshape(-1, D)
    grad_two = lax.psum(
        lax.psum_scatter(gw2, "mp", scatter_dimension=0, tiled=True), "dp"
    )
    gw1 = gw1.reshape(4, n_model, fw, D)
    grad_one = lax.psum(lax.psum_scatter(gw1, "mp", scatter_dimension=1, tiled=True), "dp")
    grad_one = grad_one.reshape(4, heads_dev, DH, D).transpose(3, 1, 0, 2).reshape(D, 4 * fw)

    sums = jnp.sum(packs, 0)
    gain_grad = sums[0:3]
    loss_sum = sums[3, 0]
    loss_count = sums[4, 0]
    grad_bias = lax.dynamic_slice_in_dim(sums[5:13, :NB], model_at * heads_dev, heads_dev)

    asked_flat = asked[:, 0, : groups * CH].reshape(-1)
    table_at = jnp.arange(rows_dev)
    hot_rows = (table_at[:, None].astype(f32) == asked_flat[None, :]).astype(bf16)
    table_grad = jnp.dot(hot_rows, incoming.reshape(-1, D), preferred_element_type=f32)
    hot_neg = (table_at[:, None] == neg_local[None, :]).astype(bf16)
    table_grad = table_grad + jnp.dot(hot_neg, gneg_all, preferred_element_type=f32)

    local = jnp.sum(table_grad * table_grad)
    dense = jnp.sum(grad_one * grad_one) + jnp.sum(grad_two * grad_two) + jnp.sum(grad_bias * grad_bias)
    local = local + jnp.where(lax.axis_index("dp") == 0, dense, 0.0)
    local = local + jnp.where(device_at == 0, jnp.sum(gain_grad * gain_grad), 0.0)
    grad_norm = jnp.sqrt(lax.psum(local, ("dp", "mp")))
    factor = jnp.minimum(1.0, clip_at / grad_norm)
    t_new, t_first, t_second = adam_step(table, table_grad * factor, table_m, table_v, 0.5, 0.1)
    a_new, a_first, a_second = adam_step(w_f1, grad_one * factor, f1_m, f1_v, 0.04, 0.1)
    b_new, b_first, b_second = adam_step(w_f2, grad_two * factor, f2_m, f2_v, 0.04, 0.1)
    c_new, c_first, c_second = adam_step(gains, gain_grad * factor, gains_m, gains_v, 0.5, 0.0)
    e_new, e_first, e_second = adam_step(bias, grad_bias * factor, bias_m, bias_v, 1.0, 0.0)
    return (
        loss_sum, loss_count, grad_norm,
        t_new, t_first, t_second, t_new.astype(bf16),
        a_new, a_first, a_second, a_new.astype(bf16),
        b_new, b_first, b_second, b_new.astype(bf16),
        c_new, c_first, c_second,
        e_new, e_first, e_second,
    )


def solution(mesh):
    rows, cols = P(("dp", "mp"), None), P(None, "mp")
    heads = P("mp", None)
    in_specs = (
        P(None, "dp"), P(None, "dp", None, None), P(None, "dp", None), P(None, "dp", None), P(),
        rows, rows, rows, cols, cols, cols, heads, heads, heads, P(), P(), P(), heads, heads, heads,
    )
    out_specs = (
        P(), P(), P(), rows, rows, rows, rows, cols, cols, cols, cols,
        heads, heads, heads, heads, P(), P(), P(), heads, heads, heads,
    )
    return jax.shard_map(
        per_device, mesh=mesh, in_specs=in_specs, out_specs=out_specs, check_vma=False
    )
```

```python
import functools

import jax
import jax.numpy as jnp
from jax import lax
from jax.experimental import pallas as pl
from jax.experimental.pallas import tpu as pltpu
from jax.sharding import PartitionSpec as P

DH = 64
D = 512
NB = 128
LEN = 1024
MB = 4
STEP = 10

TB = 256
NT = LEN // TB
HEADS = D // DH
PAIRS = HEADS // 2
WIDE = 2 * DH
CH = 16
LANES = 128
ASK = 4

epsilon = 1e-06
clip_at = 1.0
beta_one = 0.9
beta_two = 0.95
adam_floor = 1e-08
highest = lax.Precision.HIGHEST
f32 = jnp.float32
bf16 = jnp.bfloat16
MESH = pl.DeviceIdType.MESH
VM = pl.BlockSpec(memory_space=pltpu.VMEM)
LIMIT = 60 * 1024 * 1024

NN = (((1,), (0,)), ((), ()))
NT_ = (((1,), (1,)), ((), ()))
TN = (((0,), (0,)), ((), ()))


def mm(a, b, dims=NN):
    return lax.dot_general(a, b, dims, preferred_element_type=f32)


def spot(index, n_model):
    return (index // n_model, lax.rem(index, n_model))


def cross(rows):
    lane = lax.broadcasted_iota(jnp.int32, (LANES, LANES), 1)
    eye = lax.broadcasted_iota(jnp.int32, (LANES, LANES), 0) == lane
    spread = jnp.broadcast_to(rows, (LANES, LANES))
    return jnp.sum(jnp.where(eye, spread, 0.0), axis=1, keepdims=True)


def remote(src, dst, send_sem, recv_sem, to):
    return pltpu.make_async_remote_copy(
        src_ref=src,
        dst_ref=dst,
        send_sem=send_sem,
        recv_sem=recv_sem,
        device_id=to,
        device_id_type=MESH,
    )


class Sizes:
    def __init__(self, n_data, n_model, heads_dev, rows_dev, negs):
        self.n_data, self.n_model, self.heads_dev, self.rows_dev = n_data, n_model, heads_dev, rows_dev
        self.n_every = n_data * n_model
        self.copies = n_model // MB
        look = LEN // n_model
        cap = max(2, 2 * look // self.n_every)
        self.group_len = look * max(1, CH // cap)
        self.groups = LEN // self.group_len
        self.slots = self.n_every * CH
        self.fw = heads_dev * DH
        self.half = n_data // 2
        self.r1 = 4 * self.fw // n_data
        self.r2 = self.fw // n_data
        self.r2p = -(-self.r2 // 16) * 16
        self.rw = self.r1 + self.r2p
        self.rn = negs // n_data
        self.ra = n_model * self.r2p + self.rn
        self.npp = n_model // PAIRS

    def order(self, d):
        return (d % 2) * self.half + d // 2

    def block(self, d):
        flat = d * self.r1
        return flat // (4 * DH), flat % (4 * DH) // DH, flat % DH


def silu_parts(values):
    sigma = 0.5 + 0.5 * jnp.tanh(0.5 * values)
    return sigma, sigma * (1.0 + values * (1.0 - sigma))


def halves(tile):
    low = lax.broadcasted_iota(jnp.int32, tile.shape, 1) < DH
    zero = jnp.zeros_like(tile)
    return jnp.concatenate([jnp.where(low, tile, zero), jnp.where(low, zero, tile)], axis=0)


def beside(tile):
    half = tile.shape[0] // 2
    return jnp.concatenate([tile[:half], tile[half:]], axis=1)


def row_sum(values):
    return jnp.sum(values, axis=0, keepdims=True)


def place_weights(z, w_ref, w1_ref, w2_ref):
    for d in range(z.n_data):
        head, part, first = z.block(d)
        for k in range(z.n_model):
            at = k * z.fw + head * DH + first
            w1_ref[part, at : at + z.r1, :] = w_ref[z.order(d), k, 0 : z.r1, :]
            if w2_ref is not None:
                at = k * z.fw + d * z.r2
                w2_ref[at : at + z.r2, :] = w_ref[z.order(d), k, z.r1 : z.r1 + z.r2, :]


def key_bias(bias_ref, bucket_ref, length):
    table = jnp.sum(bias_ref[...], axis=0)
    hot = jnp.where(
        lax.broadcasted_iota(jnp.int32, (NB, LEN), 0) == bucket_ref[...], 1.0, 0.0
    )
    rows = lax.dot_general(table, hot, NN, precision=highest, preferred_element_type=f32)
    inside = lax.broadcasted_iota(jnp.int32, (8, LEN), 1) < length
    return jnp.where(inside, 0.5 * rows, -1e30)


def front_kernel(
    z, len_ref, table_ref, f1_ref, f2_ref, bias_ref, owner_ref, local_ref, ids_ref, bucket_ref, gains_ref,
    asked_ref, slot_ref, w_ref, bias_all_ref,
    x_ref, n1o_ref, q_ref, k_ref, v_ref, do_ref, ghu_ref, gres_ref, ga_ref, stat_ref,
    low_ref, req_ref, send_ref, got_ref, t2_ref, n1_ref, n2_ref, n3_ref, acc_ref, plane_ref, neg_ref,
    xf_ref, hu_ref, o_ref, carry_ref, kb_ref, w1_ref, w2_ref, gw2_ref, gneg_ref,
    ask_send, ask_recv, row_send, row_recv,
    wz_send, wz_recv, wc_send, wc_recv, wp_send, wp_recv, bz_send, bz_recv,
    n1_send, n1_recv, n2_send, n2_recv, n3_send, n3_recv, n4_send, n4_recv, n5_send, n5_recv,
):
    n_every, n_model, half = z.n_every, z.n_model, z.half
    mine = z.groups * CH
    d = lax.axis_index("dp")
    k = lax.axis_index("mp")
    me = d * n_model + k
    side = lax.rem(d, 2)
    chip = d // 2
    here = side * half + chip
    other = d + 1 - 2 * side
    barrier = pltpu.get_barrier_semaphore()

    def signal(i, carry):
        to = spot(lax.rem(me + i, n_every), n_model)
        pl.semaphore_signal(barrier, inc=1, device_id=to, device_id_type=MESH)
        return carry

    lax.fori_loop(1, n_every, signal, 0)

    micro = k // z.copies
    owner_row = owner_ref[micro].astype(f32)
    value_row = local_ref[micro].astype(f32) + 1.0
    high_row = jnp.floor(value_row * (1.0 / 32.0))
    low_row = value_row - 32.0 * high_row
    length = z.group_len
    earlier = jnp.where(
        lax.broadcasted_iota(jnp.int32, (length, length), 0)
        < lax.broadcasted_iota(jnp.int32, (length, length), 1), 1.0, 0.0
    ).astype(bf16)
    pieces = []
    for g in range(z.groups):
        lanes = slice(g * length, (g + 1) * length)
        own = owner_row[:, lanes]
        owner_at = lax.broadcasted_iota(jnp.int32, (n_every, length), 0).astype(f32)
        hot = jnp.where(owner_at == own, 1.0, 0.0)
        rank = row_sum(mm(hot.astype(bf16), earlier) * hot)
        place = own * CH + rank
        for b in range(length // TB):
            slot_ref[g * (length // TB) + b] = place[:, b * TB : (b + 1) * TB]
        ranks = lax.broadcasted_iota(jnp.int32, (CH, length), 0).astype(f32)
        rank_hot = jnp.where(ranks == rank, 1.0, 0.0).astype(bf16)
        high = mm((hot * high_row[:, lanes]).astype(bf16), rank_hot, NT_)
        lower = mm((hot * low_row[:, lanes]).astype(bf16), rank_hot, NT_)
        pieces.append(high * 32.0 + lower - 1.0)
    pieces.append(jnp.full((n_every, LANES - mine), -1.0, f32))
    wanted = jnp.concatenate(pieces, axis=1)
    for o in range(n_every):
        req_ref[o] = wanted[o : o + 1]

    pl.semaphore_wait(barrier, n_every - 1)

    def ask_copy(src, dst, to):
        return remote(
            req_ref.at[to], asked_ref.at[dst], ask_send.at[to], ask_recv.at[src], spot(to, n_model)
        )

    def ask(i, carry):
        to = lax.rem(me + i, n_every)
        ask_copy(me, me, to).start()
        return carry

    lax.fori_loop(1, n_every, ask, 0)
    asked_ref[me] = req_ref[me]

    take = (
        lax.broadcasted_iota(jnp.int32, (z.r1, 4 * z.fw), 1)
        == lax.broadcasted_iota(jnp.int32, (z.r1, 4 * z.fw), 0) + d * z.r1
    )
    w_ref[here, k, 0 : z.r1, :] = mm(
        jnp.where(take, 1.0, 0.0).astype(bf16), f1_ref[...].astype(bf16), NT_
    ).astype(bf16)
    take = (
        lax.broadcasted_iota(jnp.int32, (z.r2p, z.fw), 1)
        == lax.broadcasted_iota(jnp.int32, (z.r2p, z.fw), 0) + d * z.r2
    )
    w_ref[here, k, z.r1 :, :] = mm(
        jnp.where(take, 1.0, 0.0).astype(bf16), f2_ref[...].astype(bf16)
    ).astype(bf16)
    bias_all_ref[k] = bias_ref[...]

    def wz_copy(i, at, to):
        return remote(
            w_ref.at[here, at], w_ref.at[here, at], wz_send.at[i], wz_recv.at[at], (d, to)
        )

    def bz_copy(i, at, to):
        return remote(bias_ref, bias_all_ref.at[at], bz_send.at[i], bz_recv.at[at], (d, to))

    for i in range(1, n_model):
        to = lax.rem(k + i, n_model)
        wz_copy(i, k, to).start()
        bz_copy(i, k, to).start()
    low_ref[...] = table_ref[...].astype(bf16)

    def row_copy(g, src, dst, to):
        return remote(
            send_ref.at[g, to], got_ref.at[g, dst], row_send.at[g, to], row_recv.at[g, src],
            spot(to, n_model),
        )

    def asked_all(i, carry):
        src = lax.rem(me + i, n_every)
        ask_copy(src, src, src).wait_recv()
        return carry

    lax.fori_loop(1, n_every, asked_all, 0)
    asked = asked_ref[...].reshape(n_every, LANES) + 1.0
    asked_high = jnp.floor(asked * (1.0 / 32.0))
    asked_low = (asked - 32.0 * asked_high).astype(bf16)
    asked_high = asked_high.astype(bf16)
    per = min(TB // CH, n_every)
    spread = jnp.where(
        lax.broadcasted_iota(jnp.int32, (per * CH, CH), 1)
        == lax.rem(lax.broadcasted_iota(jnp.int32, (per * CH, CH), 0), CH), 1.0, 0.0
    ).astype(bf16)
    turn = lax.broadcasted_iota(jnp.int32, (per * CH, n_every), 0) // CH
    asker = lax.broadcasted_iota(jnp.int32, (per * CH, n_every), 1)
    lane = lax.broadcasted_iota(jnp.int32, (per * CH, z.rows_dev), 1).astype(f32)

    def serve(g):
        lanes = slice(g * CH, (g + 1) * CH)
        for b in range(n_every // per):
            at = mm(spread, asked_high[:, lanes], NT_) * 32.0 + mm(spread, asked_low[:, lanes], NT_)
            at = jnp.where(asker == turn + b * per, at, 0.0)
            column = jnp.sum(at, axis=1, keepdims=True) - 1.0
            hot = jnp.where(lane == column, 1.0, 0.0).astype(bf16)
            found = mm(hot, low_ref[...]).astype(bf16)
            send_ref[g, b * per : (b + 1) * per] = found.reshape(per, CH, D)
        got_ref[g, me] = send_ref[g, me]

    def send_group(g):
        def send(i, carry):
            row_copy(g, me, me, lax.rem(me + i, n_every)).start()
            return carry

        lax.fori_loop(1, n_every, send, 0)

    def release(g):
        def follow(i, carry):
            at = lax.rem(me + i, n_every)
            row_copy(g - 1, at, at, at).wait_send()
            row_copy(g, me, me, at).start()
            return carry

        lax.fori_loop(1, n_every, follow, 0)

    serve(0)
    send_group(0)

    per_side = half * MB * z.rn
    span = MB * z.rn
    n_lane = lax.broadcasted_iota(jnp.int32, (TB, z.rows_dev), 1).astype(f32)

    def negatives(i, carry, first):
        at = first * (per_side // TB) + i
        columns = [cross(ids_ref[at * (TB // LANES) + j]) for j in range(TB // LANES)]
        column = jnp.concatenate(columns, axis=0) - (me * z.rows_dev).astype(f32)
        hot = jnp.where(n_lane == column, 1.0, 0.0).astype(bf16)
        t2_ref[first, pl.ds(pl.multiple_of(i * TB, TB), TB), :] = mm(hot, low_ref[...]).astype(bf16)
        return carry

    def wc_copy(i, at, to):
        return remote(
            w_ref.at[at], w_ref.at[at], wc_send.at[i], wc_recv.at[at], (2 * to + side, k)
        )

    def wp_copy(at):
        return remote(w_ref.at[at], w_ref.at[at], wp_send.at[at], wp_recv.at[at], (other, k))

    n1_copy = remote(t2_ref.at[1 - side], n1_ref, n1_send, n1_recv, (other, k))

    def n2_copy(i, at, to):
        return remote(
            acc_ref.at[pl.ds(pl.multiple_of(to * span, 16), span)], n2_ref.at[at],
            n2_send.at[i], n2_recv.at[at], (2 * to + side, k),
        )

    def n3_copy(i, at, to):
        return remote(
            plane_ref.at[to // z.copies], n3_ref.at[at], n3_send.at[i], n3_recv.at[at], (d, to)
        )

    def n4_copy(i, at, to):
        return remote(
            neg_ref.at[at], neg_ref.at[at], n4_send.at[i], n4_recv.at[at], (2 * to + side, k)
        )

    def n5_copy(at):
        return remote(neg_ref.at[at], neg_ref.at[at], n5_send.at[at], n5_recv.at[at], (other, k))

    for i in range(1, n_model):
        wz_copy(i, lax.rem(k + i, n_model), k).wait_recv()
    for i in range(1, half):
        wc_copy(i, here, lax.rem(chip + i, half)).start()
    wp_copy(here).start()
    lax.fori_loop(0, per_side // TB, functools.partial(negatives, first=1 - side), 0)
    n1_copy.start()
    lax.fori_loop(0, per_side // TB, functools.partial(negatives, first=side), 0)
    if z.groups > 1:
        serve(1)
    n1_copy.wait_recv()
    acc_ref[...] = t2_ref[side] + n1_ref[...]
    for i in range(1, half):
        n2_copy(i, chip, lax.rem(chip + i, half)).start()
    for g in range(2, z.groups):
        serve(g)

    length = len_ref[0]
    lead = len_ref[1]
    gain_in = gains_ref[0:1, :]
    gain_attn = gains_ref[1:2, :]
    gain_out = gains_ref[2:3, :]
    for i in range(1, n_model):
        at = lax.rem(k + i, n_model)
        bz_copy(i, at, k).wait_recv()
    kb = key_bias(bias_all_ref, bucket_ref, length)
    for j in range(NT):
        kb_ref[j] = kb[:, j * TB : (j + 1) * TB]
    xf_ref[LEN:, :] = jnp.zeros((8, D), f32)
    carry_ref[...] = jnp.zeros_like(carry_ref)
    stat_ref[...] = jnp.zeros_like(stat_ref)
    gw2_ref[...] = jnp.zeros_like(gw2_ref)
    gneg_ref[...] = jnp.zeros_like(gneg_ref)
    if z.groups > 1:
        release(1)
    for i in range(1, half):
        from_chip = lax.rem(chip + i, half)
        wc_copy(i, side * half + from_chip, chip).wait_recv()
        wp_copy(side * half + from_chip).start()
    for g in range(2, min(3, z.groups)):
        release(g)
    for i in range(half):
        wp_copy((1 - side) * half + i).wait_recv()
    place_weights(z, w_ref, w1_ref, w2_ref)

    def neg_one():
        total = acc_ref[pl.ds(pl.multiple_of(chip * span, 16), span), :]
        for i in range(1, half):
            from_chip = lax.rem(chip + i, half)
            n2_copy(i, from_chip, chip).wait_recv()
            total = total + n2_ref[from_chip]
        plane_ref[...] = total.reshape(MB, z.rn, D)
        for i in range(1, n_model):
            n3_copy(i, k, lax.rem(k + i, n_model)).start()

    def neg_two():
        total = plane_ref[micro]
        for i in range(1, n_model):
            at = lax.rem(k + i, n_model)
            n3_copy(i, at, k).wait_recv()
            total = total + n3_ref[at]
        neg_ref[here] = total
        for i in range(1, half):
            n4_copy(i, here, lax.rem(chip + i, half)).start()
        n5_copy(here).start()

    def neg_three():
        for i in range(1, half):
            at = side * half + lax.rem(chip + i, half)
            n4_copy(i, at, chip).wait_recv()
            n5_copy(at).start()

    def neg_four():
        for i in range(half):
            n5_copy((1 - side) * half + i).wait_recv()

    slots = z.slots

    def arrive(g):
        def wait(i, carry):
            at = lax.rem(me + i, n_every)
            row_copy(g, at, at, at).wait_recv()
            return carry

        lax.fori_loop(1, n_every, wait, 0)

    def inputs(i):
        rows = pl.ds(pl.multiple_of(i * TB, TB), TB)
        hot = lax.broadcasted_iota(jnp.int32, (slots, TB), 0).astype(f32) == slot_ref[i]
        found = got_ref[i * TB // z.group_len]
        x = mm(jnp.where(hot, 1.0, 0.0).astype(bf16), found.reshape(slots, D), TN)
        x_ref[rows, :] = x.astype(bf16)
        xf_ref[rows, :] = x
        factor = lax.rsqrt(jnp.mean(x * x, -1, keepdims=True) + epsilon)
        n1 = (x * factor * gain_in).astype(bf16)
        n1o_ref[rows, :] = n1
        hu_ref[rows, :] = mm(n1, w1_ref[0], NT_)
        for c, ref in ((1, v_ref), (2, q_ref), (3, k_ref)):
            hidden = mm(n1, w1_ref[c], NT_)
            act = (hidden * silu_parts(hidden)[0]).astype(bf16)
            if c == 2:
                act = act * jnp.asarray(0.5 * DH ** (-0.5), bf16)
            for p in range(PAIRS):
                ref[p, rows, :] = act[:, p * WIDE : (p + 1) * WIDE]

    scale = 2.0 * D ** (-0.5)
    in_row = lax.broadcasted_iota(jnp.int32, (2 * TB, TB), 0)
    in_col = lax.broadcasted_iota(jnp.int32, (2 * TB, TB), 1)
    causal = in_col <= lax.rem(in_row, TB)
    first_half = in_row < TB

    def attend(i):
        rows = pl.ds(pl.multiple_of(i * TB, TB), TB)
        place = lax.broadcasted_iota(jnp.int32, (TB, 1), 0) + i * TB
        inv = 1.0 / (place.astype(f32) + 1.0)
        inv2 = jnp.concatenate([inv, inv], axis=0)
        for p in range(PAIRS):
            q2 = halves(q_ref[p, rows, :])

            def part(j, total, masked, p=p, q2=q2):
                keys = pl.ds(pl.multiple_of(j * TB, TB), TB)
                kb = kb_ref[j]
                kb = jnp.where(first_half, kb[2 * p : 2 * p + 1, :], kb[2 * p + 1 : 2 * p + 2, :])
                h = mm(q2, k_ref[p, keys, :], NT_) + kb
                w = (h + h * jnp.tanh(h)) * inv2
                if masked:
                    w = jnp.where(causal, w, 0.0)
                return total + mm(beside(w.astype(bf16)), halves(v_ref[p, keys, :]))

            total = lax.fori_loop(
                0, i, functools.partial(part, masked=False), jnp.zeros((TB, WIDE), f32)
            )
            o_ref[p, rows, :] = part(i, total, True)

    def lose(i):
        rows = pl.ds(pl.multiple_of(i * TB, TB), TB)
        place = lax.broadcasted_iota(jnp.int32, (TB, 1), 0) + i * TB
        o = jnp.concatenate([o_ref[p, rows, :] for p in range(PAIRS)], axis=1)
        factor_attn = lax.rsqrt(jnp.mean(o * o, -1, keepdims=True) + epsilon)
        na = o * factor_attn * gain_attn
        hu = hu_ref[rows, :]
        sigma, slope = silu_parts(hu)
        upper = hu * sigma
        gated = (na * upper).astype(bf16)
        y = xf_ref[rows, :] + mm(gated, w2_ref[...])
        factor_out = lax.rsqrt(jnp.mean(y * y, -1, keepdims=True) + epsilon)
        out = (y * factor_out * gain_out).astype(bf16)
        zf = out.astype(f32)
        after = xf_ref[pl.ds(pl.multiple_of(i * TB + TB, 8), 8), :]
        last = lax.broadcasted_iota(jnp.int32, (TB, 1), 0) == TB - 1
        target = jnp.where(last, after[0:1, :], pltpu.roll(xf_ref[rows, :], TB - 1, 0))
        neg_logits = mm(out, neg_ref[...].reshape(half * 2 * z.rn, D), NT_) * scale
        pos = jnp.sum(zf * target, -1, keepdims=True) * scale
        top = jnp.maximum(jnp.max(neg_logits, -1, keepdims=True), pos)
        neg_exp = jnp.exp(neg_logits - top)
        pos_exp = jnp.exp(pos - top)
        total = pos_exp + jnp.sum(neg_exp, -1, keepdims=True)
        live = jnp.where(place + 1 < length, 1.0, 0.0) * lead.astype(f32)
        per = (top + jnp.log(total) - pos) * live
        gneg = (neg_exp / total * live).astype(bf16)
        gpos = (pos_exp / total - 1.0) * live
        gz = mm(gneg, neg_ref[...].reshape(half * 2 * z.rn, D)) * scale + gpos * target * scale
        gneg_ref[...] += mm(gneg, out, TN) * scale
        target_grad = gpos * zf * scale
        first = lax.broadcasted_iota(jnp.int32, (TB, 1), 0) == 0
        shifted = jnp.where(first, carry_ref[0:1, :], pltpu.roll(target_grad, 1, 0))
        carry_ref[0:1, :] = target_grad[TB - 1 : TB, :]
        scaled = gz * gain_out
        gy = factor_out * (
            scaled - y * factor_out * factor_out * jnp.mean(y * scaled, -1, keepdims=True)
        )
        gres_ref[rows, :] = gy + shifted
        low = gy.astype(bf16)
        gg = mm(low, w2_ref[...], NT_)
        gw2_ref[...] += mm(gated, low, TN)
        gnorm = gg * upper
        gup = gg * na
        og = gain_attn * gnorm
        inner = jnp.sum(o * og, -1, keepdims=True)
        go = factor_attn * (og - o * factor_attn * factor_attn * (inner / D))
        go = go.astype(bf16)
        for p in range(PAIRS):
            do_ref[p, rows, :] = go[:, p * WIDE : (p + 1) * WIDE]
        ghu_ref[rows, :] = (gup * slope).astype(bf16)
        stat_ref[1:2, :] += row_sum(gnorm * o * factor_attn)
        stat_ref[2:3, :] += row_sum(gz * y * factor_out)
        stat_ref[3:4, :] += jnp.broadcast_to(row_sum(per), (1, D))
        stat_ref[4:5, :] += jnp.broadcast_to(row_sum(live), (1, D))


    per_group = z.group_len // TB
    arrive(0)

    def last(i, carry):
        lose(i)
        return carry

    def after_one():
        neg_one()
        for g in range(3, z.groups):
            release(g)

    def after_two():
        neg_two()
        neg_three()
        neg_four()
        lax.fori_loop(0, NT - 2, last, 0)

    def step(i, carry):
        if per_group == 1:
            pl.when(i > 0)(lambda: arrive(i))
        inputs(i)
        attend(i)
        pl.when(i == 1)(after_one)
        pl.when(i == NT - 2)(after_two)
        return carry

    lax.fori_loop(0, NT, step, 0)
    lax.fori_loop(NT - 2, NT, last, 0)
    for dd in range(z.n_data):
        at = z.order(dd)
        for kk in range(z.n_model):
            piece = gw2_ref[kk * z.fw + dd * z.r2 : kk * z.fw + (dd + 1) * z.r2, :]
            if z.r2p > z.r2:
                piece = jnp.concatenate([piece, jnp.zeros((z.r2p - z.r2, D), f32)], axis=0)
            ga_ref[at, kk * z.r2p : (kk + 1) * z.r2p, :] = piece
        ga_ref[at, z.n_model * z.r2p :, :] = gneg_ref[at * z.rn : (at + 1) * z.rn, :]

    for i in range(half):
        wp_copy(side * half + i).wait_send()
        n5_copy(side * half + i).wait_send()
    for i in range(1, half):
        to = lax.rem(chip + i, half)
        wc_copy(i, here, to).wait_send()
        n2_copy(i, chip, to).wait_send()
        n4_copy(i, here, to).wait_send()
    for i in range(1, n_model):
        at = lax.rem(k + i, n_model)
        wz_copy(i, k, at).wait_send()
        n3_copy(i, k, at).wait_send()
        bz_copy(i, k, at).wait_send()
    n1_copy.wait_send()

    def finish(i, carry):
        at = lax.rem(me + i, n_every)
        ask_copy(at, at, at).wait_send()
        row_copy(z.groups - 1, at, at, at).wait_send()
        return carry

    lax.fori_loop(1, n_every, finish, 0)


def front(z, scalars, table, w_f1, w_f2, bias_tile, owner, local, ids, bucket, gains):
    sds = jax.ShapeDtypeStruct
    dma = pltpu.SemaphoreType.DMA
    vm = pltpu.VMEM
    per_side = z.half * MB * z.rn
    every, model, half, data = (z.n_every,), (z.n_model,), (z.half,), (z.n_data,)
    groups_every = (z.groups, z.n_every)
    pairs_shape = sds((PAIRS, LEN, WIDE), bf16)
    return pl.pallas_call(
        functools.partial(front_kernel, z),
        out_shape=(
            sds((z.n_every, 1, LANES), f32),
            sds((NT, 1, TB), f32),
            sds((z.n_data, z.n_model, z.rw, D), bf16),
            sds((z.n_model, 8, LANES), f32),
            sds((LEN, D), bf16), sds((LEN, D), bf16),
            pairs_shape, pairs_shape, pairs_shape, pairs_shape,
            sds((LEN, D), bf16), sds((LEN, D), f32),
            sds((z.n_data, z.ra, D), f32), sds((8, D), f32),
        ),
        in_specs=[pl.BlockSpec(memory_space=pltpu.SMEM)] + [VM] * 9,
        out_specs=(VM,) * 14,
        scratch_shapes=[
            vm(table.shape, bf16),
            vm((z.n_every, 1, LANES), f32),
            vm((z.groups, z.n_every, CH, D), bf16),
            vm((z.groups, z.n_every, CH, D), bf16),
            vm((2, per_side, D), bf16),
            vm((per_side, D), bf16),
            vm((z.half, MB * z.rn, D), bf16),
            vm((z.n_model, z.rn, D), bf16),
            vm((per_side, D), bf16),
            vm((MB, z.rn, D), bf16),
            vm((z.n_data, z.rn, D), bf16),
            vm((LEN + 8, D), f32),
            vm((LEN, D), f32),
            vm((PAIRS, LEN, WIDE), f32),
            vm((8, D), f32),
            vm((NT, 8, TB), f32),
            vm((4, D, D), bf16),
            vm((D, D), bf16),
            vm((D, D), f32),
            vm((z.n_data * z.rn, D), f32),
            dma(every), dma(every), dma(groups_every), dma(groups_every),
            dma(model), dma(model), dma(half), dma(data), dma(data), dma(data), dma(model), dma(model),
            dma, dma, dma(half), dma(half), dma(model), dma(model), dma(half), dma(data), dma(data), dma(data),
        ],
        compiler_params=pltpu.CompilerParams(
            collective_id=0, has_side_effects=True, vmem_limit_bytes=LIMIT
        ),
        cost_estimate=pl.CostEstimate(
            flops=60_000_000_000, bytes_accessed=30_000_000, transcendentals=6_000_000
        ),
        name="front",
    )(scalars, table, w_f1, w_f2, bias_tile, owner, local, ids, bucket, gains)


def rear_kernel(
    z, len_ref, x_ref, n1_ref, q_ref, k_ref, v_ref, do_ref, ghu_ref, gres_ref, w_ref, bias_ref, bucket_ref,
    gains_ref, slot_ref, stat_in_ref, ga_ref, asked_ref, ids_ref,
    tg_ref, wg_ref, packs_ref, squares_ref,
    gh_ref, hid_ref, kb_ref, dq_ref, dk_ref, dv_ref, bs_ref, w1_ref, stat_ref, pack_ref, out_ref, gb_ref,
    got_ref, pa_ref, pb_ref, sa_ref, sb_ref, ca_ref, cb_ref, zs_ref, zr_ref, ng_ref, sq_ref,
    row_send, row_recv, pack_send, pack_recv,
    pa_send, pa_recv, pb_send, pb_recv, ca_send, ca_recv, cb_send, cb_recv,
    zw_send, zw_recv, zn_send, zn_recv, gw_send, gw_recv, gn_send, gn_recv,
    hw_send, hw_recv, hn_send, hn_recv, sq_send, sq_recv,
):
    n_every, n_model, half = z.n_every, z.n_model, z.half
    slots = z.slots
    d = lax.axis_index("dp")
    k = lax.axis_index("mp")
    me = d * n_model + k
    side = lax.rem(d, 2)
    chip = d // 2
    here = side * half + chip
    other = d + 1 - 2 * side
    barrier = pltpu.get_barrier_semaphore()

    def signal(i, carry):
        to = spot(lax.rem(me + i, n_every), n_model)
        pl.semaphore_signal(barrier, inc=1, device_id=to, device_id_type=MESH)
        return carry

    lax.fori_loop(1, n_every, signal, 0)

    pa_copy = remote(ga_ref.at[1 - side], pa_ref, pa_send, pa_recv, (other, k))

    def pb_copy(p):
        return remote(gb_ref.at[1 - side, p], pb_ref.at[p], pb_send.at[p], pb_recv.at[p], (other, k))

    def row_copy(g, src, dst, to):
        return remote(
            out_ref.at[g, to], got_ref.at[g, dst], row_send.at[g, to], row_recv.at[g, src],
            spot(to, n_model),
        )

    def pack_copy(src, dst, to):
        return remote(
            pack_ref, packs_ref.at[dst], pack_send.at[to], pack_recv.at[src], spot(to, n_model)
        )

    def ca_copy(i, at, to):
        return remote(
            sa_ref.at[to], ca_ref.at[at], ca_send.at[i], ca_recv.at[at], (2 * to + side, k)
        )

    def cb_copy(p, i, at, to):
        return remote(
            sb_ref.at[p, to], cb_ref.at[p, at], cb_send.at[p, i], cb_recv.at[p, at], (2 * to + side, k)
        )

    def zn_copy(i, at, to):
        return remote(
            ng_ref.at[here, at], ng_ref.at[here, at], zn_send.at[i], zn_recv.at[at], (d, to)
        )

    def zw_copy(at, to):
        return remote(zs_ref.at[to], zr_ref.at[at], zw_send.at[to], zw_recv.at[at], (d, to))

    def gw_copy(i, at, to):
        return remote(
            wg_ref.at[at], wg_ref.at[at], gw_send.at[i], gw_recv.at[at], (2 * to + side, k)
        )

    def gn_copy(i, at, to):
        return remote(
            ng_ref.at[at], ng_ref.at[at], gn_send.at[i], gn_recv.at[at], (2 * to + side, k)
        )

    def hw_copy(at):
        return remote(wg_ref.at[at], wg_ref.at[at], hw_send.at[at], hw_recv.at[at], (other, k))

    def hn_copy(at):
        return remote(ng_ref.at[at], ng_ref.at[at], hn_send.at[at], hn_recv.at[at], (other, k))

    def sq_copy(src, dst, to):
        return remote(
            sq_ref, squares_ref.at[dst], sq_send.at[to], sq_recv.at[src], spot(to, n_model)
        )

    def chips_a():
        pa_copy.wait_recv()
        sa_ref[...] = (ga_ref[side] + pa_ref[...]).astype(bf16)
        for i in range(1, half):
            ca_copy(i, chip, lax.rem(chip + i, half)).start()

    def chips_b(p):
        pb_copy(p).wait_recv()
        sb_ref[p] = (gb_ref[side, p] + pb_ref[p]).astype(bf16)
        for i in range(1, half):
            cb_copy(p, i, chip, lax.rem(chip + i, half)).start()

    def planes_a():
        total = sa_ref[chip].astype(f32)
        for i in range(1, half):
            at = lax.rem(chip + i, half)
            ca_copy(i, at, chip).wait_recv()
            total = total + ca_ref[at].astype(f32)
        ng_ref[here, k] = total[n_model * z.r2p :].astype(bf16)
        zs_ref[:, z.r1 :, :] = total[: n_model * z.r2p].reshape(n_model, z.r2p, D)
        for i in range(1, n_model):
            zn_copy(i, k, lax.rem(k + i, n_model)).start()

    def planes_b(p):
        total = sb_ref[p, chip].astype(f32)
        for i in range(1, half):
            at = lax.rem(chip + i, half)
            cb_copy(p, i, at, chip).wait_recv()
            total = total + cb_ref[p, at].astype(f32)
        for i in range(z.npp):
            to = p * z.npp + i
            zs_ref[to, : z.r1, :] = total[i * z.r1 : (i + 1) * z.r1]
            pl.when(k != to)(lambda to=to: zw_copy(k, to).start())

    def spread_a():
        for i in range(1, n_model):
            zn_copy(i, lax.rem(k + i, n_model), k).wait_recv()
        for i in range(1, half):
            gn_copy(i, here, lax.rem(chip + i, half)).start()
        hn_copy(here).start()

    def swap_a():
        for i in range(1, half):
            at = side * half + lax.rem(chip + i, half)
            gn_copy(i, at, chip).wait_recv()
            hn_copy(at).start()

    gain_in = gains_ref[0:1, :]
    place_weights(z, w_ref, w1_ref, None)
    kb_ref[...] = key_bias(bias_ref, bucket_ref, len_ref[0]).T

    def inputs(i, carry):
        rows = pl.ds(pl.multiple_of(i * TB, TB), TB)
        for c in (1, 2, 3):
            hid_ref[c - 1, rows, :] = mm(n1_ref[rows, :], w1_ref[c], NT_)
        return carry

    lax.fori_loop(0, NT, inputs, 0)
    bs_ref[...] = jnp.zeros_like(bs_ref)
    in_row = lax.broadcasted_iota(jnp.int32, (2 * TB, TB), 0)
    in_col = lax.broadcasted_iota(jnp.int32, (2 * TB, TB), 1)
    causal = lax.rem(in_row, TB) <= in_col
    ones_lane = lax.broadcasted_iota(jnp.int32, (2 * TB, LANES), 1)
    ones_half = lax.broadcasted_iota(jnp.int32, (2 * TB, LANES), 0) >= TB
    stat_ref[...] = jnp.zeros_like(stat_ref)
    per_group = z.group_len // TB

    def outputs(i):
        rows = pl.ds(pl.multiple_of(i * TB, TB), TB)
        gn = mm(ghu_ref[rows, :], w1_ref[0])
        for c in (1, 2, 3):
            gn += mm(gh_ref[c - 1, rows, :], w1_ref[c])
        x = x_ref[rows, :].astype(f32)
        factor = lax.rsqrt(jnp.mean(x * x, -1, keepdims=True) + epsilon)
        scaled = gn * gain_in
        gx = factor * (scaled - x * factor * factor * jnp.mean(x * scaled, -1, keepdims=True))
        gx = (gx + gres_ref[rows, :]).astype(bf16)
        stat_ref[0:1, :] += row_sum(gn * x * factor)
        group = i // per_group
        hot = lax.broadcasted_iota(jnp.int32, (slots, TB), 0).astype(f32) == slot_ref[i]
        mine = mm(jnp.where(hot, 1.0, 0.0).astype(bf16), gx).astype(bf16)
        mine = mine.reshape(z.n_every, CH, D)
        if per_group == 1:
            out_ref[group] = mine
        else:
            out_ref[group] = jnp.where(lax.rem(i, per_group) == 0, mine, out_ref[group] + mine)

    def send_group(g):
        def send(i, carry):
            row_copy(g, me, me, lax.rem(me + i, n_every)).start()
            return carry

        lax.fori_loop(1, n_every, send, 0)
        got_ref[g, me] = out_ref[g, me]

    def weights_grad(p):
        lanes = slice(p * WIDE, (p + 1) * WIDE)
        for c in range(4):
            left = ghu_ref[:, lanes] if c == 0 else gh_ref[c - 1, :, lanes]
            grads = mm(left, n1_ref[...], TN)
            for side_head in range(2):
                head = 2 * p + side_head
                for dd in range(z.n_data):
                    own_head, part, first = z.block(dd)
                    if part == c and own_head == head % z.heads_dev:
                        at = head // z.heads_dev - p * z.npp
                        gb_ref[dd % 2, p, dd // 2, at * z.r1 : (at + 1) * z.r1, :] = grads[
                            side_head * DH + first : side_head * DH + first + z.r1
                        ]
        pb_copy(p).start()

    pl.semaphore_wait(barrier, n_every - 1)
    pa_copy.start()

    for p in range(PAIRS):
        lanes = slice(p * WIDE, (p + 1) * WIDE)
        dq_ref[...] = jnp.zeros_like(dq_ref)
        mark = jnp.where(
            ones_lane == jnp.where(ones_half, 2 * p + 1, 2 * p), 1.0, 0.0
        ).astype(bf16)

        def keys_step(j, carry, p=p, lanes=lanes, mark=mark):
            keys = pl.ds(pl.multiple_of(j * TB, TB), TB)
            k2 = halves(k_ref[p, keys, :])
            v2 = halves(v_ref[p, keys, :])
            kt = k_ref[p, keys, :].astype(f32).T
            low = lax.broadcasted_iota(jnp.int32, kt.shape, 0) < DH
            kt2 = jnp.concatenate(
                [jnp.where(low, kt, 0.0), jnp.where(low, 0.0, kt)], axis=1
            ).astype(bf16)
            kb = jnp.concatenate(
                [kb_ref[keys, 2 * p : 2 * p + 1], kb_ref[keys, 2 * p + 1 : 2 * p + 2]], axis=0
            )
            dk_ref[...] = jnp.zeros_like(dk_ref)
            dv_ref[...] = jnp.zeros_like(dv_ref)

            def part(i, masked):
                rows = pl.ds(pl.multiple_of(i * TB, TB), TB)
                q = q_ref[p, rows, :]
                do = do_ref[p, rows, :]
                place = lax.broadcasted_iota(jnp.int32, (1, TB), 1) + i * TB
                inv = 1.0 / (place.astype(f32) + 1.0)
                h = mm(k2, q, NT_) + kb
                t = jnp.tanh(h)
                m = h * t
                w = (h + m) * inv
                ds = mm(v2, do, NT_) * ((1.0 + t) * (0.5 * inv)) * (1.0 + h - m)
                if masked:
                    w = jnp.where(causal, w, 0.0)
                    ds = jnp.where(causal, ds, 0.0)
                ds = ds.astype(bf16)
                dv_ref[...] += mm(beside(w.astype(bf16)), halves(do))
                dk_ref[...] += mm(beside(ds), jnp.concatenate([halves(q), mark], axis=1))
                dq_ref[i] += mm(kt2, ds)

            part(j, True)

            def later(i, inner):
                part(i, False)
                return inner

            lax.fori_loop(j + 1, NT, later, 0)
            slope_v = silu_parts(hid_ref[0, keys, lanes])[1]
            slope_k = silu_parts(hid_ref[2, keys, lanes])[1]
            gh_ref[0, keys, lanes] = (dv_ref[...] * slope_v).astype(bf16)
            gh_ref[2, keys, lanes] = (dk_ref[:, :WIDE] * 2.0 * slope_k).astype(bf16)
            bs_ref[keys, :] += dk_ref[:, WIDE:]
            slope_q = silu_parts(hid_ref[1, keys, lanes])[1]
            gh_ref[1, keys, lanes] = (dq_ref[j].T * DH ** (-0.5) * slope_q).astype(bf16)
            if p == PAIRS - 1:
                outputs(j)
                if per_group == 1:
                    send_group(j)
                pl.when(j == 0)(functools.partial(chips_b, PAIRS - 2))
                pl.when(j == 1)(functools.partial(planes_b, PAIRS - 3))
                pl.when(j == 2)(spread_a)
            return carry

        lax.fori_loop(0, NT, keys_step, 0)
        weights_grad(p)
        if p == 0:
            chips_a()
        elif p < PAIRS - 1:
            chips_b(p - 1)
            if p == 1:
                planes_a()
            else:
                planes_b(p - 2)

    if per_group > 1:
        for g in range(z.groups):
            send_group(g)
    hot = jnp.where(
        lax.broadcasted_iota(jnp.int32, (NB, LEN), 0) == bucket_ref[...], 1.0, 0.0
    )
    bias_grad = lax.dot_general(hot, bs_ref[...], NN, precision=highest, preferred_element_type=f32)
    for i in range(D // LANES):
        lanes = slice(i * LANES, (i + 1) * LANES)
        pack_ref[i : i + 1] = stat_ref[0:1, lanes]
        pack_ref[4 + i : 5 + i] = stat_in_ref[1:2, lanes]
        pack_ref[8 + i : 9 + i] = stat_in_ref[2:3, lanes]
    pack_ref[12:14] = stat_in_ref[3:5, :LANES]
    pack_ref[14:16] = jnp.zeros((2, LANES), f32)
    pack_ref[16:24] = bias_grad.T[0:8, :]
    packs_ref[me] = pack_ref[...]

    def pack_all(i, carry):
        pack_copy(me, me, lax.rem(me + i, n_every)).start()
        return carry

    lax.fori_loop(1, n_every, pack_all, 0)

    tg_ref[...] = jnp.zeros_like(tg_ref)
    wide = min(TB, slots)
    ask_at = lax.broadcasted_iota(jnp.int32, (z.rows_dev, wide), 0).astype(f32)

    def collect(g):
        def wait(i, carry):
            at = lax.rem(me + i, n_every)
            row_copy(g, at, at, at).wait_recv()
            return carry

        lax.fori_loop(1, n_every, wait, 0)
        for b in range(slots // wide):
            asked = asked_ref[g][:, b * wide : (b + 1) * wide]
            hot = jnp.where(ask_at == asked, 1.0, 0.0).astype(bf16)
            rows = got_ref[g, b * (wide // CH) : (b + 1) * (wide // CH)].reshape(wide, D)
            tg_ref[...] += mm(hot, rows)

    neg_rows = n_model * z.rn
    row_at = lax.broadcasted_iota(jnp.int32, (z.rows_dev, neg_rows), 0).astype(f32)
    base = (me * z.rows_dev).astype(f32)

    def negatives(at):
        hot = jnp.where(row_at == ids_ref[at] - base, 1.0, 0.0).astype(bf16)
        tg_ref[...] += mm(hot, ng_ref[at].reshape(neg_rows, D))

    planes_b(PAIRS - 2)
    swap_a()
    chips_b(PAIRS - 1)
    collect(0)
    for i in range(half):
        negatives(side * half + i)
    planes_b(PAIRS - 1)
    for g in range(1, max(1, z.groups - 1)):
        collect(g)
    total = zs_ref[k]
    for i in range(1, n_model):
        at = lax.rem(k + i, n_model)
        zw_copy(at, k).wait_recv()
        total = total + zr_ref[at]
    wg_ref[here] = total
    for i in range(1, half):
        gw_copy(i, here, lax.rem(chip + i, half)).start()
    hw_copy(here).start()
    for i in range(half):
        hn_copy((1 - side) * half + i).wait_recv()
        negatives((1 - side) * half + i)
    if z.groups > 1:
        collect(z.groups - 1)

    table_grad = tg_ref[...]
    slice_grad = wg_ref[here]
    squares = row_sum(table_grad * table_grad) + row_sum(slice_grad * slice_grad)
    sq_ref[...] = sum(squares[:, i * LANES : (i + 1) * LANES] for i in range(D // LANES))
    squares_ref[me] = sq_ref[...]

    def share(i, carry):
        to = lax.rem(me + i, n_every)
        sq_copy(me, me, to).start()
        return carry

    lax.fori_loop(1, n_every, share, 0)
    for i in range(1, half):
        at = side * half + lax.rem(chip + i, half)
        gw_copy(i, at, chip).wait_recv()
        hw_copy(at).start()
    for i in range(half):
        hw_copy((1 - side) * half + i).wait_recv()
        hw_copy(side * half + i).wait_send()
        hn_copy(side * half + i).wait_send()
    for i in range(1, half):
        to = lax.rem(chip + i, half)
        ca_copy(i, chip, to).wait_send()
        for p in range(PAIRS):
            cb_copy(p, i, chip, to).wait_send()
        gn_copy(i, here, to).wait_send()
        gw_copy(i, here, to).wait_send()
    for i in range(1, n_model):
        to = lax.rem(k + i, n_model)
        zn_copy(i, k, to).wait_send()
        zw_copy(k, to).wait_send()
    pa_copy.wait_send()
    for p in range(PAIRS):
        pb_copy(p).wait_send()

    def finish(i, carry):
        at = lax.rem(me + i, n_every)
        for g in range(z.groups):
            row_copy(g, at, at, at).wait_send()
        pack_copy(at, at, at).wait_send()
        pack_copy(at, at, at).wait_recv()
        sq_copy(at, at, at).wait_send()
        sq_copy(at, at, at).wait_recv()
        return carry

    lax.fori_loop(1, n_every, finish, 0)


def rear(
    z, scalars, x, n1, q, k, v, do, ghu, gres, w, bias, bucket, gains, slot, stat, ga, asked, ids
):
    sds = jax.ShapeDtypeStruct
    dma = pltpu.SemaphoreType.DMA
    vm = pltpu.VMEM
    every, model, half, data = (z.n_every,), (z.n_model,), (z.half,), (z.n_data,)
    groups_every = (z.groups, z.n_every)
    pairs, pairs_half = (PAIRS,), (PAIRS, z.half)
    rows_b = z.npp * z.r1
    return pl.pallas_call(
        functools.partial(rear_kernel, z),
        out_shape=(
            sds((z.rows_dev, D), f32),
            sds((z.n_data, z.rw, D), f32),
            sds((z.n_every, 24, LANES), f32),
            sds((z.n_every, 1, LANES), f32),
        ),
        in_specs=[pl.BlockSpec(memory_space=pltpu.SMEM)] + [VM] * 17,
        out_specs=(VM,) * 4,
        scratch_shapes=[
            vm((3, LEN, D), bf16),
            vm((3, LEN, D), f32),
            vm((LEN, 8), f32),
            vm((NT, WIDE, TB), f32),
            vm((TB, WIDE + LANES), f32),
            vm((TB, WIDE), f32),
            vm((LEN, LANES), f32),
            vm((4, D, D), bf16),
            vm((8, D), f32),
            vm((24, LANES), f32),
            vm((z.groups, z.n_every, CH, D), bf16),
            vm((2, PAIRS, z.half, rows_b, D), f32),
            vm((z.groups, z.n_every, CH, D), bf16),
            vm((z.half, z.ra, D), f32),
            vm((PAIRS, z.half, rows_b, D), f32),
            vm((z.half, z.ra, D), bf16),
            vm((PAIRS, z.half, rows_b, D), bf16),
            vm((z.half, z.ra, D), bf16),
            vm((PAIRS, z.half, rows_b, D), bf16),
            vm((z.n_model, z.rw, D), f32),
            vm((z.n_model, z.rw, D), f32),
            vm((z.n_data, z.n_model, z.rn, D), bf16),
            vm((1, LANES), f32),
            dma(groups_every), dma(groups_every), dma(every), dma(every),
            dma, dma, dma(pairs), dma(pairs), dma(half), dma(half), dma(pairs_half), dma(pairs_half),
            dma(model), dma(model), dma(model), dma(model), dma(half), dma(data), dma(half), dma(data),
            dma(data), dma(data), dma(data), dma(data), dma(every), dma(every),
        ],
        compiler_params=pltpu.CompilerParams(
            collective_id=1, has_side_effects=True, vmem_limit_bytes=LIMIT
        ),
        cost_estimate=pl.CostEstimate(
            flops=60_000_000_000, bytes_accessed=30_000_000, transcendentals=6_000_000
        ),
        name="rear",
    )(scalars, x, n1, q, k, v, do, ghu, gres, w, bias, bucket, gains, slot, stat, ga, asked, ids)


def adam_step(weight, grad, first, second, rate, decay):
    first_new = beta_one * first + (1.0 - beta_one) * grad
    second_new = beta_two * second + (1.0 - beta_two) * grad * grad
    fix_one = 1.0 - beta_one**STEP
    fix_two = 1.0 - beta_two**STEP
    move = first_new / fix_one / (jnp.sqrt(second_new / fix_two) + adam_floor) + decay * weight
    return (weight - rate * move, first_new, second_new)


def settle_kernel(
    z, squares_ref, packs_ref, wg_ref, tg_ref, t_ref, tm_ref, tv_ref, a_ref, am_ref, av_ref,
    b_ref, bm_ref, bv_ref, c_ref, cm_ref, cv_ref, e_ref, em_ref, ev_ref,
    t_out, tm_out, tv_out, tl_out, a_out, am_out, av_out, al_out, b_out, bm_out, bv_out, bl_out,
    c_out, cm_out, cv_out, e_out, em_out, ev_out, flat_out, factor_ref,
):
    def update(grad, refs, outs, rate, decay):
        new, first, second = adam_step(refs[0][...], grad, refs[1][...], refs[2][...], rate, decay)
        outs[0][...] = new
        outs[1][...] = first
        outs[2][...] = second
        if len(outs) > 3:
            outs[3][...] = new.astype(bf16)

    @pl.when(pl.program_id(0) == 0)
    def _():
        packs = jnp.sum(packs_ref[...], axis=0)
        gain_grad = jnp.concatenate(
            [
                jnp.concatenate([packs[4 * r + i : 4 * r + i + 1] for i in range(D // LANES)], axis=1)
                for r in range(3)
            ],
            axis=0,
        )
        bias_all = packs[16:24]
        squares = jnp.sum(squares_ref[...], axis=0) + row_sum(packs[0:12] * packs[0:12])
        squares = squares + row_sum(bias_all * bias_all)
        norm = jnp.sqrt(jnp.sum(squares, axis=1, keepdims=True))
        factor = jnp.minimum(1.0, clip_at / norm)
        factor_ref[...] = jnp.broadcast_to(factor, factor_ref.shape)
        flat_out[0:2] = packs[12:14]
        flat_out[2:3] = jnp.broadcast_to(norm, (1, LANES))
        flat_out[3:8] = jnp.zeros((5, LANES), f32)
        one = jnp.concatenate([wg_ref[z.order(d), 0 : z.r1] for d in range(z.n_data)], axis=0)
        two = jnp.concatenate(
            [wg_ref[z.order(d), z.r1 : z.r1 + z.r2] for d in range(z.n_data)], axis=0
        )
        update(one.T * factor, (a_ref, am_ref, av_ref), (a_out, am_out, av_out, al_out), 0.04, 0.1)
        update(two * factor, (b_ref, bm_ref, bv_ref), (b_out, bm_out, bv_out, bl_out), 0.04, 0.1)
        update(gain_grad * factor, (c_ref, cm_ref, cv_ref), (c_out, cm_out, cv_out), 0.5, 0.0)
        head = lax.broadcasted_iota(jnp.int32, bias_all.shape, 0)
        first_head = lax.axis_index("mp") * z.heads_dev
        mine = [
            row_sum(jnp.where(head == first_head + r, bias_all, 0.0)) for r in range(z.heads_dev)
        ]
        bias_grad = jnp.concatenate(mine, axis=0)
        update(bias_grad * factor, (e_ref, em_ref, ev_ref), (e_out, em_out, ev_out), 1.0, 0.0)

    update(
        tg_ref[...] * factor_ref[0:1, 0:1], (t_ref, tm_ref, tv_ref), (t_out, tm_out, tv_out, tl_out), 0.5, 0.1
    )


def settle(z, squares, packs, wg, tg, table, f1, f2, gains, bias):
    sds = jax.ShapeDtypeStruct
    rows = next(r for r in range(112, 0, -16) if z.rows_dev % r == 0)
    block = pl.BlockSpec((rows, D), lambda i: (i, 0))

    def like(array, dtype=f32):
        return sds(array.shape, dtype)

    return pl.pallas_call(
        functools.partial(settle_kernel, z),
        grid=(z.rows_dev // rows,),
        out_shape=(
            like(tg), like(tg), like(tg), like(tg, bf16),
            like(f1[0]), like(f1[0]), like(f1[0]), like(f1[0], bf16),
            like(f2[0]), like(f2[0]), like(f2[0]), like(f2[0], bf16),
            like(gains[0]), like(gains[0]), like(gains[0]),
            like(bias[0]), like(bias[0]), like(bias[0]), sds((8, LANES), f32),
        ),
        in_specs=[VM] * 3 + [block] * 4 + [VM] * 12,
        out_specs=(block,) * 4 + (VM,) * 15,
        scratch_shapes=[pltpu.VMEM((8, LANES), f32)],
        compiler_params=pltpu.CompilerParams(vmem_limit_bytes=LIMIT),
        cost_estimate=pl.CostEstimate(
            flops=20 * z.rows_dev * D, bytes_accessed=20_000_000, transcendentals=1_000_000
        ),
        name="settle",
    )(squares, packs, wg, tg, *table, *f1, *f2, *gains, *bias)


def pick(array, index):
    return lax.dynamic_index_in_dim(array, index, 0, keepdims=False)


def per_device(
    lengths, owners, item_rows, buckets, negatives, table, table_m, table_v, w_f1, f1_m, f1_v,
    w_f2, f2_m, f2_v, gains, gains_m, gains_v, bias, bias_m, bias_v,
):
    n_model = lax.axis_size("mp")
    n_data = lax.axis_size("dp")
    model_at = lax.axis_index("mp")
    z = Sizes(n_data, n_model, bias.shape[0], table.shape[0], negatives.shape[1])
    micro = model_at // z.copies
    heads_dev = z.heads_dev
    bucket = pick(buckets, micro)
    lead = (lax.rem(model_at, z.copies) == 0).astype(jnp.int32)
    scalars = jnp.stack([pick(lengths, micro)[0], lead])
    ids = negatives.astype(f32).reshape(MB, n_data, z.rn).transpose(1, 0, 2)
    ids_rows = ids.reshape(-1, 1, LANES)
    ids_cols = jnp.repeat(ids, z.copies, axis=1).reshape(n_data, 1, n_model * z.rn)
    bias_tile = lax.dynamic_update_slice(
        jnp.zeros((HEADS, NB), f32), bias, (model_at * heads_dev, 0)
    )

    asked, slot, w, bias_all, x, n1, q, k, v, do, ghu, gres, ga, stat_a = front(
        z, scalars, table, w_f1, w_f2, bias_tile, owners.reshape(MB, 1, LEN), item_rows, ids_rows,
        bucket, gains,
    )
    asked = asked.reshape(z.n_every, LANES)[:, : z.groups * CH].reshape(z.n_every, z.groups, CH)
    asked = asked.transpose(1, 0, 2).reshape(z.groups, 1, z.slots)
    table_grad, wg, packs, squares = rear(
        z, scalars, x, n1, q, k, v, do, ghu, gres, w, bias_all, bucket, gains, slot, stat_a,
        ga.reshape(2, z.half, z.ra, D), asked, ids_cols,
    )
    *new, flat = settle(
        z, squares, packs, wg, table_grad, (table, table_m, table_v), (w_f1, f1_m, f1_v),
        (w_f2, f2_m, f2_v), (gains, gains_m, gains_v), (bias, bias_m, bias_v),
    )
    return (flat[0, 0], flat[1, 0], flat[2, 0], *new)


def solution(mesh):
    rows, cols = P(("dp", "mp"), None), P(None, "mp")
    heads = P("mp", None)
    in_specs = (
        P(None, "dp"), P(None, "dp", None, None), P(None, "dp", None), P(None, "dp", None), P(),
        rows, rows, rows, cols, cols, cols, heads, heads, heads, P(), P(), P(), heads, heads, heads,
    )
    out_specs = (
        P(), P(), P(), rows, rows, rows, rows, cols, cols, cols, cols,
        heads, heads, heads, heads, P(), P(), P(), heads, heads, heads,
    )
    return jax.shard_map(
        per_device, mesh=mesh, in_specs=in_specs, out_specs=out_specs, check_vma=False
    )
```

```python
import functools

import jax
import jax.numpy as jnp
from jax import lax
from jax.experimental import pallas as pl
from jax.experimental.pallas import tpu as pltpu
from jax.sharding import PartitionSpec as P

DH = 64
D = 512
NB = 128
LEN = 1024
MB = 4
STEP = 10

TB = 256
NT = LEN // TB
HEADS = D // DH
PAIRS = HEADS // 2
WIDE = 2 * DH
CH = 16
LANES = 128
SPAN = 2

epsilon = 1e-06
clip_at = 1.0
beta_one = 0.9
beta_two = 0.95
adam_floor = 1e-08
highest = lax.Precision.HIGHEST
f32 = jnp.float32
bf16 = jnp.bfloat16
MESH = pl.DeviceIdType.MESH
VM = pl.BlockSpec(memory_space=pltpu.VMEM)
LIMIT = 61 * 1024 * 1024

NN = (((1,), (0,)), ((), ()))
NT_ = (((1,), (1,)), ((), ()))
TN = (((0,), (0,)), ((), ()))


def mm(a, b, dims=NN):
    return lax.dot_general(a, b, dims, preferred_element_type=f32)


def spot(index, n_model):
    return (index // n_model, lax.rem(index, n_model))


def cross(rows):
    lane = lax.broadcasted_iota(jnp.int32, (LANES, LANES), 1)
    eye = lax.broadcasted_iota(jnp.int32, (LANES, LANES), 0) == lane
    spread = jnp.broadcast_to(rows, (LANES, LANES))
    return jnp.sum(jnp.where(eye, spread, 0.0), axis=1, keepdims=True)


def remote(src, dst, send_sem, recv_sem, to):
    return pltpu.make_async_remote_copy(
        src_ref=src,
        dst_ref=dst,
        send_sem=send_sem,
        recv_sem=recv_sem,
        device_id=to,
        device_id_type=MESH,
    )


class Sizes:
    def __init__(self, n_data, n_model, heads_dev, rows_dev, negs):
        self.n_data, self.n_model, self.heads_dev, self.rows_dev = n_data, n_model, heads_dev, rows_dev
        self.n_every = n_data * n_model
        self.copies = n_model // MB
        look = LEN // n_model
        cap = max(2, 2 * look // self.n_every)
        self.group_len = look * max(1, CH // cap)
        self.groups = LEN // self.group_len
        self.slots = self.n_every * CH
        self.fw = heads_dev * DH
        self.half = n_data // 2
        self.r1 = 4 * self.fw // n_data
        self.r2 = self.fw // n_data
        self.r2p = -(-self.r2 // 16) * 16
        self.rw = self.r1 + self.r2p
        self.rn = negs // n_data
        self.ra = n_model * self.r2p + self.rn
        self.npp = n_model // PAIRS

    def order(self, d):
        return (d % 2) * self.half + d // 2

    def block(self, d):
        flat = d * self.r1
        return flat // (4 * DH), flat % (4 * DH) // DH, flat % DH


def silu_parts(values):
    sigma = 0.5 + 0.5 * jnp.tanh(0.5 * values)
    return sigma, sigma * (1.0 + values * (1.0 - sigma))


def halves(tile):
    low = lax.broadcasted_iota(jnp.int32, tile.shape, 1) < DH
    zero = jnp.zeros_like(tile)
    return jnp.concatenate([jnp.where(low, tile, zero), jnp.where(low, zero, tile)], axis=0)


def beside(tile):
    half = tile.shape[0] // 2
    return jnp.concatenate([tile[:half], tile[half:]], axis=1)


def row_sum(values):
    return jnp.sum(values, axis=0, keepdims=True)


def place_weights(z, w_ref, w1_ref, w2_ref):
    for d in range(z.n_data):
        head, part, first = z.block(d)
        for k in range(z.n_model):
            at = k * z.fw + head * DH + first
            w1_ref[part, at : at + z.r1, :] = w_ref[z.order(d), k, 0 : z.r1, :]
            if w2_ref is not None:
                at = k * z.fw + d * z.r2
                w2_ref[at : at + z.r2, :] = w_ref[z.order(d), k, z.r1 : z.r1 + z.r2, :]


def key_bias(bias_ref, bucket, length):
    table = jnp.sum(bias_ref[...], axis=0)
    hot = jnp.where(
        lax.broadcasted_iota(jnp.int32, (NB, LEN), 0) == bucket, 1.0, 0.0
    )
    rows = lax.dot_general(table, hot, NN, precision=highest, preferred_element_type=f32)
    inside = lax.broadcasted_iota(jnp.int32, (8, LEN), 1) < length
    return jnp.where(inside, 0.5 * rows, -1e30)


def front_kernel(
    z, len_ref, table_ref, f1_ref, f2_ref, bias_ref, owner_ref, local_ref, ids_ref, bucket_ref, gains_ref,
    asked_ref, slot_ref, w_ref, bias_all_ref,
    x_ref, n1o_ref, q_ref, k_ref, v_ref, do_ref, ghu_ref, gres_ref, ga_ref, stat_ref,
    low_ref, req_ref, send_ref, got_ref, t2_ref, n1_ref, n2_ref, n3_ref, acc_ref, plane_ref, neg_ref,
    xf_ref, hu_ref, o_ref, carry_ref, kb_ref, w1_ref, w2_ref, gw2_ref, gneg_ref,
    ask_send, ask_recv, row_send, row_recv,
    wz_send, wz_recv, wc_send, wc_recv, wp_send, wp_recv, bz_send, bz_recv,
    n1_send, n1_recv, n2_send, n2_recv, n3_send, n3_recv, n4_send, n4_recv, n5_send, n5_recv,
):
    n_every, n_model, half = z.n_every, z.n_model, z.half
    mine = z.groups * CH
    d = lax.axis_index("dp")
    k = lax.axis_index("mp")
    me = d * n_model + k
    side = lax.rem(d, 2)
    chip = d // 2
    here = side * half + chip
    other = d + 1 - 2 * side
    barrier = pltpu.get_barrier_semaphore()

    def signal(i, carry):
        to = spot(lax.rem(me + i, n_every), n_model)
        pl.semaphore_signal(barrier, inc=1, device_id=to, device_id_type=MESH)
        return carry

    lax.fori_loop(1, n_every, signal, 0)

    micro = k // z.copies
    owner_row = owner_ref[micro].astype(f32)
    value_row = local_ref[micro].astype(f32) + 1.0
    high_row = jnp.floor(value_row * (1.0 / 32.0))
    low_row = value_row - 32.0 * high_row
    length = z.group_len
    earlier = jnp.where(
        lax.broadcasted_iota(jnp.int32, (length, length), 0)
        < lax.broadcasted_iota(jnp.int32, (length, length), 1), 1.0, 0.0
    ).astype(bf16)
    pieces = []
    for g in range(z.groups):
        lanes = slice(g * length, (g + 1) * length)
        own = owner_row[:, lanes]
        owner_at = lax.broadcasted_iota(jnp.int32, (n_every, length), 0).astype(f32)
        hot = jnp.where(owner_at == own, 1.0, 0.0)
        rank = row_sum(mm(hot.astype(bf16), earlier) * hot)
        place = own * CH + rank
        for b in range(length // TB):
            slot_ref[g * (length // TB) + b] = place[:, b * TB : (b + 1) * TB]
        ranks = lax.broadcasted_iota(jnp.int32, (CH, length), 0).astype(f32)
        rank_hot = jnp.where(ranks == rank, 1.0, 0.0).astype(bf16)
        high = mm((hot * high_row[:, lanes]).astype(bf16), rank_hot, NT_)
        lower = mm((hot * low_row[:, lanes]).astype(bf16), rank_hot, NT_)
        pieces.append(high * 32.0 + lower - 1.0)
    pieces.append(jnp.full((n_every, LANES - mine), -1.0, f32))
    wanted = jnp.concatenate(pieces, axis=1)
    for o in range(n_every):
        req_ref[o] = wanted[o : o + 1]

    pl.semaphore_wait(barrier, n_every - 1)

    def ask_copy(src, dst, to):
        return remote(
            req_ref.at[to], asked_ref.at[dst], ask_send.at[to], ask_recv.at[src], spot(to, n_model)
        )

    def ask(i, carry):
        to = lax.rem(me + i, n_every)
        ask_copy(me, me, to).start()
        return carry

    lax.fori_loop(1, n_every, ask, 0)
    asked_ref[me] = req_ref[me]

    take = (
        lax.broadcasted_iota(jnp.int32, (z.r1, 4 * z.fw), 1)
        == lax.broadcasted_iota(jnp.int32, (z.r1, 4 * z.fw), 0) + d * z.r1
    )
    w_ref[here, k, 0 : z.r1, :] = mm(
        jnp.where(take, 1.0, 0.0).astype(bf16), f1_ref[...].astype(bf16), NT_
    ).astype(bf16)
    take = (
        lax.broadcasted_iota(jnp.int32, (z.r2p, z.fw), 1)
        == lax.broadcasted_iota(jnp.int32, (z.r2p, z.fw), 0) + d * z.r2
    )
    w_ref[here, k, z.r1 :, :] = mm(
        jnp.where(take, 1.0, 0.0).astype(bf16), f2_ref[...].astype(bf16)
    ).astype(bf16)
    head = lax.broadcasted_iota(jnp.int32, (HEADS, NB), 0)
    bias_tile = jnp.zeros((HEADS, NB), f32)
    for r in range(z.heads_dev):
        bias_tile += jnp.where(head == k * z.heads_dev + r, bias_ref[r : r + 1, :], 0.0)
    bias_all_ref[k] = bias_tile

    def wz_copy(i, at, to):
        return remote(
            w_ref.at[here, at], w_ref.at[here, at], wz_send.at[i], wz_recv.at[at], (d, to)
        )

    def bz_copy(i, at, to):
        return remote(
            bias_all_ref.at[k], bias_all_ref.at[at], bz_send.at[i], bz_recv.at[at], (d, to)
        )

    for i in range(1, n_model):
        to = lax.rem(k + i, n_model)
        wz_copy(i, k, to).start()
        bz_copy(i, k, to).start()
    low_ref[...] = table_ref[...].astype(bf16)

    def row_copy(g, src, dst, to):
        return remote(
            send_ref.at[g, to], got_ref.at[g, dst], row_send.at[g, to], row_recv.at[g, src],
            spot(to, n_model),
        )

    def asked_all(i, carry):
        src = lax.rem(me + i, n_every)
        ask_copy(src, src, src).wait_recv()
        return carry

    lax.fori_loop(1, n_every, asked_all, 0)
    asked = asked_ref[...].reshape(n_every, LANES) + 1.0
    asked_high = jnp.floor(asked * (1.0 / 32.0))
    asked_low = (asked - 32.0 * asked_high).astype(bf16)
    asked_high = asked_high.astype(bf16)
    per = min(TB // CH, n_every)
    spread = jnp.where(
        lax.broadcasted_iota(jnp.int32, (per * CH, CH), 1)
        == lax.rem(lax.broadcasted_iota(jnp.int32, (per * CH, CH), 0), CH), 1.0, 0.0
    ).astype(bf16)
    turn = lax.broadcasted_iota(jnp.int32, (per * CH, n_every), 0) // CH
    asker = lax.broadcasted_iota(jnp.int32, (per * CH, n_every), 1)
    lane = lax.broadcasted_iota(jnp.int32, (per * CH, z.rows_dev), 1).astype(f32)

    def serve(g):
        lanes = slice(g * CH, (g + 1) * CH)
        for b in range(n_every // per):
            at = mm(spread, asked_high[:, lanes], NT_) * 32.0 + mm(spread, asked_low[:, lanes], NT_)
            at = jnp.where(asker == turn + b * per, at, 0.0)
            column = jnp.sum(at, axis=1, keepdims=True) - 1.0
            hot = jnp.where(lane == column, 1.0, 0.0).astype(bf16)
            found = mm(hot, low_ref[...]).astype(bf16)
            send_ref[g, b * per : (b + 1) * per] = found.reshape(per, CH, D)
        got_ref[g, me] = send_ref[g, me]

    def send_group(g):
        def send(i, carry):
            row_copy(g, me, me, lax.rem(me + i, n_every)).start()
            return carry

        lax.fori_loop(1, n_every, send, 0)

    def release(g):
        def follow(i, carry):
            at = lax.rem(me + i, n_every)
            row_copy(g - 1, at, at, at).wait_send()
            row_copy(g, me, me, at).start()
            return carry

        lax.fori_loop(1, n_every, follow, 0)

    serve(0)
    send_group(0)

    per_side = half * MB * z.rn
    span = MB * z.rn
    n_lane = lax.broadcasted_iota(jnp.int32, (TB, z.rows_dev), 1).astype(f32)

    def negatives(i, carry, first):
        at = first * (per_side // TB) + i
        columns = [cross(ids_ref[at * (TB // LANES) + j]) for j in range(TB // LANES)]
        column = jnp.concatenate(columns, axis=0) - (me * z.rows_dev).astype(f32)
        hot = jnp.where(n_lane == column, 1.0, 0.0).astype(bf16)
        t2_ref[first, pl.ds(pl.multiple_of(i * TB, TB), TB), :] = mm(hot, low_ref[...]).astype(bf16)
        return carry

    def wc_copy(i, at, to):
        return remote(
            w_ref.at[at], w_ref.at[at], wc_send.at[i], wc_recv.at[at], (2 * to + side, k)
        )

    def wp_copy(at):
        return remote(w_ref.at[at], w_ref.at[at], wp_send.at[at], wp_recv.at[at], (other, k))

    n1_copy = remote(t2_ref.at[1 - side], n1_ref, n1_send, n1_recv, (other, k))

    def n2_copy(i, at, to):
        return remote(
            acc_ref.at[pl.ds(pl.multiple_of(to * span, 16), span)], n2_ref.at[at],
            n2_send.at[i], n2_recv.at[at], (2 * to + side, k),
        )

    def n3_copy(i, at, to):
        return remote(
            plane_ref.at[to // z.copies], n3_ref.at[at], n3_send.at[i], n3_recv.at[at], (d, to)
        )

    def n4_copy(i, at, to):
        return remote(
            neg_ref.at[at], neg_ref.at[at], n4_send.at[i], n4_recv.at[at], (2 * to + side, k)
        )

    def n5_copy(at):
        return remote(neg_ref.at[at], neg_ref.at[at], n5_send.at[at], n5_recv.at[at], (other, k))

    for i in range(1, n_model):
        wz_copy(i, lax.rem(k + i, n_model), k).wait_recv()
    for i in range(1, half):
        wc_copy(i, here, lax.rem(chip + i, half)).start()
    wp_copy(here).start()
    lax.fori_loop(0, per_side // TB, functools.partial(negatives, first=1 - side), 0)
    n1_copy.start()
    lax.fori_loop(0, per_side // TB, functools.partial(negatives, first=side), 0)
    if z.groups > 1:
        serve(1)
    n1_copy.wait_recv()
    acc_ref[...] = t2_ref[side] + n1_ref[...]
    for i in range(1, half):
        n2_copy(i, chip, lax.rem(chip + i, half)).start()
    for g in range(2, z.groups):
        serve(g)

    length = len_ref[micro, 0]
    lead = (lax.rem(k, z.copies) == 0).astype(jnp.int32)
    gain_in = gains_ref[0:1, :]
    gain_attn = gains_ref[1:2, :]
    gain_out = gains_ref[2:3, :]
    for i in range(1, n_model):
        at = lax.rem(k + i, n_model)
        bz_copy(i, at, k).wait_recv()
    kb = key_bias(bias_all_ref, bucket_ref[micro], length)
    for j in range(NT):
        kb_ref[j] = kb[:, j * TB : (j + 1) * TB]
    xf_ref[LEN:, :] = jnp.zeros((8, D), f32)
    carry_ref[...] = jnp.zeros_like(carry_ref)
    stat_ref[...] = jnp.zeros_like(stat_ref)
    gw2_ref[...] = jnp.zeros_like(gw2_ref)
    gneg_ref[...] = jnp.zeros_like(gneg_ref)
    if z.groups > 1:
        release(1)
    for i in range(1, half):
        from_chip = lax.rem(chip + i, half)
        wc_copy(i, side * half + from_chip, chip).wait_recv()
        wp_copy(side * half + from_chip).start()
    for g in range(2, min(3, z.groups)):
        release(g)
    for i in range(half):
        wp_copy((1 - side) * half + i).wait_recv()
    place_weights(z, w_ref, w1_ref, w2_ref)

    def neg_one():
        total = acc_ref[pl.ds(pl.multiple_of(chip * span, 16), span), :]
        for i in range(1, half):
            from_chip = lax.rem(chip + i, half)
            n2_copy(i, from_chip, chip).wait_recv()
            total = total + n2_ref[from_chip]
        plane_ref[...] = total.reshape(MB, z.rn, D)
        for i in range(1, n_model):
            n3_copy(i, k, lax.rem(k + i, n_model)).start()

    def neg_two():
        total = plane_ref[micro]
        for i in range(1, n_model):
            at = lax.rem(k + i, n_model)
            n3_copy(i, at, k).wait_recv()
            total = total + n3_ref[at]
        neg_ref[here] = total
        for i in range(1, half):
            n4_copy(i, here, lax.rem(chip + i, half)).start()
        n5_copy(here).start()

    def neg_three():
        for i in range(1, half):
            at = side * half + lax.rem(chip + i, half)
            n4_copy(i, at, chip).wait_recv()
            n5_copy(at).start()

    def neg_four():
        for i in range(half):
            n5_copy((1 - side) * half + i).wait_recv()

    slots = z.slots

    def arrive(g):
        def wait(i, carry):
            at = lax.rem(me + i, n_every)
            row_copy(g, at, at, at).wait_recv()
            return carry

        lax.fori_loop(1, n_every, wait, 0)

    def inputs(i):
        rows = pl.ds(pl.multiple_of(i * TB, TB), TB)
        hot = lax.broadcasted_iota(jnp.int32, (slots, TB), 0).astype(f32) == slot_ref[i]
        found = got_ref[i * TB // z.group_len]
        x = mm(jnp.where(hot, 1.0, 0.0).astype(bf16), found.reshape(slots, D), TN)
        x_ref[rows, :] = x.astype(bf16)
        xf_ref[rows, :] = x
        factor = lax.rsqrt(jnp.mean(x * x, -1, keepdims=True) + epsilon)
        n1 = (x * factor * gain_in).astype(bf16)
        n1o_ref[rows, :] = n1
        hu_ref[rows, :] = mm(n1, w1_ref[0], NT_)
        for c, ref in ((1, v_ref), (2, q_ref), (3, k_ref)):
            hidden = mm(n1, w1_ref[c], NT_)
            act = (hidden * silu_parts(hidden)[0]).astype(bf16)
            if c == 2:
                act = act * jnp.asarray(0.5 * DH ** (-0.5), bf16)
            for p in range(PAIRS):
                ref[p, rows, :] = act[:, p * WIDE : (p + 1) * WIDE]

    scale = 2.0 * D ** (-0.5)
    in_row = lax.broadcasted_iota(jnp.int32, (2 * TB, TB), 0)
    in_col = lax.broadcasted_iota(jnp.int32, (2 * TB, TB), 1)
    causal = in_col <= lax.rem(in_row, TB)
    first_half = in_row < TB

    def attend(i):
        rows = pl.ds(pl.multiple_of(i * TB, TB), TB)
        place = lax.broadcasted_iota(jnp.int32, (TB, 1), 0) + i * TB
        inv = 1.0 / (place.astype(f32) + 1.0)
        inv2 = jnp.concatenate([inv, inv], axis=0)
        o_ref[:, rows, :] = jnp.zeros((PAIRS, TB, WIDE), f32)

        def part(j, masked):
            keys = pl.ds(pl.multiple_of(j * TB, TB), TB)
            kb = kb_ref[j]
            for p in range(PAIRS):
                kb2 = jnp.where(first_half, kb[2 * p : 2 * p + 1, :], kb[2 * p + 1 : 2 * p + 2, :])
                h = mm(halves(q_ref[p, rows, :]), k_ref[p, keys, :], NT_) + kb2
                w = (h + h * jnp.tanh(h)) * inv2
                if masked:
                    w = jnp.where(causal, w, 0.0)
                o_ref[p, rows, :] += mm(beside(w.astype(bf16)), halves(v_ref[p, keys, :]))

        def before(j, carry):
            part(j, False)
            return carry

        lax.fori_loop(0, i, before, 0)
        part(i, True)

    def lose(i):
        rows = pl.ds(pl.multiple_of(i * TB, TB), TB)
        place = lax.broadcasted_iota(jnp.int32, (TB, 1), 0) + i * TB
        o = jnp.concatenate([o_ref[p, rows, :] for p in range(PAIRS)], axis=1)
        factor_attn = lax.rsqrt(jnp.mean(o * o, -1, keepdims=True) + epsilon)
        na = o * factor_attn * gain_attn
        hu = hu_ref[rows, :]
        sigma, slope = silu_parts(hu)
        upper = hu * sigma
        gated = (na * upper).astype(bf16)
        y = xf_ref[rows, :] + mm(gated, w2_ref[...])
        factor_out = lax.rsqrt(jnp.mean(y * y, -1, keepdims=True) + epsilon)
        out = (y * factor_out * gain_out).astype(bf16)
        zf = out.astype(f32)
        after = xf_ref[pl.ds(pl.multiple_of(i * TB + TB, 8), 8), :]
        last = lax.broadcasted_iota(jnp.int32, (TB, 1), 0) == TB - 1
        target = jnp.where(last, after[0:1, :], pltpu.roll(xf_ref[rows, :], TB - 1, 0))
        neg_logits = mm(out, neg_ref[...].reshape(half * 2 * z.rn, D), NT_) * scale
        pos = jnp.sum(zf * target, -1, keepdims=True) * scale
        top = jnp.maximum(jnp.max(neg_logits, -1, keepdims=True), pos)
        neg_exp = jnp.exp(neg_logits - top)
        pos_exp = jnp.exp(pos - top)
        total = pos_exp + jnp.sum(neg_exp, -1, keepdims=True)
        live = jnp.where(place + 1 < length, 1.0, 0.0) * lead.astype(f32)
        per = (top + jnp.log(total) - pos) * live
        gneg = (neg_exp / total * live).astype(bf16)
        gpos = (pos_exp / total - 1.0) * live
        gz = mm(gneg, neg_ref[...].reshape(half * 2 * z.rn, D)) * scale + gpos * target * scale
        gneg_ref[...] += mm(gneg, out, TN) * scale
        target_grad = gpos * zf * scale
        first = lax.broadcasted_iota(jnp.int32, (TB, 1), 0) == 0
        shifted = jnp.where(first, carry_ref[0:1, :], pltpu.roll(target_grad, 1, 0))
        carry_ref[0:1, :] = target_grad[TB - 1 : TB, :]
        scaled = gz * gain_out
        gy = factor_out * (
            scaled - y * factor_out * factor_out * jnp.mean(y * scaled, -1, keepdims=True)
        )
        gres_ref[rows, :] = gy + shifted
        low = gy.astype(bf16)
        gg = mm(low, w2_ref[...], NT_)
        gw2_ref[...] += mm(gated, low, TN)
        gnorm = gg * upper
        gup = gg * na
        og = gain_attn * gnorm
        inner = jnp.sum(o * og, -1, keepdims=True)
        go = factor_attn * (og - o * factor_attn * factor_attn * (inner / D))
        go = go.astype(bf16)
        for p in range(PAIRS):
            do_ref[p, rows, :] = go[:, p * WIDE : (p + 1) * WIDE]
        ghu_ref[rows, :] = (gup * slope).astype(bf16)
        stat_ref[1:2, :] += row_sum(gnorm * o * factor_attn)
        stat_ref[2:3, :] += row_sum(gz * y * factor_out)
        stat_ref[3:4, :] += jnp.broadcast_to(row_sum(per), (1, D))
        stat_ref[4:5, :] += jnp.broadcast_to(row_sum(live), (1, D))


    per_group = z.group_len // TB
    arrive(0)

    def last(i, carry):
        lose(i)
        return carry

    def after_one():
        neg_one()
        for g in range(3, z.groups):
            release(g)

    def after_two():
        neg_three()
        neg_four()
        lax.fori_loop(0, NT - 2, last, 0)

    def step(i, carry):
        if per_group == 1:
            pl.when(i > 0)(lambda: arrive(i))
        pl.when(i == NT - 2)(neg_two)
        inputs(i)
        attend(i)
        pl.when(i == 1)(after_one)
        pl.when(i == NT - 2)(after_two)
        return carry

    lax.fori_loop(0, NT, step, 0)
    lax.fori_loop(NT - 2, NT, last, 0)
    for dd in range(z.n_data):
        at = z.order(dd)
        for kk in range(z.n_model):
            piece = gw2_ref[kk * z.fw + dd * z.r2 : kk * z.fw + (dd + 1) * z.r2, :]
            if z.r2p > z.r2:
                piece = jnp.concatenate([piece, jnp.zeros((z.r2p - z.r2, D), f32)], axis=0)
            ga_ref[at, kk * z.r2p : (kk + 1) * z.r2p, :] = piece
        ga_ref[at, z.n_model * z.r2p :, :] = gneg_ref[at * z.rn : (at + 1) * z.rn, :]

    for i in range(half):
        wp_copy(side * half + i).wait_send()
        n5_copy(side * half + i).wait_send()
    for i in range(1, half):
        to = lax.rem(chip + i, half)
        wc_copy(i, here, to).wait_send()
        n2_copy(i, chip, to).wait_send()
        n4_copy(i, here, to).wait_send()
    for i in range(1, n_model):
        at = lax.rem(k + i, n_model)
        wz_copy(i, k, at).wait_send()
        n3_copy(i, k, at).wait_send()
        bz_copy(i, k, at).wait_send()
    n1_copy.wait_send()

    def finish(i, carry):
        at = lax.rem(me + i, n_every)
        ask_copy(at, at, at).wait_send()
        row_copy(z.groups - 1, at, at, at).wait_send()
        return carry

    lax.fori_loop(1, n_every, finish, 0)


def front(z, scalars, table, w_f1, w_f2, bias_tile, owner, local, ids, bucket, gains):
    sds = jax.ShapeDtypeStruct
    dma = pltpu.SemaphoreType.DMA
    vm = pltpu.VMEM
    per_side = z.half * MB * z.rn
    every, model, half, data = (z.n_every,), (z.n_model,), (z.half,), (z.n_data,)
    groups_every = (z.groups, z.n_every)
    pairs_shape = sds((PAIRS, LEN, WIDE), bf16)
    return pl.pallas_call(
        functools.partial(front_kernel, z),
        out_shape=(
            sds((z.n_every, 1, LANES), f32),
            sds((NT, 1, TB), f32),
            sds((z.n_data, z.n_model, z.rw, D), bf16),
            sds((z.n_model, 8, LANES), f32),
            sds((LEN, D), bf16), sds((LEN, D), bf16),
            pairs_shape, pairs_shape, pairs_shape, pairs_shape,
            sds((LEN, D), bf16), sds((LEN, D), f32),
            sds((z.n_data, z.ra, D), f32), sds((8, D), f32),
        ),
        in_specs=[pl.BlockSpec(memory_space=pltpu.SMEM)] + [VM] * 9,
        out_specs=(VM,) * 14,
        scratch_shapes=[
            vm(table.shape, bf16),
            vm((z.n_every, 1, LANES), f32),
            vm((z.groups, z.n_every, CH, D), bf16),
            vm((z.groups, z.n_every, CH, D), bf16),
            vm((2, per_side, D), bf16),
            vm((per_side, D), bf16),
            vm((z.half, MB * z.rn, D), bf16),
            vm((z.n_model, z.rn, D), bf16),
            vm((per_side, D), bf16),
            vm((MB, z.rn, D), bf16),
            vm((z.n_data, z.rn, D), bf16),
            vm((LEN + 8, D), f32),
            vm((LEN, D), f32),
            vm((PAIRS, LEN, WIDE), f32),
            vm((8, D), f32),
            vm((NT, 8, TB), f32),
            vm((4, D, D), bf16),
            vm((D, D), bf16),
            vm((D, D), f32),
            vm((z.n_data * z.rn, D), f32),
            dma(every), dma(every), dma(groups_every), dma(groups_every),
            dma(model), dma(model), dma(half), dma(data), dma(data), dma(data), dma(model), dma(model),
            dma, dma, dma(half), dma(half), dma(model), dma(model), dma(half), dma(data), dma(data), dma(data),
        ],
        compiler_params=pltpu.CompilerParams(
            collective_id=0, has_side_effects=True, vmem_limit_bytes=LIMIT
        ),
        cost_estimate=pl.CostEstimate(
            flops=60_000_000_000, bytes_accessed=30_000_000, transcendentals=6_000_000
        ),
        name="front",
    )(scalars, table, w_f1, w_f2, bias_tile, owner, local, ids, bucket, gains)


def rear_kernel(
    z, len_ref, x_ref, n1_ref, q_ref, k_ref, v_ref, do_ref, ghu_ref, gres_ref, w_ref, bias_ref, bucket_ref,
    gains_ref, slot_ref, stat_in_ref, ga_ref, asked_ref, ids_ref,
    tg_ref, wg_ref, packs_ref, squares_ref,
    gh_ref, hid_ref, kb_ref, dq_ref, dk_ref, dv_ref, kt_ref, bs_ref, w1_ref, stat_ref, pack_ref, out_ref, gb_ref,
    got_ref, pa_ref, pb_ref, sa_ref, sb_ref, ca_ref, cb_ref, zs_ref, zr_ref, ng_ref, sq_ref,
    row_send, row_recv, pack_send, pack_recv,
    pa_send, pa_recv, pb_send, pb_recv, ca_send, ca_recv, cb_send, cb_recv,
    zw_send, zw_recv, zf_send, zf_recv, zn_send, zn_recv, gw_send, gw_recv, gn_send, gn_recv,
    hw_send, hw_recv, hn_send, hn_recv, sq_send, sq_recv,
):
    n_every, n_model, half = z.n_every, z.n_model, z.half
    slots = z.slots
    d = lax.axis_index("dp")
    k = lax.axis_index("mp")
    me = d * n_model + k
    side = lax.rem(d, 2)
    chip = d // 2
    here = side * half + chip
    other = d + 1 - 2 * side
    micro = k // z.copies
    barrier = pltpu.get_barrier_semaphore()

    def signal(i, carry):
        to = spot(lax.rem(me + i, n_every), n_model)
        pl.semaphore_signal(barrier, inc=1, device_id=to, device_id_type=MESH)
        return carry

    lax.fori_loop(1, n_every, signal, 0)

    pa_copy = remote(ga_ref.at[1 - side], pa_ref, pa_send, pa_recv, (other, k))

    def pb_copy(p):
        return remote(gb_ref.at[1 - side, p], pb_ref.at[p], pb_send.at[p], pb_recv.at[p], (other, k))

    def row_copy(g, src, dst, to):
        return remote(
            out_ref.at[g, to], got_ref.at[g, dst], row_send.at[g, to], row_recv.at[g, src],
            spot(to, n_model),
        )

    def pack_copy(src, dst, to):
        return remote(
            pack_ref, packs_ref.at[dst], pack_send.at[to], pack_recv.at[src], spot(to, n_model)
        )

    def ca_copy(i, at, to):
        return remote(
            sa_ref.at[to], ca_ref.at[at], ca_send.at[i], ca_recv.at[at], (2 * to + side, k)
        )

    def cb_copy(p, i, at, to):
        return remote(
            sb_ref.at[p, to], cb_ref.at[p, at], cb_send.at[p, i], cb_recv.at[p, at], (2 * to + side, k)
        )

    def zn_copy(i, at, to):
        return remote(
            ng_ref.at[here, at], ng_ref.at[here, at], zn_send.at[i], zn_recv.at[at], (d, to)
        )

    def zw_copy(at, to):
        part = pl.ds(0, z.r1)
        return remote(
            zs_ref.at[to, part], zr_ref.at[at, part], zw_send.at[to], zw_recv.at[at], (d, to)
        )

    def zf_copy(at, to):
        part = pl.ds(z.r1, z.r2p)
        return remote(
            zs_ref.at[to, part], zr_ref.at[at, part], zf_send.at[to], zf_recv.at[at], (d, to)
        )

    def gw_copy(i, at, to):
        return remote(
            wg_ref.at[at], wg_ref.at[at], gw_send.at[i], gw_recv.at[at], (2 * to + side, k)
        )

    def gn_copy(i, at, to):
        return remote(
            ng_ref.at[at], ng_ref.at[at], gn_send.at[i], gn_recv.at[at], (2 * to + side, k)
        )

    def hw_copy(at):
        return remote(wg_ref.at[at], wg_ref.at[at], hw_send.at[at], hw_recv.at[at], (other, k))

    def hn_copy(at):
        return remote(ng_ref.at[at], ng_ref.at[at], hn_send.at[at], hn_recv.at[at], (other, k))

    def sq_copy(src, dst, to):
        return remote(
            sq_ref, squares_ref.at[dst], sq_send.at[to], sq_recv.at[src], spot(to, n_model)
        )

    def chips_a():
        pa_copy.wait_recv()
        sa_ref[...] = (ga_ref[side] + pa_ref[...]).astype(bf16)
        for i in range(1, half):
            ca_copy(i, chip, lax.rem(chip + i, half)).start()

    def chips_b(p):
        pb_copy(p).wait_recv()
        sb_ref[p] = (gb_ref[side, p] + pb_ref[p]).astype(bf16)
        for i in range(1, half):
            cb_copy(p, i, chip, lax.rem(chip + i, half)).start()

    def planes_a():
        total = sa_ref[chip].astype(f32)
        for i in range(1, half):
            at = lax.rem(chip + i, half)
            ca_copy(i, at, chip).wait_recv()
            total = total + ca_ref[at].astype(f32)
        ng_ref[here, k] = total[n_model * z.r2p :].astype(bf16)
        zs_ref[:, z.r1 :, :] = total[: n_model * z.r2p].reshape(n_model, z.r2p, D)
        for i in range(1, n_model):
            to = lax.rem(k + i, n_model)
            zn_copy(i, k, to).start()
            zf_copy(k, to).start()

    def planes_b(p):
        total = sb_ref[p, chip].astype(f32)
        for i in range(1, half):
            at = lax.rem(chip + i, half)
            cb_copy(p, i, at, chip).wait_recv()
            total = total + cb_ref[p, at].astype(f32)
        for i in range(z.npp):
            to = p * z.npp + i
            zs_ref[to, : z.r1, :] = total[i * z.r1 : (i + 1) * z.r1]
            pl.when(k != to)(lambda to=to: zw_copy(k, to).start())

    def spread_a():
        for i in range(1, n_model):
            zn_copy(i, lax.rem(k + i, n_model), k).wait_recv()
        for i in range(1, half):
            gn_copy(i, here, lax.rem(chip + i, half)).start()
        hn_copy(here).start()

    def swap_a():
        for i in range(1, half):
            at = side * half + lax.rem(chip + i, half)
            gn_copy(i, at, chip).wait_recv()
            hn_copy(at).start()

    gain_in = gains_ref[0:1, :]
    place_weights(z, w_ref, w1_ref, None)
    kb_ref[...] = key_bias(bias_ref, bucket_ref[micro], len_ref[micro, 0]).T

    def inputs(i, carry):
        rows = pl.ds(pl.multiple_of(i * TB, TB), TB)
        for c in (1, 2, 3):
            hid_ref[c - 1, rows, :] = mm(n1_ref[rows, :], w1_ref[c], NT_)
        return carry

    lax.fori_loop(0, NT, inputs, 0)
    bs_ref[...] = jnp.zeros_like(bs_ref)
    in_row = lax.broadcasted_iota(jnp.int32, (2 * TB, TB), 0)
    in_col = lax.broadcasted_iota(jnp.int32, (2 * TB, TB), 1)
    causal = lax.rem(in_row, TB) <= in_col
    ones_lane = lax.broadcasted_iota(jnp.int32, (2 * TB, LANES), 1)
    ones_half = lax.broadcasted_iota(jnp.int32, (2 * TB, LANES), 0) >= TB
    stat_ref[...] = jnp.zeros_like(stat_ref)
    per_group = z.group_len // TB

    def outputs(i):
        rows = pl.ds(pl.multiple_of(i * TB, TB), TB)
        gn = mm(ghu_ref[rows, :], w1_ref[0])
        for c in (1, 2, 3):
            gn += mm(gh_ref[c - 1, rows, :], w1_ref[c])
        x = x_ref[rows, :].astype(f32)
        factor = lax.rsqrt(jnp.mean(x * x, -1, keepdims=True) + epsilon)
        scaled = gn * gain_in
        gx = factor * (scaled - x * factor * factor * jnp.mean(x * scaled, -1, keepdims=True))
        gx = (gx + gres_ref[rows, :]).astype(bf16)
        stat_ref[0:1, :] += row_sum(gn * x * factor)
        group = i // per_group
        hot = lax.broadcasted_iota(jnp.int32, (slots, TB), 0).astype(f32) == slot_ref[i]
        mine = mm(jnp.where(hot, 1.0, 0.0).astype(bf16), gx).astype(bf16)
        mine = mine.reshape(z.n_every, CH, D)
        if per_group == 1:
            out_ref[group] = mine
        else:
            out_ref[group] = jnp.where(lax.rem(i, per_group) == 0, mine, out_ref[group] + mine)

    def send_group(g):
        def send(i, carry):
            row_copy(g, me, me, lax.rem(me + i, n_every)).start()
            return carry

        lax.fori_loop(1, n_every, send, 0)
        got_ref[g, me] = out_ref[g, me]

    def weights_grad(p):
        lanes = slice(p * WIDE, (p + 1) * WIDE)
        for c in range(4):
            left = ghu_ref[:, lanes] if c == 0 else gh_ref[c - 1, :, lanes]
            grads = mm(left, n1_ref[...], TN)
            for side_head in range(2):
                head = 2 * p + side_head
                for dd in range(z.n_data):
                    own_head, part, first = z.block(dd)
                    if part == c and own_head == head % z.heads_dev:
                        at = head // z.heads_dev - p * z.npp
                        gb_ref[dd % 2, p, dd // 2, at * z.r1 : (at + 1) * z.r1, :] = grads[
                            side_head * DH + first : side_head * DH + first + z.r1
                        ]
        pb_copy(p).start()

    early = range(PAIRS - SPAN)
    late = range(PAIRS - SPAN, PAIRS)

    def first_hook():
        for p in early:
            chips_b(p)

    def second_hook():
        swap_a()
        for p in early:
            planes_b(p)

    def late_weights():
        for p in late:
            weights_grad(p)

    pl.semaphore_wait(barrier, n_every - 1)
    pa_copy.start()

    def keys_of(p, j):
        keys = pl.ds(pl.multiple_of(j * TB, TB), TB)
        at = p % SPAN
        kt = k_ref[p, keys, :].astype(f32).T
        low = lax.broadcasted_iota(jnp.int32, kt.shape, 0) < DH
        kt_ref[at] = jnp.concatenate(
            [jnp.where(low, kt, 0.0), jnp.where(low, 0.0, kt)], axis=1
        ).astype(bf16)
        dk_ref[at] = jnp.zeros((TB, WIDE + LANES), f32)
        dv_ref[at] = jnp.zeros((TB, WIDE), f32)

    def part(p, i, j, masked):
        keys = pl.ds(pl.multiple_of(j * TB, TB), TB)
        rows = pl.ds(pl.multiple_of(i * TB, TB), TB)
        at = p % SPAN
        q = q_ref[p, rows, :]
        do = do_ref[p, rows, :]
        kb = jnp.concatenate(
            [kb_ref[keys, 2 * p : 2 * p + 1], kb_ref[keys, 2 * p + 1 : 2 * p + 2]], axis=0
        )
        mark = jnp.where(
            ones_lane == jnp.where(ones_half, 2 * p + 1, 2 * p), 1.0, 0.0
        ).astype(bf16)
        place = lax.broadcasted_iota(jnp.int32, (1, TB), 1) + i * TB
        inv = 1.0 / (place.astype(f32) + 1.0)
        h = mm(halves(k_ref[p, keys, :]), q, NT_) + kb
        t = jnp.tanh(h)
        m = h * t
        w = (h + m) * inv
        ds = mm(halves(v_ref[p, keys, :]), do, NT_) * ((1.0 + t) * (0.5 * inv)) * (1.0 + h - m)
        if masked:
            w = jnp.where(causal, w, 0.0)
            ds = jnp.where(causal, ds, 0.0)
        ds = ds.astype(bf16)
        dv_ref[at] += mm(beside(w.astype(bf16)), halves(do))
        dk_ref[at] += mm(beside(ds), jnp.concatenate([halves(q), mark], axis=1))
        dq_ref[at, i] += mm(kt_ref[at], ds)

    def keys_end(p, j):
        keys = pl.ds(pl.multiple_of(j * TB, TB), TB)
        lanes = slice(p * WIDE, (p + 1) * WIDE)
        at = p % SPAN
        slope_v = silu_parts(hid_ref[0, keys, lanes])[1]
        slope_k = silu_parts(hid_ref[2, keys, lanes])[1]
        slope_q = silu_parts(hid_ref[1, keys, lanes])[1]
        gh_ref[0, keys, lanes] = (dv_ref[at] * slope_v).astype(bf16)
        gh_ref[2, keys, lanes] = (dk_ref[at, :, :WIDE] * 2.0 * slope_k).astype(bf16)
        gh_ref[1, keys, lanes] = (dq_ref[at, j].T * DH ** (-0.5) * slope_q).astype(bf16)
        bs_ref[keys, :] += dk_ref[at, :, WIDE:]

    for phase in range(PAIRS // SPAN):
        pairs = range(phase * SPAN, (phase + 1) * SPAN)
        final = phase == PAIRS // SPAN - 1
        dq_ref[...] = jnp.zeros_like(dq_ref)

        def keys_step(j, carry, pairs=pairs, final=final, phase=phase):
            for p in pairs:
                keys_of(p, j)
            for p in pairs:
                part(p, j, j, True)

            def later(i, inner):
                for p in pairs:
                    part(p, i, j, False)
                return inner

            lax.fori_loop(j + 1, NT, later, 0)
            for p in pairs:
                keys_end(p, j)
            if phase == 0:
                pl.when(j == 0)(chips_a)
                pl.when(j == 1)(planes_a)
                pl.when(j == 2)(spread_a)
            if final:
                pl.when(j == NT - 1)(late_weights)
                outputs(j)
                if per_group == 1:
                    send_group(j)
                pl.when(j == 0)(first_hook)
                pl.when(j == 2)(second_hook)
            return carry

        lax.fori_loop(0, NT, keys_step, 0)
        if not final:
            for p in pairs:
                weights_grad(p)

    if per_group > 1:
        for g in range(z.groups):
            send_group(g)
    hot = jnp.where(
        lax.broadcasted_iota(jnp.int32, (NB, LEN), 0) == bucket_ref[micro], 1.0, 0.0
    )
    bias_grad = lax.dot_general(hot, bs_ref[...], NN, precision=highest, preferred_element_type=f32)
    for i in range(D // LANES):
        lanes = slice(i * LANES, (i + 1) * LANES)
        pack_ref[i : i + 1] = stat_ref[0:1, lanes]
        pack_ref[4 + i : 5 + i] = stat_in_ref[1:2, lanes]
        pack_ref[8 + i : 9 + i] = stat_in_ref[2:3, lanes]
    pack_ref[12:14] = stat_in_ref[3:5, :LANES]
    pack_ref[14:16] = jnp.zeros((2, LANES), f32)
    pack_ref[16:24] = bias_grad.T[0:8, :]
    packs_ref[me] = pack_ref[...]

    def pack_all(i, carry):
        pack_copy(me, me, lax.rem(me + i, n_every)).start()
        return carry

    lax.fori_loop(1, n_every, pack_all, 0)

    tg_ref[...] = jnp.zeros_like(tg_ref)
    wide = min(TB, slots)
    ask_at = lax.broadcasted_iota(jnp.int32, (z.rows_dev, wide), 0).astype(f32)

    def collect(g):
        def wait(i, carry):
            at = lax.rem(me + i, n_every)
            row_copy(g, at, at, at).wait_recv()
            return carry

        lax.fori_loop(1, n_every, wait, 0)
        for b in range(slots // wide):
            asked = asked_ref[g][:, b * wide : (b + 1) * wide]
            hot = jnp.where(ask_at == asked, 1.0, 0.0).astype(bf16)
            rows = got_ref[g, b * (wide // CH) : (b + 1) * (wide // CH)].reshape(wide, D)
            tg_ref[...] += mm(hot, rows)

    neg_rows = n_model * z.rn
    row_at = lax.broadcasted_iota(jnp.int32, (z.rows_dev, neg_rows), 0).astype(f32)
    base = (me * z.rows_dev).astype(f32)

    def negatives(at):
        hot = jnp.where(row_at == ids_ref[at] - base, 1.0, 0.0).astype(bf16)
        tg_ref[...] += mm(hot, ng_ref[at].reshape(neg_rows, D))

    for p in late:
        chips_b(p)
    collect(0)
    for i in range(half):
        negatives(side * half + i)
    for i in range(half):
        hn_copy((1 - side) * half + i).wait_recv()
        negatives((1 - side) * half + i)
    for p in late:
        planes_b(p)
    for g in range(1, max(1, z.groups - 1)):
        collect(g)
    total = zs_ref[k]
    for i in range(1, n_model):
        at = lax.rem(k + i, n_model)
        zw_copy(at, k).wait_recv()
        zf_copy(at, k).wait_recv()
        total = total + zr_ref[at]
    wg_ref[here] = total
    for i in range(1, half):
        gw_copy(i, here, lax.rem(chip + i, half)).start()
    hw_copy(here).start()
    if z.groups > 1:
        collect(z.groups - 1)

    table_grad = tg_ref[...]
    slice_grad = wg_ref[here]
    squares = row_sum(table_grad * table_grad) + row_sum(slice_grad * slice_grad)
    sq_ref[...] = sum(squares[:, i * LANES : (i + 1) * LANES] for i in range(D // LANES))
    squares_ref[me] = sq_ref[...]

    def share(i, carry):
        to = lax.rem(me + i, n_every)
        sq_copy(me, me, to).start()
        return carry

    lax.fori_loop(1, n_every, share, 0)
    for i in range(1, half):
        at = side * half + lax.rem(chip + i, half)
        gw_copy(i, at, chip).wait_recv()
        hw_copy(at).start()
    for i in range(half):
        hw_copy((1 - side) * half + i).wait_recv()
        hw_copy(side * half + i).wait_send()
        hn_copy(side * half + i).wait_send()
    for i in range(1, half):
        to = lax.rem(chip + i, half)
        ca_copy(i, chip, to).wait_send()
        for p in range(PAIRS):
            cb_copy(p, i, chip, to).wait_send()
        gn_copy(i, here, to).wait_send()
        gw_copy(i, here, to).wait_send()
    for i in range(1, n_model):
        to = lax.rem(k + i, n_model)
        zn_copy(i, k, to).wait_send()
        zw_copy(k, to).wait_send()
        zf_copy(k, to).wait_send()
    pa_copy.wait_send()
    for p in range(PAIRS):
        pb_copy(p).wait_send()

    def finish(i, carry):
        at = lax.rem(me + i, n_every)
        for g in range(z.groups):
            row_copy(g, at, at, at).wait_send()
        pack_copy(at, at, at).wait_send()
        pack_copy(at, at, at).wait_recv()
        sq_copy(at, at, at).wait_send()
        sq_copy(at, at, at).wait_recv()
        return carry

    lax.fori_loop(1, n_every, finish, 0)


def rear(
    z, scalars, x, n1, q, k, v, do, ghu, gres, w, bias, bucket, gains, slot, stat, ga, asked, ids
):
    sds = jax.ShapeDtypeStruct
    dma = pltpu.SemaphoreType.DMA
    vm = pltpu.VMEM
    every, model, half, data = (z.n_every,), (z.n_model,), (z.half,), (z.n_data,)
    groups_every = (z.groups, z.n_every)
    pairs, pairs_half = (PAIRS,), (PAIRS, z.half)
    rows_b = z.npp * z.r1
    return pl.pallas_call(
        functools.partial(rear_kernel, z),
        out_shape=(
            sds((z.rows_dev, D), f32),
            sds((z.n_data, z.rw, D), f32),
            sds((z.n_every, 24, LANES), f32),
            sds((z.n_every, 1, LANES), f32),
        ),
        in_specs=[pl.BlockSpec(memory_space=pltpu.SMEM)] + [VM] * 17,
        out_specs=(VM,) * 4,
        scratch_shapes=[
            vm((3, LEN, D), bf16),
            vm((3, LEN, D), f32),
            vm((LEN, 8), f32),
            vm((SPAN, NT, WIDE, TB), f32),
            vm((SPAN, TB, WIDE + LANES), f32),
            vm((SPAN, TB, WIDE), f32),
            vm((SPAN, WIDE, 2 * TB), bf16),
            vm((LEN, LANES), f32),
            vm((4, D, D), bf16),
            vm((8, D), f32),
            vm((24, LANES), f32),
            vm((z.groups, z.n_every, CH, D), bf16),
            vm((2, PAIRS, z.half, rows_b, D), f32),
            vm((z.groups, z.n_every, CH, D), bf16),
            vm((z.half, z.ra, D), f32),
            vm((PAIRS, z.half, rows_b, D), f32),
            vm((z.half, z.ra, D), bf16),
            vm((PAIRS, z.half, rows_b, D), bf16),
            vm((z.half, z.ra, D), bf16),
            vm((PAIRS, z.half, rows_b, D), bf16),
            vm((z.n_model, z.rw, D), f32),
            vm((z.n_model, z.rw, D), f32),
            vm((z.n_data, z.n_model, z.rn, D), bf16),
            vm((1, LANES), f32),
            dma(groups_every), dma(groups_every), dma(every), dma(every),
            dma, dma, dma(pairs), dma(pairs), dma(half), dma(half), dma(pairs_half), dma(pairs_half),
            dma(model), dma(model), dma(model), dma(model), dma(model), dma(model),
            dma(half), dma(data), dma(half), dma(data),
            dma(data), dma(data), dma(data), dma(data), dma(every), dma(every),
        ],
        compiler_params=pltpu.CompilerParams(
            collective_id=1, has_side_effects=True, vmem_limit_bytes=LIMIT
        ),
        cost_estimate=pl.CostEstimate(
            flops=60_000_000_000, bytes_accessed=30_000_000, transcendentals=6_000_000
        ),
        name="rear",
    )(scalars, x, n1, q, k, v, do, ghu, gres, w, bias, bucket, gains, slot, stat, ga, asked, ids)


def adam_step(weight, grad, first, second, rate, decay):
    first_new = beta_one * first + (1.0 - beta_one) * grad
    second_new = beta_two * second + (1.0 - beta_two) * grad * grad
    fix_one = 1.0 - beta_one**STEP
    fix_two = 1.0 - beta_two**STEP
    move = first_new / fix_one / (jnp.sqrt(second_new / fix_two) + adam_floor) + decay * weight
    return (weight - rate * move, first_new, second_new)


def settle_kernel(
    z, squares_ref, packs_ref, wg_ref, tg_ref, t_ref, tm_ref, tv_ref, a_ref, am_ref, av_ref,
    b_ref, bm_ref, bv_ref, c_ref, cm_ref, cv_ref, e_ref, em_ref, ev_ref,
    t_out, tm_out, tv_out, tl_out, a_out, am_out, av_out, al_out, b_out, bm_out, bv_out, bl_out,
    c_out, cm_out, cv_out, e_out, em_out, ev_out, flat_out, factor_ref, one_ref,
):
    def update(grad, refs, outs, rate, decay):
        new, first, second = adam_step(refs[0][...], grad, refs[1][...], refs[2][...], rate, decay)
        outs[0][...] = new
        outs[1][...] = first
        outs[2][...] = second
        if len(outs) > 3:
            outs[3][...] = new.astype(bf16)

    @pl.when(pl.program_id(0) == 0)
    def _():
        packs = jnp.sum(packs_ref[...], axis=0)
        gain_grad = jnp.concatenate(
            [
                jnp.concatenate([packs[4 * r + i : 4 * r + i + 1] for i in range(D // LANES)], axis=1)
                for r in range(3)
            ],
            axis=0,
        )
        bias_all = packs[16:24]
        squares = jnp.sum(squares_ref[...], axis=0) + row_sum(packs[0:12] * packs[0:12])
        squares = squares + row_sum(bias_all * bias_all)
        norm = jnp.sqrt(jnp.sum(squares, axis=1, keepdims=True))
        factor = jnp.minimum(1.0, clip_at / norm)
        factor_ref[...] = jnp.broadcast_to(factor, factor_ref.shape)
        flat_out[0:2] = packs[12:14]
        flat_out[2:3] = jnp.broadcast_to(norm, (1, LANES))
        flat_out[3:8] = jnp.zeros((5, LANES), f32)
        one = jnp.concatenate([wg_ref[z.order(d), 0 : z.r1] for d in range(z.n_data)], axis=0)
        two = jnp.concatenate(
            [wg_ref[z.order(d), z.r1 : z.r1 + z.r2] for d in range(z.n_data)], axis=0
        )
        one_ref[...] = one.T * factor
        update(two * factor, (b_ref, bm_ref, bv_ref), (b_out, bm_out, bv_out, bl_out), 0.04, 0.1)
        update(gain_grad * factor, (c_ref, cm_ref, cv_ref), (c_out, cm_out, cv_out), 0.5, 0.0)
        head = lax.broadcasted_iota(jnp.int32, bias_all.shape, 0)
        first_head = lax.axis_index("mp") * z.heads_dev
        mine = [
            row_sum(jnp.where(head == first_head + r, bias_all, 0.0)) for r in range(z.heads_dev)
        ]
        bias_grad = jnp.concatenate(mine, axis=0)
        update(bias_grad * factor, (e_ref, em_ref, ev_ref), (e_out, em_out, ev_out), 1.0, 0.0)

    size = a_ref.shape[0]
    rows = pl.ds(pl.multiple_of(pl.program_id(0) * size, size), size)
    update(one_ref[rows, :], (a_ref, am_ref, av_ref), (a_out, am_out, av_out, al_out), 0.04, 0.1)
    update(
        tg_ref[...] * factor_ref[0:1, 0:1], (t_ref, tm_ref, tv_ref), (t_out, tm_out, tv_out, tl_out), 0.5, 0.1
    )


def settle(z, squares, packs, wg, tg, table, f1, f2, gains, bias):
    sds = jax.ShapeDtypeStruct
    rows = next(r for r in range(112, 0, -16) if z.rows_dev % r == 0)
    blocks = z.rows_dev // rows
    steps = next(n for n in range(blocks, 512) if D % n == 0 and D // n % 16 == 0)
    block = pl.BlockSpec((rows, D), lambda i: (jnp.minimum(i, blocks - 1), 0))
    part = pl.BlockSpec((D // steps, 4 * z.fw), lambda i: (i, 0))

    def like(array, dtype=f32):
        return sds(array.shape, dtype)

    return pl.pallas_call(
        functools.partial(settle_kernel, z),
        grid=(steps,),
        out_shape=(
            like(tg), like(tg), like(tg), like(tg, bf16),
            like(f1[0]), like(f1[0]), like(f1[0]), like(f1[0], bf16),
            like(f2[0]), like(f2[0]), like(f2[0]), like(f2[0], bf16),
            like(gains[0]), like(gains[0]), like(gains[0]),
            like(bias[0]), like(bias[0]), like(bias[0]), sds((8, LANES), f32),
        ),
        in_specs=[VM] * 3 + [block] * 4 + [part] * 3 + [VM] * 9,
        out_specs=(block,) * 4 + (part,) * 4 + (VM,) * 11,
        scratch_shapes=[pltpu.VMEM((8, LANES), f32), pltpu.VMEM((D, 4 * z.fw), f32)],
        compiler_params=pltpu.CompilerParams(vmem_limit_bytes=LIMIT),
        cost_estimate=pl.CostEstimate(
            flops=20 * z.rows_dev * D, bytes_accessed=20_000_000, transcendentals=1_000_000
        ),
        name="settle",
    )(squares, packs, wg, tg, *table, *f1, *f2, *gains, *bias)


def settle_kernel(
    z, squares_ref, packs_ref, wg_ref, tg_ref, t_ref, tm_ref, tv_ref, a_ref, am_ref, av_ref,
    b_ref, bm_ref, bv_ref, c_ref, cm_ref, cv_ref, e_ref, em_ref, ev_ref,
    t_out, tm_out, tv_out, tl_out, a_out, am_out, av_out, al_out, b_out, bm_out, bv_out, bl_out,
    c_out, cm_out, cv_out, e_out, em_out, ev_out, flat_out, factor_ref, one_ref,
):
    def update(grad, refs, outs, rate, decay):
        new, first, second = adam_step(refs[0][...], grad, refs[1][...], refs[2][...], rate, decay)
        outs[0][...] = new
        outs[1][...] = first
        outs[2][...] = second
        if len(outs) > 3:
            outs[3][...] = new.astype(bf16)

    @pl.when(pl.program_id(0) == 0)
    def _():
        packs = jnp.sum(packs_ref[...], axis=0)
        gain_grad = jnp.concatenate(
            [
                jnp.concatenate([packs[4 * r + i : 4 * r + i + 1] for i in range(D // LANES)], axis=1)
                for r in range(3)
            ],
            axis=0,
        )
        bias_all = packs[16:24]
        squares = jnp.sum(squares_ref[...], axis=0) + row_sum(packs[0:12] * packs[0:12])
        squares = squares + row_sum(bias_all * bias_all)
        norm = jnp.sqrt(jnp.sum(squares, axis=1, keepdims=True))
        factor = jnp.minimum(1.0, clip_at / norm)
        factor_ref[...] = jnp.broadcast_to(factor, factor_ref.shape)
        flat_out[0:2] = packs[12:14]
        flat_out[2:3] = jnp.broadcast_to(norm, (1, LANES))
        flat_out[3:8] = jnp.zeros((5, LANES), f32)
        one = jnp.concatenate([wg_ref[z.order(d), 0 : z.r1] for d in range(z.n_data)], axis=0)
        two = jnp.concatenate(
            [wg_ref[z.order(d), z.r1 : z.r1 + z.r2] for d in range(z.n_data)], axis=0
        )
        one_ref[...] = one.T * factor
        update(two * factor, (b_ref, bm_ref, bv_ref), (b_out, bm_out, bv_out, bl_out), 0.04, 0.1)
        update(gain_grad * factor, (c_ref, cm_ref, cv_ref), (c_out, cm_out, cv_out), 0.5, 0.0)
        head = lax.broadcasted_iota(jnp.int32, bias_all.shape, 0)
        first_head = lax.axis_index("mp") * z.heads_dev
        mine = [
            row_sum(jnp.where(head == first_head + r, bias_all, 0.0)) for r in range(z.heads_dev)
        ]
        bias_grad = jnp.concatenate(mine, axis=0)
        update(bias_grad * factor, (e_ref, em_ref, ev_ref), (e_out, em_out, ev_out), 1.0, 0.0)

    size = a_ref.shape[0]
    rows = pl.ds(pl.multiple_of(pl.program_id(0) * size, size), size)
    update(one_ref[rows, :], (a_ref, am_ref, av_ref), (a_out, am_out, av_out, al_out), 0.04, 0.1)
    update(
        tg_ref[...] * factor_ref[0:1, 0:1], (t_ref, tm_ref, tv_ref), (t_out, tm_out, tv_out, tl_out), 0.5, 0.1
    )


def settle(z, squares, packs, wg, tg, table, f1, f2, gains, bias):
    sds = jax.ShapeDtypeStruct
    rows = next(r for r in range(112, 0, -16) if z.rows_dev % r == 0)
    blocks = z.rows_dev // rows
    steps = next(n for n in range(blocks, 512) if D % n == 0 and D // n % 16 == 0)
    block = pl.BlockSpec((rows, D), lambda i: (jnp.minimum(i, blocks - 1), 0))
    part = pl.BlockSpec((D // steps, 4 * z.fw), lambda i: (i, 0))

    def like(array, dtype=f32):
        return sds(array.shape, dtype)

    return pl.pallas_call(
        functools.partial(settle_kernel, z),
        grid=(steps,),
        out_shape=(
            like(tg), like(tg), like(tg), like(tg, bf16),
            like(f1[0]), like(f1[0]), like(f1[0]), like(f1[0], bf16),
            like(f2[0]), like(f2[0]), like(f2[0]), like(f2[0], bf16),
            like(gains[0]), like(gains[0]), like(gains[0]),
            like(bias[0]), like(bias[0]), like(bias[0]), sds((8, LANES), f32),
        ),
        in_specs=[VM] * 3 + [block] * 4 + [part] * 3 + [VM] * 9,
        out_specs=(block,) * 4 + (part,) * 4 + (VM,) * 11,
        scratch_shapes=[pltpu.VMEM((8, LANES), f32), pltpu.VMEM((D, 4 * z.fw), f32)],
        compiler_params=pltpu.CompilerParams(vmem_limit_bytes=LIMIT),
        cost_estimate=pl.CostEstimate(
            flops=20 * z.rows_dev * D, bytes_accessed=20_000_000, transcendentals=1_000_000
        ),
        name="settle",
    )(squares, packs, wg, tg, *table, *f1, *f2, *gains, *bias)


def pick(array, index):
    return lax.dynamic_index_in_dim(array, index, 0, keepdims=False)


def per_device(
    lengths, owners, item_rows, buckets, negatives, table, table_m, table_v, w_f1, f1_m, f1_v,
    w_f2, f2_m, f2_v, gains, gains_m, gains_v, bias, bias_m, bias_v,
):
    n_model = lax.axis_size("mp")
    n_data = lax.axis_size("dp")
    z = Sizes(n_data, n_model, bias.shape[0], table.shape[0], negatives.shape[1])
    ids = negatives.astype(f32).reshape(MB, n_data, z.rn).transpose(1, 0, 2)
    ids_rows = ids.reshape(-1, 1, LANES)
    ids_cols = jnp.repeat(ids, z.copies, axis=1).reshape(n_data, 1, n_model * z.rn)

    asked, slot, w, bias_all, x, n1, q, k, v, do, ghu, gres, ga, stat_a = front(
        z, lengths, table, w_f1, w_f2, bias, owners.reshape(MB, 1, LEN), item_rows, ids_rows,
        buckets, gains,
    )
    asked = asked.reshape(z.n_every, LANES)[:, : z.groups * CH].reshape(z.n_every, z.groups, CH)
    asked = asked.transpose(1, 0, 2).reshape(z.groups, 1, z.slots)
    table_grad, wg, packs, squares = rear(
        z, lengths, x, n1, q, k, v, do, ghu, gres, w, bias_all, buckets, gains, slot, stat_a,
        ga.reshape(2, z.half, z.ra, D), asked, ids_cols,
    )
    *new, flat = settle(
        z, squares, packs, wg, table_grad, (table, table_m, table_v), (w_f1, f1_m, f1_v),
        (w_f2, f2_m, f2_v), (gains, gains_m, gains_v), (bias, bias_m, bias_v),
    )
    return (flat[0, 0], flat[1, 0], flat[2, 0], *new)


def solution(mesh):
    rows, cols = P(("dp", "mp"), None), P(None, "mp")
    heads = P("mp", None)
    in_specs = (
        P(None, "dp"), P(None, "dp", None, None), P(None, "dp", None), P(None, "dp", None), P(),
        rows, rows, rows, cols, cols, cols, heads, heads, heads, P(), P(), P(), heads, heads, heads,
    )
    out_specs = (
        P(), P(), P(), rows, rows, rows, rows, cols, cols, cols, cols,
        heads, heads, heads, heads, P(), P(), P(), heads, heads, heads,
    )
    return jax.shard_map(
        per_device, mesh=mesh, in_specs=in_specs, out_specs=out_specs, check_vma=False
    )
```

```python
import functools

import jax
import jax.numpy as jnp
from jax import lax
from jax.experimental import pallas as pl
from jax.experimental.pallas import tpu as pltpu
from jax.sharding import PartitionSpec as P

DH = 64
D = 512
NB = 128
LEN = 1024
MB = 4
STEP = 10

TB = 256
NT = LEN // TB
HEADS = D // DH
PAIRS = HEADS // 2
WIDE = 2 * DH
CH = 16
LANES = 128
SPAN = 2

epsilon = 1e-06
clip_at = 1.0
beta_one = 0.9
beta_two = 0.95
adam_floor = 1e-08
highest = lax.Precision.HIGHEST
f32 = jnp.float32
bf16 = jnp.bfloat16
MESH = pl.DeviceIdType.MESH
VM = pl.BlockSpec(memory_space=pltpu.VMEM)
LIMIT = 61 * 1024 * 1024

NN = (((1,), (0,)), ((), ()))
NT_ = (((1,), (1,)), ((), ()))
TN = (((0,), (0,)), ((), ()))


def mm(a, b, dims=NN):
    return lax.dot_general(a, b, dims, preferred_element_type=f32)


def spot(index, n_model):
    return (index // n_model, lax.rem(index, n_model))


def cross(rows):
    lane = lax.broadcasted_iota(jnp.int32, (LANES, LANES), 1)
    eye = lax.broadcasted_iota(jnp.int32, (LANES, LANES), 0) == lane
    spread = jnp.broadcast_to(rows, (LANES, LANES))
    return jnp.sum(jnp.where(eye, spread, 0.0), axis=1, keepdims=True)


def remote(src, dst, send_sem, recv_sem, to):
    return pltpu.make_async_remote_copy(
        src_ref=src,
        dst_ref=dst,
        send_sem=send_sem,
        recv_sem=recv_sem,
        device_id=to,
        device_id_type=MESH,
    )


class Sizes:
    def __init__(self, n_data, n_model, heads_dev, rows_dev, negs):
        self.n_data, self.n_model, self.heads_dev, self.rows_dev = n_data, n_model, heads_dev, rows_dev
        self.n_every = n_data * n_model
        self.copies = n_model // MB
        look = LEN // n_model
        cap = max(2, 2 * look // self.n_every)
        self.group_len = look * max(1, CH // cap)
        self.groups = LEN // self.group_len
        self.slots = self.n_every * CH
        self.fw = heads_dev * DH
        self.half = n_data // 2
        self.r1 = 4 * self.fw // n_data
        self.r2 = self.fw // n_data
        self.r2p = -(-self.r2 // 16) * 16
        self.rw = self.r1 + self.r2p
        self.rn = negs // n_data
        self.ra = n_model * self.r2p + self.rn
        self.npp = n_model // PAIRS

    def order(self, d):
        return (d % 2) * self.half + d // 2

    def block(self, d):
        flat = d * self.r1
        return flat // (4 * DH), flat % (4 * DH) // DH, flat % DH


def silu_parts(values):
    sigma = 0.5 + 0.5 * jnp.tanh(0.5 * values)
    return sigma, sigma * (1.0 + values * (1.0 - sigma))


def halves(tile):
    low = lax.broadcasted_iota(jnp.int32, tile.shape, 1) < DH
    zero = jnp.zeros_like(tile)
    return jnp.concatenate([jnp.where(low, tile, zero), jnp.where(low, zero, tile)], axis=0)


def beside(tile):
    half = tile.shape[0] // 2
    return jnp.concatenate([tile[:half], tile[half:]], axis=1)


def row_sum(values):
    return jnp.sum(values, axis=0, keepdims=True)


def place_weights(z, w_ref, w1_ref, w2_ref):
    for d in range(z.n_data):
        head, part, first = z.block(d)
        for k in range(z.n_model):
            at = k * z.fw + head * DH + first
            w1_ref[part, at : at + z.r1, :] = w_ref[z.order(d), k, 0 : z.r1, :]
            if w2_ref is not None:
                at = k * z.fw + d * z.r2
                w2_ref[at : at + z.r2, :] = w_ref[z.order(d), k, z.r1 : z.r1 + z.r2, :]


def key_bias(bias_ref, bucket, length):
    table = jnp.sum(bias_ref[...], axis=0)
    hot = jnp.where(
        lax.broadcasted_iota(jnp.int32, (NB, LEN), 0) == bucket, 1.0, 0.0
    )
    rows = lax.dot_general(table, hot, NN, precision=highest, preferred_element_type=f32)
    inside = lax.broadcasted_iota(jnp.int32, (8, LEN), 1) < length
    return jnp.where(inside, 0.5 * rows, -1e30)


def front_kernel(
    z, len_ref, table_ref, f1_ref, f2_ref, bias_ref, owner_ref, local_ref, ids_ref, bucket_ref, gains_ref,
    asked_ref, slot_ref, w_ref, bias_all_ref,
    x_ref, n1o_ref, q_ref, k_ref, v_ref, do_ref, ghu_ref, gres_ref, ga_ref, stat_ref,
    low_ref, req_ref, send_ref, got_ref, t2_ref, n1_ref, n2_ref, n3_ref, acc_ref, plane_ref, neg_ref,
    xf_ref, hu_ref, o_ref, carry_ref, kb_ref, w1_ref, w2_ref, gw2_ref, gneg_ref,
    ask_send, ask_recv, row_send, row_recv,
    wz_send, wz_recv, wc_send, wc_recv, wp_send, wp_recv, bz_send, bz_recv,
    n1_send, n1_recv, n2_send, n2_recv, n3_send, n3_recv, n4_send, n4_recv, n5_send, n5_recv,
):
    n_every, n_model, half = z.n_every, z.n_model, z.half
    mine = z.groups * CH
    d = lax.axis_index("dp")
    k = lax.axis_index("mp")
    me = d * n_model + k
    side = lax.rem(d, 2)
    chip = d // 2
    here = side * half + chip
    other = d + 1 - 2 * side
    barrier = pltpu.get_barrier_semaphore()

    def signal(i, carry):
        to = spot(lax.rem(me + i, n_every), n_model)
        pl.semaphore_signal(barrier, inc=1, device_id=to, device_id_type=MESH)
        return carry

    lax.fori_loop(1, n_every, signal, 0)

    micro = k // z.copies
    owner_row = owner_ref[micro].astype(f32)
    value_row = local_ref[micro].astype(f32) + 1.0
    high_row = jnp.floor(value_row * (1.0 / 32.0))
    low_row = value_row - 32.0 * high_row
    length = z.group_len
    earlier = jnp.where(
        lax.broadcasted_iota(jnp.int32, (length, length), 0)
        < lax.broadcasted_iota(jnp.int32, (length, length), 1), 1.0, 0.0
    ).astype(bf16)
    pieces = []
    for g in range(z.groups):
        lanes = slice(g * length, (g + 1) * length)
        own = owner_row[:, lanes]
        owner_at = lax.broadcasted_iota(jnp.int32, (n_every, length), 0).astype(f32)
        hot = jnp.where(owner_at == own, 1.0, 0.0)
        rank = row_sum(mm(hot.astype(bf16), earlier) * hot)
        place = own * CH + rank
        for b in range(length // TB):
            slot_ref[g * (length // TB) + b] = place[:, b * TB : (b + 1) * TB]
        ranks = lax.broadcasted_iota(jnp.int32, (CH, length), 0).astype(f32)
        rank_hot = jnp.where(ranks == rank, 1.0, 0.0).astype(bf16)
        high = mm((hot * high_row[:, lanes]).astype(bf16), rank_hot, NT_)
        lower = mm((hot * low_row[:, lanes]).astype(bf16), rank_hot, NT_)
        pieces.append(high * 32.0 + lower - 1.0)
    pieces.append(jnp.full((n_every, LANES - mine), -1.0, f32))
    wanted = jnp.concatenate(pieces, axis=1)
    for o in range(n_every):
        req_ref[o] = wanted[o : o + 1]

    pl.semaphore_wait(barrier, n_every - 1)

    def ask_copy(src, dst, to):
        return remote(
            req_ref.at[to], asked_ref.at[dst], ask_send.at[to], ask_recv.at[src], spot(to, n_model)
        )

    def ask(i, carry):
        to = lax.rem(me + i, n_every)
        ask_copy(me, me, to).start()
        return carry

    lax.fori_loop(1, n_every, ask, 0)
    asked_ref[me] = req_ref[me]

    take = (
        lax.broadcasted_iota(jnp.int32, (z.r1, 4 * z.fw), 1)
        == lax.broadcasted_iota(jnp.int32, (z.r1, 4 * z.fw), 0) + d * z.r1
    )
    w_ref[here, k, 0 : z.r1, :] = mm(
        jnp.where(take, 1.0, 0.0).astype(bf16), f1_ref[...].astype(bf16), NT_
    ).astype(bf16)
    take = (
        lax.broadcasted_iota(jnp.int32, (z.r2p, z.fw), 1)
        == lax.broadcasted_iota(jnp.int32, (z.r2p, z.fw), 0) + d * z.r2
    )
    w_ref[here, k, z.r1 :, :] = mm(
        jnp.where(take, 1.0, 0.0).astype(bf16), f2_ref[...].astype(bf16)
    ).astype(bf16)
    head = lax.broadcasted_iota(jnp.int32, (HEADS, NB), 0)
    bias_tile = jnp.zeros((HEADS, NB), f32)
    for r in range(z.heads_dev):
        bias_tile += jnp.where(head == k * z.heads_dev + r, bias_ref[r : r + 1, :], 0.0)
    bias_all_ref[k] = bias_tile

    def wz_copy(i, at, to):
        return remote(
            w_ref.at[here, at], w_ref.at[here, at], wz_send.at[i], wz_recv.at[at], (d, to)
        )

    def bz_copy(i, at, to):
        return remote(
            bias_all_ref.at[k], bias_all_ref.at[at], bz_send.at[i], bz_recv.at[at], (d, to)
        )

    for i in range(1, n_model):
        to = lax.rem(k + i, n_model)
        wz_copy(i, k, to).start()
        bz_copy(i, k, to).start()
    low_ref[...] = table_ref[...].astype(bf16)

    def row_copy(g, src, dst, to):
        return remote(
            send_ref.at[g, to], got_ref.at[g, dst], row_send.at[g, to], row_recv.at[g, src],
            spot(to, n_model),
        )

    def asked_all(i, carry):
        src = lax.rem(me + i, n_every)
        ask_copy(src, src, src).wait_recv()
        return carry

    lax.fori_loop(1, n_every, asked_all, 0)
    asked = asked_ref[...].reshape(n_every, LANES) + 1.0
    asked_high = jnp.floor(asked * (1.0 / 32.0))
    asked_low = (asked - 32.0 * asked_high).astype(bf16)
    asked_high = asked_high.astype(bf16)
    per = min(TB // CH, n_every)
    spread = jnp.where(
        lax.broadcasted_iota(jnp.int32, (per * CH, CH), 1)
        == lax.rem(lax.broadcasted_iota(jnp.int32, (per * CH, CH), 0), CH), 1.0, 0.0
    ).astype(bf16)
    turn = lax.broadcasted_iota(jnp.int32, (per * CH, n_every), 0) // CH
    asker = lax.broadcasted_iota(jnp.int32, (per * CH, n_every), 1)
    lane = lax.broadcasted_iota(jnp.int32, (per * CH, z.rows_dev), 1).astype(f32)

    def serve(g):
        lanes = slice(g * CH, (g + 1) * CH)
        for b in range(n_every // per):
            at = mm(spread, asked_high[:, lanes], NT_) * 32.0 + mm(spread, asked_low[:, lanes], NT_)
            at = jnp.where(asker == turn + b * per, at, 0.0)
            column = jnp.sum(at, axis=1, keepdims=True) - 1.0
            hot = jnp.where(lane == column, 1.0, 0.0).astype(bf16)
            found = mm(hot, low_ref[...]).astype(bf16)
            send_ref[g, b * per : (b + 1) * per] = found.reshape(per, CH, D)
        got_ref[g, me] = send_ref[g, me]

    def send_group(g):
        def send(i, carry):
            row_copy(g, me, me, lax.rem(me + i, n_every)).start()
            return carry

        lax.fori_loop(1, n_every, send, 0)

    def release(g):
        def follow(i, carry):
            at = lax.rem(me + i, n_every)
            row_copy(g - 2, at, at, at).wait_send()
            row_copy(g, me, me, at).start()
            return carry

        lax.fori_loop(1, n_every, follow, 0)

    serve(0)
    send_group(0)

    per_side = half * MB * z.rn
    span = MB * z.rn
    n_lane = lax.broadcasted_iota(jnp.int32, (TB, z.rows_dev), 1).astype(f32)

    def negatives(i, carry, first):
        at = first * (per_side // TB) + i
        columns = [cross(ids_ref[at * (TB // LANES) + j]) for j in range(TB // LANES)]
        column = jnp.concatenate(columns, axis=0) - (me * z.rows_dev).astype(f32)
        hot = jnp.where(n_lane == column, 1.0, 0.0).astype(bf16)
        t2_ref[first, pl.ds(pl.multiple_of(i * TB, TB), TB), :] = mm(hot, low_ref[...]).astype(bf16)
        return carry

    def wc_copy(i, at, to):
        return remote(
            w_ref.at[at], w_ref.at[at], wc_send.at[i], wc_recv.at[at], (2 * to + side, k)
        )

    def wp_copy(at):
        return remote(w_ref.at[at], w_ref.at[at], wp_send.at[at], wp_recv.at[at], (other, k))

    n1_copy = remote(t2_ref.at[1 - side], n1_ref, n1_send, n1_recv, (other, k))

    def n2_copy(i, at, to):
        return remote(
            acc_ref.at[pl.ds(pl.multiple_of(to * span, 16), span)], n2_ref.at[at],
            n2_send.at[i], n2_recv.at[at], (2 * to + side, k),
        )

    def n3_copy(i, at, to):
        return remote(
            plane_ref.at[to // z.copies], n3_ref.at[at], n3_send.at[i], n3_recv.at[at], (d, to)
        )

    def n4_copy(i, at, to):
        return remote(
            neg_ref.at[at], neg_ref.at[at], n4_send.at[i], n4_recv.at[at], (2 * to + side, k)
        )

    def n5_copy(at):
        return remote(neg_ref.at[at], neg_ref.at[at], n5_send.at[at], n5_recv.at[at], (other, k))

    for i in range(1, n_model):
        wz_copy(i, lax.rem(k + i, n_model), k).wait_recv()
    for i in range(1, half):
        wc_copy(i, here, lax.rem(chip + i, half)).start()
    wp_copy(here).start()
    lax.fori_loop(0, per_side // TB, functools.partial(negatives, first=1 - side), 0)
    n1_copy.start()
    lax.fori_loop(0, per_side // TB, functools.partial(negatives, first=side), 0)
    if z.groups > 1:
        serve(1)
        send_group(1)
    n1_copy.wait_recv()
    acc_ref[...] = t2_ref[side] + n1_ref[...]
    for i in range(1, half):
        n2_copy(i, chip, lax.rem(chip + i, half)).start()
    for g in range(2, z.groups):
        serve(g)

    length = len_ref[micro, 0]
    lead = (lax.rem(k, z.copies) == 0).astype(jnp.int32)
    gain_in = gains_ref[0:1, :]
    gain_attn = gains_ref[1:2, :]
    gain_out = gains_ref[2:3, :]
    for i in range(1, n_model):
        at = lax.rem(k + i, n_model)
        bz_copy(i, at, k).wait_recv()
    kb = key_bias(bias_all_ref, bucket_ref[micro], length)
    for j in range(NT):
        kb_ref[j] = kb[:, j * TB : (j + 1) * TB]
    xf_ref[LEN:, :] = jnp.zeros((8, D), f32)
    carry_ref[...] = jnp.zeros_like(carry_ref)
    stat_ref[...] = jnp.zeros_like(stat_ref)
    gw2_ref[...] = jnp.zeros_like(gw2_ref)
    gneg_ref[...] = jnp.zeros_like(gneg_ref)
    for i in range(1, half):
        from_chip = lax.rem(chip + i, half)
        wc_copy(i, side * half + from_chip, chip).wait_recv()
        wp_copy(side * half + from_chip).start()
    for i in range(half):
        wp_copy((1 - side) * half + i).wait_recv()
    place_weights(z, w_ref, w1_ref, w2_ref)

    def neg_one():
        total = acc_ref[pl.ds(pl.multiple_of(chip * span, 16), span), :]
        for i in range(1, half):
            from_chip = lax.rem(chip + i, half)
            n2_copy(i, from_chip, chip).wait_recv()
            total = total + n2_ref[from_chip]
        plane_ref[...] = total.reshape(MB, z.rn, D)
        for i in range(1, n_model):
            n3_copy(i, k, lax.rem(k + i, n_model)).start()

    def neg_two():
        total = plane_ref[micro]
        for i in range(1, n_model):
            at = lax.rem(k + i, n_model)
            n3_copy(i, at, k).wait_recv()
            total = total + n3_ref[at]
        neg_ref[here] = total
        for i in range(1, half):
            n4_copy(i, here, lax.rem(chip + i, half)).start()
        n5_copy(here).start()

    def neg_three():
        for i in range(1, half):
            at = side * half + lax.rem(chip + i, half)
            n4_copy(i, at, chip).wait_recv()
            n5_copy(at).start()

    def neg_four():
        for i in range(half):
            n5_copy((1 - side) * half + i).wait_recv()

    slots = z.slots

    def arrive(g):
        def wait(i, carry):
            at = lax.rem(me + i, n_every)
            row_copy(g, at, at, at).wait_recv()
            return carry

        lax.fori_loop(1, n_every, wait, 0)

    def inputs(i):
        rows = pl.ds(pl.multiple_of(i * TB, TB), TB)
        hot = lax.broadcasted_iota(jnp.int32, (slots, TB), 0).astype(f32) == slot_ref[i]
        found = got_ref[i * TB // z.group_len]
        x = mm(jnp.where(hot, 1.0, 0.0).astype(bf16), found.reshape(slots, D), TN)
        x_ref[rows, :] = x.astype(bf16)
        xf_ref[rows, :] = x
        factor = lax.rsqrt(jnp.mean(x * x, -1, keepdims=True) + epsilon)
        n1 = (x * factor * gain_in).astype(bf16)
        n1o_ref[rows, :] = n1
        hu_ref[rows, :] = mm(n1, w1_ref[0], NT_)
        for c, ref in ((1, v_ref), (2, q_ref), (3, k_ref)):
            hidden = mm(n1, w1_ref[c], NT_)
            act = (hidden * silu_parts(hidden)[0]).astype(bf16)
            if c == 2:
                act = act * jnp.asarray(0.5 * DH ** (-0.5), bf16)
            for p in range(PAIRS):
                ref[p, rows, :] = act[:, p * WIDE : (p + 1) * WIDE]

    scale = 2.0 * D ** (-0.5)
    in_row = lax.broadcasted_iota(jnp.int32, (2 * TB, TB), 0)
    in_col = lax.broadcasted_iota(jnp.int32, (2 * TB, TB), 1)
    causal = in_col <= lax.rem(in_row, TB)
    first_half = in_row < TB

    def attend(i):
        rows = pl.ds(pl.multiple_of(i * TB, TB), TB)
        place = lax.broadcasted_iota(jnp.int32, (TB, 1), 0) + i * TB
        inv = 1.0 / (place.astype(f32) + 1.0)
        inv2 = jnp.concatenate([inv, inv], axis=0)
        o_ref[:, rows, :] = jnp.zeros((PAIRS, TB, WIDE), f32)

        def part(j, masked):
            keys = pl.ds(pl.multiple_of(j * TB, TB), TB)
            kb = kb_ref[j]
            for p in range(PAIRS):
                kb2 = jnp.where(first_half, kb[2 * p : 2 * p + 1, :], kb[2 * p + 1 : 2 * p + 2, :])
                h = mm(halves(q_ref[p, rows, :]), k_ref[p, keys, :], NT_) + kb2
                w = (h + h * jnp.tanh(h)) * inv2
                if masked:
                    w = jnp.where(causal, w, 0.0)
                o_ref[p, rows, :] += mm(beside(w.astype(bf16)), halves(v_ref[p, keys, :]))

        def before(j, carry):
            part(j, False)
            return carry

        lax.fori_loop(0, i, before, 0)
        part(i, True)

    def lose(i):
        rows = pl.ds(pl.multiple_of(i * TB, TB), TB)
        place = lax.broadcasted_iota(jnp.int32, (TB, 1), 0) + i * TB
        o = jnp.concatenate([o_ref[p, rows, :] for p in range(PAIRS)], axis=1)
        factor_attn = lax.rsqrt(jnp.mean(o * o, -1, keepdims=True) + epsilon)
        na = o * factor_attn * gain_attn
        hu = hu_ref[rows, :]
        sigma, slope = silu_parts(hu)
        upper = hu * sigma
        gated = (na * upper).astype(bf16)
        y = xf_ref[rows, :] + mm(gated, w2_ref[...])
        factor_out = lax.rsqrt(jnp.mean(y * y, -1, keepdims=True) + epsilon)
        out = (y * factor_out * gain_out).astype(bf16)
        zf = out.astype(f32)
        after = xf_ref[pl.ds(pl.multiple_of(i * TB + TB, 8), 8), :]
        last = lax.broadcasted_iota(jnp.int32, (TB, 1), 0) == TB - 1
        target = jnp.where(last, after[0:1, :], pltpu.roll(xf_ref[rows, :], TB - 1, 0))
        neg_logits = mm(out, neg_ref[...].reshape(half * 2 * z.rn, D), NT_) * scale
        pos = jnp.sum(zf * target, -1, keepdims=True) * scale
        top = jnp.maximum(jnp.max(neg_logits, -1, keepdims=True), pos)
        neg_exp = jnp.exp(neg_logits - top)
        pos_exp = jnp.exp(pos - top)
        total = pos_exp + jnp.sum(neg_exp, -1, keepdims=True)
        live = jnp.where(place + 1 < length, 1.0, 0.0) * lead.astype(f32)
        per = (top + jnp.log(total) - pos) * live
        share = 1.0 / total
        gneg = (neg_exp * (share * live)).astype(bf16)
        gpos = (pos_exp * share - 1.0) * live
        gz = mm(gneg, neg_ref[...].reshape(half * 2 * z.rn, D)) * scale + gpos * target * scale
        gneg_ref[...] += mm(gneg, out, TN) * scale
        target_grad = gpos * zf * scale
        first = lax.broadcasted_iota(jnp.int32, (TB, 1), 0) == 0
        shifted = jnp.where(first, carry_ref[0:1, :], pltpu.roll(target_grad, 1, 0))
        carry_ref[0:1, :] = target_grad[TB - 1 : TB, :]
        scaled = gz * gain_out
        gy = factor_out * (
            scaled - y * factor_out * factor_out * jnp.mean(y * scaled, -1, keepdims=True)
        )
        gres_ref[rows, :] = gy + shifted
        low = gy.astype(bf16)
        gg = mm(low, w2_ref[...], NT_)
        gw2_ref[...] += mm(gated, low, TN)
        gnorm = gg * upper
        gup = gg * na
        og = gain_attn * gnorm
        inner = jnp.sum(o * og, -1, keepdims=True)
        go = factor_attn * (og - o * factor_attn * factor_attn * (inner / D))
        go = go.astype(bf16)
        for p in range(PAIRS):
            do_ref[p, rows, :] = go[:, p * WIDE : (p + 1) * WIDE]
        ghu_ref[rows, :] = (gup * slope).astype(bf16)
        stat_ref[1:2, :] += row_sum(gnorm * o * factor_attn)
        stat_ref[2:3, :] += row_sum(gz * y * factor_out)
        stat_ref[3:4, :] += jnp.broadcast_to(row_sum(per), (1, D))
        stat_ref[4:5, :] += jnp.broadcast_to(row_sum(live), (1, D))


    per_group = z.group_len // TB
    arrive(0)

    def last(i, carry):
        lose(i)
        return carry

    def after_one():
        neg_one()
        for g in range(3, z.groups):
            release(g)

    def after_two():
        neg_three()
        neg_four()
        lax.fori_loop(0, NT - 2, last, 0)

    def step(i, carry):
        if per_group == 1:
            pl.when(i > 0)(lambda: arrive(i))
        pl.when(i == NT - 2)(neg_two)
        inputs(i)
        attend(i)
        if z.groups > 2:
            pl.when(i == 0)(lambda: release(2))
        pl.when(i == 1)(after_one)
        pl.when(i == NT - 2)(after_two)
        return carry

    lax.fori_loop(0, NT, step, 0)
    lax.fori_loop(NT - 2, NT, last, 0)
    for dd in range(z.n_data):
        at = z.order(dd)
        for kk in range(z.n_model):
            piece = gw2_ref[kk * z.fw + dd * z.r2 : kk * z.fw + (dd + 1) * z.r2, :]
            if z.r2p > z.r2:
                piece = jnp.concatenate([piece, jnp.zeros((z.r2p - z.r2, D), f32)], axis=0)
            ga_ref[at, kk * z.r2p : (kk + 1) * z.r2p, :] = piece
        ga_ref[at, z.n_model * z.r2p :, :] = gneg_ref[at * z.rn : (at + 1) * z.rn, :]

    for i in range(half):
        wp_copy(side * half + i).wait_send()
        n5_copy(side * half + i).wait_send()
    for i in range(1, half):
        to = lax.rem(chip + i, half)
        wc_copy(i, here, to).wait_send()
        n2_copy(i, chip, to).wait_send()
        n4_copy(i, here, to).wait_send()
    for i in range(1, n_model):
        at = lax.rem(k + i, n_model)
        wz_copy(i, k, at).wait_send()
        n3_copy(i, k, at).wait_send()
        bz_copy(i, k, at).wait_send()
    n1_copy.wait_send()

    def finish(i, carry):
        at = lax.rem(me + i, n_every)
        ask_copy(at, at, at).wait_send()
        for g in range(max(0, z.groups - 2), z.groups):
            row_copy(g, at, at, at).wait_send()
        return carry

    lax.fori_loop(1, n_every, finish, 0)


def front(z, scalars, table, w_f1, w_f2, bias_tile, owner, local, ids, bucket, gains):
    sds = jax.ShapeDtypeStruct
    dma = pltpu.SemaphoreType.DMA
    vm = pltpu.VMEM
    per_side = z.half * MB * z.rn
    every, model, half, data = (z.n_every,), (z.n_model,), (z.half,), (z.n_data,)
    groups_every = (z.groups, z.n_every)
    pairs_shape = sds((PAIRS, LEN, WIDE), bf16)
    return pl.pallas_call(
        functools.partial(front_kernel, z),
        out_shape=(
            sds((z.n_every, 1, LANES), f32),
            sds((NT, 1, TB), f32),
            sds((z.n_data, z.n_model, z.rw, D), bf16),
            sds((z.n_model, 8, LANES), f32),
            sds((LEN, D), bf16), sds((LEN, D), bf16),
            pairs_shape, pairs_shape, pairs_shape, pairs_shape,
            sds((LEN, D), bf16), sds((LEN, D), f32),
            sds((z.n_data, z.ra, D), f32), sds((8, D), f32),
        ),
        in_specs=[pl.BlockSpec(memory_space=pltpu.SMEM)] + [VM] * 9,
        out_specs=(VM,) * 14,
        scratch_shapes=[
            vm(table.shape, bf16),
            vm((z.n_every, 1, LANES), f32),
            vm((z.groups, z.n_every, CH, D), bf16),
            vm((z.groups, z.n_every, CH, D), bf16),
            vm((2, per_side, D), bf16),
            vm((per_side, D), bf16),
            vm((z.half, MB * z.rn, D), bf16),
            vm((z.n_model, z.rn, D), bf16),
            vm((per_side, D), bf16),
            vm((MB, z.rn, D), bf16),
            vm((z.n_data, z.rn, D), bf16),
            vm((LEN + 8, D), f32),
            vm((LEN, D), f32),
            vm((PAIRS, LEN, WIDE), f32),
            vm((8, D), f32),
            vm((NT, 8, TB), f32),
            vm((4, D, D), bf16),
            vm((D, D), bf16),
            vm((D, D), f32),
            vm((z.n_data * z.rn, D), f32),
            dma(every), dma(every), dma(groups_every), dma(groups_every),
            dma(model), dma(model), dma(half), dma(data), dma(data), dma(data), dma(model), dma(model),
            dma, dma, dma(half), dma(half), dma(model), dma(model), dma(half), dma(data), dma(data), dma(data),
        ],
        compiler_params=pltpu.CompilerParams(
            collective_id=0, has_side_effects=True, vmem_limit_bytes=LIMIT
        ),
        cost_estimate=pl.CostEstimate(
            flops=60_000_000_000, bytes_accessed=30_000_000, transcendentals=6_000_000
        ),
        name="front",
    )(scalars, table, w_f1, w_f2, bias_tile, owner, local, ids, bucket, gains)


def rear_kernel(
    z, len_ref, x_ref, n1_ref, q_ref, k_ref, v_ref, do_ref, ghu_ref, gres_ref, w_ref, bias_ref, bucket_ref,
    gains_ref, slot_ref, stat_in_ref, ga_ref, asked_ref, ids_ref,
    tg_ref, wg_ref, packs_ref, squares_ref,
    gh_ref, hid_ref, kb_ref, dq_ref, dk_ref, dv_ref, kt_ref, bs_ref, w1_ref, stat_ref, pack_ref, out_ref, gb_ref,
    got_ref, pa_ref, pb_ref, sa_ref, sb_ref, ca_ref, cb_ref, zs_ref, zr_ref, ng_ref, sq_ref,
    row_send, row_recv, pack_send, pack_recv,
    pa_send, pa_recv, pb_send, pb_recv, ca_send, ca_recv, cb_send, cb_recv,
    zw_send, zw_recv, zf_send, zf_recv, zn_send, zn_recv, gw_send, gw_recv, gn_send, gn_recv,
    hw_send, hw_recv, hn_send, hn_recv, sq_send, sq_recv,
):
    n_every, n_model, half = z.n_every, z.n_model, z.half
    slots = z.slots
    d = lax.axis_index("dp")
    k = lax.axis_index("mp")
    me = d * n_model + k
    side = lax.rem(d, 2)
    chip = d // 2
    here = side * half + chip
    other = d + 1 - 2 * side
    micro = k // z.copies
    barrier = pltpu.get_barrier_semaphore()

    def signal(i, carry):
        to = spot(lax.rem(me + i, n_every), n_model)
        pl.semaphore_signal(barrier, inc=1, device_id=to, device_id_type=MESH)
        return carry

    lax.fori_loop(1, n_every, signal, 0)

    pa_copy = remote(ga_ref.at[1 - side], pa_ref, pa_send, pa_recv, (other, k))

    def pb_copy(p):
        return remote(gb_ref.at[1 - side, p], pb_ref.at[p], pb_send.at[p], pb_recv.at[p], (other, k))

    def row_copy(g, src, dst, to):
        return remote(
            out_ref.at[g, to], got_ref.at[g, dst], row_send.at[g, to], row_recv.at[g, src],
            spot(to, n_model),
        )

    def pack_copy(src, dst, to):
        return remote(
            pack_ref, packs_ref.at[dst], pack_send.at[to], pack_recv.at[src], spot(to, n_model)
        )

    def ca_copy(i, at, to):
        return remote(
            sa_ref.at[to], ca_ref.at[at], ca_send.at[i], ca_recv.at[at], (2 * to + side, k)
        )

    def cb_copy(p, i, at, to):
        return remote(
            sb_ref.at[p, to], cb_ref.at[p, at], cb_send.at[p, i], cb_recv.at[p, at], (2 * to + side, k)
        )

    def zn_copy(i, at, to):
        return remote(
            ng_ref.at[here, at], ng_ref.at[here, at], zn_send.at[i], zn_recv.at[at], (d, to)
        )

    def zw_copy(at, to):
        part = pl.ds(0, z.r1)
        return remote(
            zs_ref.at[to, part], zr_ref.at[at, part], zw_send.at[to], zw_recv.at[at], (d, to)
        )

    def zf_copy(at, to):
        part = pl.ds(z.r1, z.r2p)
        return remote(
            zs_ref.at[to, part], zr_ref.at[at, part], zf_send.at[to], zf_recv.at[at], (d, to)
        )

    def gw_copy(i, at, to):
        return remote(
            wg_ref.at[at], wg_ref.at[at], gw_send.at[i], gw_recv.at[at], (2 * to + side, k)
        )

    def gn_copy(i, at, to):
        return remote(
            ng_ref.at[at], ng_ref.at[at], gn_send.at[i], gn_recv.at[at], (2 * to + side, k)
        )

    def hw_copy(at):
        return remote(wg_ref.at[at], wg_ref.at[at], hw_send.at[at], hw_recv.at[at], (other, k))

    def hn_copy(at):
        return remote(ng_ref.at[at], ng_ref.at[at], hn_send.at[at], hn_recv.at[at], (other, k))

    def sq_copy(src, dst, to):
        return remote(
            sq_ref, squares_ref.at[dst], sq_send.at[to], sq_recv.at[src], spot(to, n_model)
        )

    def chips_a():
        pa_copy.wait_recv()
        sa_ref[...] = (ga_ref[side] + pa_ref[...]).astype(bf16)
        for i in range(1, half):
            ca_copy(i, chip, lax.rem(chip + i, half)).start()

    def chips_b(p):
        pb_copy(p).wait_recv()
        sb_ref[p] = (gb_ref[side, p] + pb_ref[p]).astype(bf16)
        for i in range(1, half):
            cb_copy(p, i, chip, lax.rem(chip + i, half)).start()

    def planes_a():
        total = sa_ref[chip].astype(f32)
        for i in range(1, half):
            at = lax.rem(chip + i, half)
            ca_copy(i, at, chip).wait_recv()
            total = total + ca_ref[at].astype(f32)
        ng_ref[here, k] = total[n_model * z.r2p :].astype(bf16)
        zs_ref[:, z.r1 :, :] = total[: n_model * z.r2p].reshape(n_model, z.r2p, D)
        for i in range(1, n_model):
            to = lax.rem(k + i, n_model)
            zn_copy(i, k, to).start()
            zf_copy(k, to).start()

    def planes_b(p):
        total = sb_ref[p, chip].astype(f32)
        for i in range(1, half):
            at = lax.rem(chip + i, half)
            cb_copy(p, i, at, chip).wait_recv()
            total = total + cb_ref[p, at].astype(f32)
        for i in range(z.npp):
            to = p * z.npp + i
            zs_ref[to, : z.r1, :] = total[i * z.r1 : (i + 1) * z.r1]
            pl.when(k != to)(lambda to=to: zw_copy(k, to).start())

    def spread_a():
        for i in range(1, n_model):
            zn_copy(i, lax.rem(k + i, n_model), k).wait_recv()
        for i in range(1, half):
            gn_copy(i, here, lax.rem(chip + i, half)).start()
        hn_copy(here).start()

    def swap_a():
        for i in range(1, half):
            at = side * half + lax.rem(chip + i, half)
            gn_copy(i, at, chip).wait_recv()
            hn_copy(at).start()

    gain_in = gains_ref[0:1, :]
    place_weights(z, w_ref, w1_ref, None)
    kb_ref[...] = key_bias(bias_ref, bucket_ref[micro], len_ref[micro, 0]).T

    def inputs(i, carry):
        rows = pl.ds(pl.multiple_of(i * TB, TB), TB)
        for c in (1, 2, 3):
            hid_ref[c - 1, rows, :] = mm(n1_ref[rows, :], w1_ref[c], NT_)
        return carry

    lax.fori_loop(0, NT, inputs, 0)
    bs_ref[...] = jnp.zeros_like(bs_ref)
    in_row = lax.broadcasted_iota(jnp.int32, (2 * TB, TB), 0)
    in_col = lax.broadcasted_iota(jnp.int32, (2 * TB, TB), 1)
    causal = lax.rem(in_row, TB) <= in_col
    ones_lane = lax.broadcasted_iota(jnp.int32, (2 * TB, LANES), 1)
    ones_half = lax.broadcasted_iota(jnp.int32, (2 * TB, LANES), 0) >= TB
    stat_ref[...] = jnp.zeros_like(stat_ref)
    per_group = z.group_len // TB

    def outputs(i):
        rows = pl.ds(pl.multiple_of(i * TB, TB), TB)
        gn = mm(ghu_ref[rows, :], w1_ref[0])
        for c in (1, 2, 3):
            gn += mm(gh_ref[c - 1, rows, :], w1_ref[c])
        x = x_ref[rows, :].astype(f32)
        factor = lax.rsqrt(jnp.mean(x * x, -1, keepdims=True) + epsilon)
        scaled = gn * gain_in
        gx = factor * (scaled - x * factor * factor * jnp.mean(x * scaled, -1, keepdims=True))
        gx = (gx + gres_ref[rows, :]).astype(bf16)
        stat_ref[0:1, :] += row_sum(gn * x * factor)
        group = i // per_group
        hot = lax.broadcasted_iota(jnp.int32, (slots, TB), 0).astype(f32) == slot_ref[i]
        mine = mm(jnp.where(hot, 1.0, 0.0).astype(bf16), gx).astype(bf16)
        mine = mine.reshape(z.n_every, CH, D)
        if per_group == 1:
            out_ref[group] = mine
        else:
            out_ref[group] = jnp.where(lax.rem(i, per_group) == 0, mine, out_ref[group] + mine)

    def send_group(g):
        def send(i, carry):
            row_copy(g, me, me, lax.rem(me + i, n_every)).start()
            return carry

        lax.fori_loop(1, n_every, send, 0)
        got_ref[g, me] = out_ref[g, me]

    def weights_grad(p):
        lanes = slice(p * WIDE, (p + 1) * WIDE)
        for c in range(4):
            left = ghu_ref[:, lanes] if c == 0 else gh_ref[c - 1, :, lanes]
            grads = mm(left, n1_ref[...], TN)
            for side_head in range(2):
                head = 2 * p + side_head
                for dd in range(z.n_data):
                    own_head, part, first = z.block(dd)
                    if part == c and own_head == head % z.heads_dev:
                        at = head // z.heads_dev - p * z.npp
                        gb_ref[dd % 2, p, dd // 2, at * z.r1 : (at + 1) * z.r1, :] = grads[
                            side_head * DH + first : side_head * DH + first + z.r1
                        ]
        pb_copy(p).start()

    early = range(PAIRS - SPAN)
    late = range(PAIRS - SPAN, PAIRS)

    def first_hook():
        for p in early:
            chips_b(p)
        spread_a()

    def second_hook():
        for p in early:
            planes_b(p)

    def late_weights():
        for p in late:
            weights_grad(p)

    pl.semaphore_wait(barrier, n_every - 1)
    pa_copy.start()

    def keys_of(p, j):
        keys = pl.ds(pl.multiple_of(j * TB, TB), TB)
        at = p % SPAN
        kt = k_ref[p, keys, :].astype(f32).T
        low = lax.broadcasted_iota(jnp.int32, kt.shape, 0) < DH
        kt_ref[at] = jnp.concatenate(
            [jnp.where(low, kt, 0.0), jnp.where(low, 0.0, kt)], axis=1
        ).astype(bf16)
        dk_ref[at] = jnp.zeros((TB, WIDE + LANES), f32)
        dv_ref[at] = jnp.zeros((TB, WIDE), f32)

    def part(p, i, j, masked):
        keys = pl.ds(pl.multiple_of(j * TB, TB), TB)
        rows = pl.ds(pl.multiple_of(i * TB, TB), TB)
        at = p % SPAN
        q = q_ref[p, rows, :]
        do = do_ref[p, rows, :]
        kb = jnp.concatenate(
            [kb_ref[keys, 2 * p : 2 * p + 1], kb_ref[keys, 2 * p + 1 : 2 * p + 2]], axis=0
        )
        mark = jnp.where(
            ones_lane == jnp.where(ones_half, 2 * p + 1, 2 * p), 1.0, 0.0
        ).astype(bf16)
        place = lax.broadcasted_iota(jnp.int32, (1, TB), 1) + i * TB
        inv = 1.0 / (place.astype(f32) + 1.0)
        h = mm(halves(k_ref[p, keys, :]), q, NT_) + kb
        t = jnp.tanh(h)
        m = h * t
        w = (h + m) * inv
        ds = mm(halves(v_ref[p, keys, :]), do, NT_) * ((1.0 + t) * (0.5 * inv)) * (1.0 + h - m)
        if masked:
            w = jnp.where(causal, w, 0.0)
            ds = jnp.where(causal, ds, 0.0)
        ds = ds.astype(bf16)
        dv_ref[at] += mm(beside(w.astype(bf16)), halves(do))
        dk_ref[at] += mm(beside(ds), jnp.concatenate([halves(q), mark], axis=1))
        dq_ref[at, i] += mm(kt_ref[at], ds)

    def keys_end(p, j):
        keys = pl.ds(pl.multiple_of(j * TB, TB), TB)
        lanes = slice(p * WIDE, (p + 1) * WIDE)
        at = p % SPAN
        slope_v = silu_parts(hid_ref[0, keys, lanes])[1]
        slope_k = silu_parts(hid_ref[2, keys, lanes])[1]
        slope_q = silu_parts(hid_ref[1, keys, lanes])[1]
        gh_ref[0, keys, lanes] = (dv_ref[at] * slope_v).astype(bf16)
        gh_ref[2, keys, lanes] = (dk_ref[at, :, :WIDE] * 2.0 * slope_k).astype(bf16)
        gh_ref[1, keys, lanes] = (dq_ref[at, j].T * DH ** (-0.5) * slope_q).astype(bf16)
        bs_ref[keys, :] += dk_ref[at, :, WIDE:]

    for phase in range(PAIRS // SPAN):
        pairs = range(phase * SPAN, (phase + 1) * SPAN)
        final = phase == PAIRS // SPAN - 1
        dq_ref[...] = jnp.zeros_like(dq_ref)

        def keys_step(j, carry, pairs=pairs, final=final, phase=phase):
            for p in pairs:
                keys_of(p, j)
            for p in pairs:
                part(p, j, j, True)

            def later(i, inner):
                for p in pairs:
                    part(p, i, j, False)
                return inner

            lax.fori_loop(j + 1, NT, later, 0)
            for p in pairs:
                keys_end(p, j)
            if phase == 0:
                pl.when(j == 0)(chips_a)
                pl.when(j == 2)(planes_a)
            if final:
                pl.when(j == NT - 1)(late_weights)
                pl.when(j == 0)(first_hook)
                outputs(j)
                if per_group == 1:
                    send_group(j)
                pl.when(j == 1)(second_hook)
                pl.when(j == 2)(swap_a)
            return carry

        lax.fori_loop(0, NT, keys_step, 0)
        if not final:
            for p in pairs:
                weights_grad(p)

    if per_group > 1:
        for g in range(z.groups):
            send_group(g)
    hot = jnp.where(
        lax.broadcasted_iota(jnp.int32, (NB, LEN), 0) == bucket_ref[micro], 1.0, 0.0
    )
    bias_grad = lax.dot_general(hot, bs_ref[...], NN, precision=highest, preferred_element_type=f32)
    for i in range(D // LANES):
        lanes = slice(i * LANES, (i + 1) * LANES)
        pack_ref[i : i + 1] = stat_ref[0:1, lanes]
        pack_ref[4 + i : 5 + i] = stat_in_ref[1:2, lanes]
        pack_ref[8 + i : 9 + i] = stat_in_ref[2:3, lanes]
    pack_ref[12:14] = stat_in_ref[3:5, :LANES]
    pack_ref[14:16] = jnp.zeros((2, LANES), f32)
    pack_ref[16:24] = bias_grad.T[0:8, :]
    packs_ref[me] = pack_ref[...]

    def pack_all(i, carry):
        pack_copy(me, me, lax.rem(me + i, n_every)).start()
        return carry

    lax.fori_loop(1, n_every, pack_all, 0)

    tg_ref[...] = jnp.zeros_like(tg_ref)
    wide = min(TB, slots)
    ask_at = lax.broadcasted_iota(jnp.int32, (z.rows_dev, wide), 0).astype(f32)

    def collect(g):
        def wait(i, carry):
            at = lax.rem(me + i, n_every)
            row_copy(g, at, at, at).wait_recv()
            return carry

        lax.fori_loop(1, n_every, wait, 0)
        for b in range(slots // wide):
            asked = asked_ref[g][:, b * wide : (b + 1) * wide]
            hot = jnp.where(ask_at == asked, 1.0, 0.0).astype(bf16)
            rows = got_ref[g, b * (wide // CH) : (b + 1) * (wide // CH)].reshape(wide, D)
            tg_ref[...] += mm(hot, rows)

    neg_rows = n_model * z.rn
    row_at = lax.broadcasted_iota(jnp.int32, (z.rows_dev, neg_rows), 0).astype(f32)
    base = (me * z.rows_dev).astype(f32)

    def negatives(at):
        hot = jnp.where(row_at == ids_ref[at] - base, 1.0, 0.0).astype(bf16)
        tg_ref[...] += mm(hot, ng_ref[at].reshape(neg_rows, D))

    for p in late:
        chips_b(p)
    collect(0)
    for p in late:
        planes_b(p)
    for i in range(half):
        negatives(side * half + i)
    for i in range(half):
        hn_copy((1 - side) * half + i).wait_recv()
        negatives((1 - side) * half + i)
    for g in range(1, max(1, z.groups - 1)):
        collect(g)
    total = zs_ref[k]
    for i in range(1, n_model):
        at = lax.rem(k + i, n_model)
        zw_copy(at, k).wait_recv()
        zf_copy(at, k).wait_recv()
        total = total + zr_ref[at]
    wg_ref[here] = total
    for i in range(1, half):
        gw_copy(i, here, lax.rem(chip + i, half)).start()
    hw_copy(here).start()
    if z.groups > 1:
        collect(z.groups - 1)

    table_grad = tg_ref[...]
    slice_grad = wg_ref[here]
    squares = row_sum(table_grad * table_grad) + row_sum(slice_grad * slice_grad)
    sq_ref[...] = sum(squares[:, i * LANES : (i + 1) * LANES] for i in range(D // LANES))
    squares_ref[me] = sq_ref[...]

    def share(i, carry):
        to = lax.rem(me + i, n_every)
        sq_copy(me, me, to).start()
        return carry

    lax.fori_loop(1, n_every, share, 0)
    for i in range(1, half):
        at = side * half + lax.rem(chip + i, half)
        gw_copy(i, at, chip).wait_recv()
        hw_copy(at).start()
    for i in range(half):
        hw_copy((1 - side) * half + i).wait_recv()
        hw_copy(side * half + i).wait_send()
        hn_copy(side * half + i).wait_send()
    for i in range(1, half):
        to = lax.rem(chip + i, half)
        ca_copy(i, chip, to).wait_send()
        for p in range(PAIRS):
            cb_copy(p, i, chip, to).wait_send()
        gn_copy(i, here, to).wait_send()
        gw_copy(i, here, to).wait_send()
    for i in range(1, n_model):
        to = lax.rem(k + i, n_model)
        zn_copy(i, k, to).wait_send()
        zw_copy(k, to).wait_send()
        zf_copy(k, to).wait_send()
    pa_copy.wait_send()
    for p in range(PAIRS):
        pb_copy(p).wait_send()

    def finish(i, carry):
        at = lax.rem(me + i, n_every)
        for g in range(z.groups):
            row_copy(g, at, at, at).wait_send()
        pack_copy(at, at, at).wait_send()
        pack_copy(at, at, at).wait_recv()
        sq_copy(at, at, at).wait_send()
        sq_copy(at, at, at).wait_recv()
        return carry

    lax.fori_loop(1, n_every, finish, 0)


def rear(
    z, scalars, x, n1, q, k, v, do, ghu, gres, w, bias, bucket, gains, slot, stat, ga, asked, ids
):
    sds = jax.ShapeDtypeStruct
    dma = pltpu.SemaphoreType.DMA
    vm = pltpu.VMEM
    every, model, half, data = (z.n_every,), (z.n_model,), (z.half,), (z.n_data,)
    groups_every = (z.groups, z.n_every)
    pairs, pairs_half = (PAIRS,), (PAIRS, z.half)
    rows_b = z.npp * z.r1
    return pl.pallas_call(
        functools.partial(rear_kernel, z),
        out_shape=(
            sds((z.rows_dev, D), f32),
            sds((z.n_data, z.rw, D), f32),
            sds((z.n_every, 24, LANES), f32),
            sds((z.n_every, 1, LANES), f32),
        ),
        in_specs=[pl.BlockSpec(memory_space=pltpu.SMEM)] + [VM] * 17,
        out_specs=(VM,) * 4,
        scratch_shapes=[
            vm((3, LEN, D), bf16),
            vm((3, LEN, D), f32),
            vm((LEN, 8), f32),
            vm((SPAN, NT, WIDE, TB), f32),
            vm((SPAN, TB, WIDE + LANES), f32),
            vm((SPAN, TB, WIDE), f32),
            vm((SPAN, WIDE, 2 * TB), bf16),
            vm((LEN, LANES), f32),
            vm((4, D, D), bf16),
            vm((8, D), f32),
            vm((24, LANES), f32),
            vm((z.groups, z.n_every, CH, D), bf16),
            vm((2, PAIRS, z.half, rows_b, D), f32),
            vm((z.groups, z.n_every, CH, D), bf16),
            vm((z.half, z.ra, D), f32),
            vm((PAIRS, z.half, rows_b, D), f32),
            vm((z.half, z.ra, D), bf16),
            vm((PAIRS, z.half, rows_b, D), bf16),
            vm((z.half, z.ra, D), bf16),
            vm((PAIRS, z.half, rows_b, D), bf16),
            vm((z.n_model, z.rw, D), f32),
            vm((z.n_model, z.rw, D), f32),
            vm((z.n_data, z.n_model, z.rn, D), bf16),
            vm((1, LANES), f32),
            dma(groups_every), dma(groups_every), dma(every), dma(every),
            dma, dma, dma(pairs), dma(pairs), dma(half), dma(half), dma(pairs_half), dma(pairs_half),
            dma(model), dma(model), dma(model), dma(model), dma(model), dma(model),
            dma(half), dma(data), dma(half), dma(data),
            dma(data), dma(data), dma(data), dma(data), dma(every), dma(every),
        ],
        compiler_params=pltpu.CompilerParams(
            collective_id=1, has_side_effects=True, vmem_limit_bytes=LIMIT
        ),
        cost_estimate=pl.CostEstimate(
            flops=60_000_000_000, bytes_accessed=30_000_000, transcendentals=6_000_000
        ),
        name="rear",
    )(scalars, x, n1, q, k, v, do, ghu, gres, w, bias, bucket, gains, slot, stat, ga, asked, ids)


def adam_step(weight, grad, first, second, rate, decay):
    first_new = beta_one * first + (1.0 - beta_one) * grad
    second_new = beta_two * second + (1.0 - beta_two) * grad * grad
    fix_one = 1.0 / (1.0 - beta_one**STEP)
    fix_two = 1.0 / (1.0 - beta_two**STEP)
    move = first_new * fix_one / (jnp.sqrt(second_new * fix_two) + adam_floor) + decay * weight
    return (weight - rate * move, first_new, second_new)


def settle_kernel(
    z, squares_ref, packs_ref, wg_ref, tg_ref, t_ref, tm_ref, tv_ref, a_ref, am_ref, av_ref,
    b_ref, bm_ref, bv_ref, c_ref, cm_ref, cv_ref, e_ref, em_ref, ev_ref,
    t_out, tm_out, tv_out, tl_out, a_out, am_out, av_out, al_out, b_out, bm_out, bv_out, bl_out,
    c_out, cm_out, cv_out, e_out, em_out, ev_out, flat_out, factor_ref, one_ref,
):
    def update(grad, refs, outs, rate, decay):
        new, first, second = adam_step(refs[0][...], grad, refs[1][...], refs[2][...], rate, decay)
        outs[0][...] = new
        outs[1][...] = first
        outs[2][...] = second
        if len(outs) > 3:
            outs[3][...] = new.astype(bf16)

    @pl.when(pl.program_id(0) == 0)
    def _():
        packs = jnp.sum(packs_ref[...], axis=0)
        gain_grad = jnp.concatenate(
            [
                jnp.concatenate([packs[4 * r + i : 4 * r + i + 1] for i in range(D // LANES)], axis=1)
                for r in range(3)
            ],
            axis=0,
        )
        bias_all = packs[16:24]
        squares = jnp.sum(squares_ref[...], axis=0) + row_sum(packs[0:12] * packs[0:12])
        squares = squares + row_sum(bias_all * bias_all)
        norm = jnp.sqrt(jnp.sum(squares, axis=1, keepdims=True))
        factor = jnp.minimum(1.0, clip_at / norm)
        factor_ref[...] = jnp.broadcast_to(factor, factor_ref.shape)
        flat_out[0:2] = packs[12:14]
        flat_out[2:3] = jnp.broadcast_to(norm, (1, LANES))
        flat_out[3:8] = jnp.zeros((5, LANES), f32)
        one = jnp.concatenate([wg_ref[z.order(d), 0 : z.r1] for d in range(z.n_data)], axis=0)
        two = jnp.concatenate(
            [wg_ref[z.order(d), z.r1 : z.r1 + z.r2] for d in range(z.n_data)], axis=0
        )
        one_ref[...] = one.T * factor
        update(two * factor, (b_ref, bm_ref, bv_ref), (b_out, bm_out, bv_out, bl_out), 0.04, 0.1)
        update(gain_grad * factor, (c_ref, cm_ref, cv_ref), (c_out, cm_out, cv_out), 0.5, 0.0)
        head = lax.broadcasted_iota(jnp.int32, bias_all.shape, 0)
        first_head = lax.axis_index("mp") * z.heads_dev
        mine = [
            row_sum(jnp.where(head == first_head + r, bias_all, 0.0)) for r in range(z.heads_dev)
        ]
        bias_grad = jnp.concatenate(mine, axis=0)
        update(bias_grad * factor, (e_ref, em_ref, ev_ref), (e_out, em_out, ev_out), 1.0, 0.0)

    size = a_ref.shape[0]
    rows = pl.ds(pl.multiple_of(pl.program_id(0) * size, size), size)
    update(one_ref[rows, :], (a_ref, am_ref, av_ref), (a_out, am_out, av_out, al_out), 0.04, 0.1)
    update(
        tg_ref[...] * factor_ref[0:1, 0:1], (t_ref, tm_ref, tv_ref), (t_out, tm_out, tv_out, tl_out), 0.5, 0.1
    )


def settle(z, squares, packs, wg, tg, table, f1, f2, gains, bias):
    sds = jax.ShapeDtypeStruct
    rows = next(r for r in range(112, 0, -16) if z.rows_dev % r == 0)
    blocks = z.rows_dev // rows
    steps = next(n for n in range(blocks, 512) if D % n == 0 and D // n % 16 == 0)
    block = pl.BlockSpec((rows, D), lambda i: (jnp.minimum(i, blocks - 1), 0))
    part = pl.BlockSpec((D // steps, 4 * z.fw), lambda i: (i, 0))

    def like(array, dtype=f32):
        return sds(array.shape, dtype)

    return pl.pallas_call(
        functools.partial(settle_kernel, z),
        grid=(steps,),
        out_shape=(
            like(tg), like(tg), like(tg), like(tg, bf16),
            like(f1[0]), like(f1[0]), like(f1[0]), like(f1[0], bf16),
            like(f2[0]), like(f2[0]), like(f2[0]), like(f2[0], bf16),
            like(gains[0]), like(gains[0]), like(gains[0]),
            like(bias[0]), like(bias[0]), like(bias[0]), sds((8, LANES), f32),
        ),
        in_specs=[VM] * 3 + [block] * 4 + [part] * 3 + [VM] * 9,
        out_specs=(block,) * 4 + (part,) * 4 + (VM,) * 11,
        scratch_shapes=[pltpu.VMEM((8, LANES), f32), pltpu.VMEM((D, 4 * z.fw), f32)],
        compiler_params=pltpu.CompilerParams(vmem_limit_bytes=LIMIT),
        cost_estimate=pl.CostEstimate(
            flops=20 * z.rows_dev * D, bytes_accessed=20_000_000, transcendentals=1_000_000
        ),
        name="settle",
    )(squares, packs, wg, tg, *table, *f1, *f2, *gains, *bias)


def settle_kernel(
    z, squares_ref, packs_ref, wg_ref, tg_ref, t_ref, tm_ref, tv_ref, a_ref, am_ref, av_ref,
    b_ref, bm_ref, bv_ref, c_ref, cm_ref, cv_ref, e_ref, em_ref, ev_ref,
    t_out, tm_out, tv_out, tl_out, a_out, am_out, av_out, al_out, b_out, bm_out, bv_out, bl_out,
    c_out, cm_out, cv_out, e_out, em_out, ev_out, flat_out, factor_ref, one_ref,
):
    def update(grad, refs, outs, rate, decay):
        new, first, second = adam_step(refs[0][...], grad, refs[1][...], refs[2][...], rate, decay)
        outs[0][...] = new
        outs[1][...] = first
        outs[2][...] = second
        if len(outs) > 3:
            outs[3][...] = new.astype(bf16)

    @pl.when(pl.program_id(0) == 0)
    def _():
        packs = jnp.sum(packs_ref[...], axis=0)
        gain_grad = jnp.concatenate(
            [
                jnp.concatenate([packs[4 * r + i : 4 * r + i + 1] for i in range(D // LANES)], axis=1)
                for r in range(3)
            ],
            axis=0,
        )
        bias_all = packs[16:24]
        squares = jnp.sum(squares_ref[...], axis=0) + row_sum(packs[0:12] * packs[0:12])
        squares = squares + row_sum(bias_all * bias_all)
        norm = jnp.sqrt(jnp.sum(squares, axis=1, keepdims=True))
        factor = jnp.minimum(1.0, clip_at / norm)
        factor_ref[...] = jnp.broadcast_to(factor, factor_ref.shape)
        flat_out[0:2] = packs[12:14]
        flat_out[2:3] = jnp.broadcast_to(norm, (1, LANES))
        flat_out[3:8] = jnp.zeros((5, LANES), f32)
        one = jnp.concatenate([wg_ref[z.order(d), 0 : z.r1] for d in range(z.n_data)], axis=0)
        two = jnp.concatenate(
            [wg_ref[z.order(d), z.r1 : z.r1 + z.r2] for d in range(z.n_data)], axis=0
        )
        one_ref[...] = one.T * factor
        update(two * factor, (b_ref, bm_ref, bv_ref), (b_out, bm_out, bv_out, bl_out), 0.04, 0.1)
        update(gain_grad * factor, (c_ref, cm_ref, cv_ref), (c_out, cm_out, cv_out), 0.5, 0.0)
        head = lax.broadcasted_iota(jnp.int32, bias_all.shape, 0)
        first_head = lax.axis_index("mp") * z.heads_dev
        mine = [
            row_sum(jnp.where(head == first_head + r, bias_all, 0.0)) for r in range(z.heads_dev)
        ]
        bias_grad = jnp.concatenate(mine, axis=0)
        update(bias_grad * factor, (e_ref, em_ref, ev_ref), (e_out, em_out, ev_out), 1.0, 0.0)

    size = a_ref.shape[0]
    rows = pl.ds(pl.multiple_of(pl.program_id(0) * size, size), size)
    update(one_ref[rows, :], (a_ref, am_ref, av_ref), (a_out, am_out, av_out, al_out), 0.04, 0.1)
    update(
        tg_ref[...] * factor_ref[0:1, 0:1], (t_ref, tm_ref, tv_ref), (t_out, tm_out, tv_out, tl_out), 0.5, 0.1
    )


def settle(z, squares, packs, wg, tg, table, f1, f2, gains, bias):
    sds = jax.ShapeDtypeStruct
    rows = next(r for r in range(112, 0, -16) if z.rows_dev % r == 0)
    blocks = z.rows_dev // rows
    steps = next(n for n in range(blocks, 512) if D % n == 0 and D // n % 16 == 0)
    block = pl.BlockSpec((rows, D), lambda i: (jnp.minimum(i, blocks - 1), 0))
    part = pl.BlockSpec((D // steps, 4 * z.fw), lambda i: (i, 0))

    def like(array, dtype=f32):
        return sds(array.shape, dtype)

    return pl.pallas_call(
        functools.partial(settle_kernel, z),
        grid=(steps,),
        out_shape=(
            like(tg), like(tg), like(tg), like(tg, bf16),
            like(f1[0]), like(f1[0]), like(f1[0]), like(f1[0], bf16),
            like(f2[0]), like(f2[0]), like(f2[0]), like(f2[0], bf16),
            like(gains[0]), like(gains[0]), like(gains[0]),
            like(bias[0]), like(bias[0]), like(bias[0]), sds((8, LANES), f32),
        ),
        in_specs=[VM] * 3 + [block] * 4 + [part] * 3 + [VM] * 9,
        out_specs=(block,) * 4 + (part,) * 4 + (VM,) * 11,
        scratch_shapes=[pltpu.VMEM((8, LANES), f32), pltpu.VMEM((D, 4 * z.fw), f32)],
        compiler_params=pltpu.CompilerParams(vmem_limit_bytes=LIMIT),
        cost_estimate=pl.CostEstimate(
            flops=20 * z.rows_dev * D, bytes_accessed=20_000_000, transcendentals=1_000_000
        ),
        name="settle",
    )(squares, packs, wg, tg, *table, *f1, *f2, *gains, *bias)


def pick(array, index):
    return lax.dynamic_index_in_dim(array, index, 0, keepdims=False)


def per_device(
    lengths, owners, item_rows, buckets, negatives, table, table_m, table_v, w_f1, f1_m, f1_v,
    w_f2, f2_m, f2_v, gains, gains_m, gains_v, bias, bias_m, bias_v,
):
    n_model = lax.axis_size("mp")
    n_data = lax.axis_size("dp")
    z = Sizes(n_data, n_model, bias.shape[0], table.shape[0], negatives.shape[1])
    ids = negatives.astype(f32).reshape(MB, n_data, z.rn).transpose(1, 0, 2)
    ids_rows = ids.reshape(-1, 1, LANES)
    ids_cols = jnp.repeat(ids, z.copies, axis=1).reshape(n_data, 1, n_model * z.rn)

    asked, slot, w, bias_all, x, n1, q, k, v, do, ghu, gres, ga, stat_a = front(
        z, lengths, table, w_f1, w_f2, bias, owners.reshape(MB, 1, LEN), item_rows, ids_rows,
        buckets, gains,
    )
    asked = asked.reshape(z.n_every, LANES)[:, : z.groups * CH].reshape(z.n_every, z.groups, CH)
    asked = asked.transpose(1, 0, 2).reshape(z.groups, 1, z.slots)
    table_grad, wg, packs, squares = rear(
        z, lengths, x, n1, q, k, v, do, ghu, gres, w, bias_all, buckets, gains, slot, stat_a,
        ga.reshape(2, z.half, z.ra, D), asked, ids_cols,
    )
    *new, flat = settle(
        z, squares, packs, wg, table_grad, (table, table_m, table_v), (w_f1, f1_m, f1_v),
        (w_f2, f2_m, f2_v), (gains, gains_m, gains_v), (bias, bias_m, bias_v),
    )
    return (flat[0, 0], flat[1, 0], flat[2, 0], *new)


def solution(mesh):
    rows, cols = P(("dp", "mp"), None), P(None, "mp")
    heads = P("mp", None)
    in_specs = (
        P(None, "dp"), P(None, "dp", None, None), P(None, "dp", None), P(None, "dp", None), P(),
        rows, rows, rows, cols, cols, cols, heads, heads, heads, P(), P(), P(), heads, heads, heads,
    )
    out_specs = (
        P(), P(), P(), rows, rows, rows, rows, cols, cols, cols, cols,
        heads, heads, heads, heads, P(), P(), P(), heads, heads, heads,
    )
    return jax.shard_map(
        per_device, mesh=mesh, in_specs=in_specs, out_specs=out_specs, check_vma=False
    )
```

```python
import functools

import jax
import jax.numpy as jnp
from jax import lax
from jax.experimental import pallas as pl
from jax.experimental.pallas import tpu as pltpu
from jax.sharding import PartitionSpec as P

DH = 64
D = 512
NB = 128
LEN = 1024
MB = 4
STEP = 10

TB = 256
NT = LEN // TB
HEADS = D // DH
PAIRS = HEADS // 2
WIDE = 2 * DH
CH = 16
LANES = 128
SPAN = 2

epsilon = 1e-06
clip_at = 1.0
beta_one = 0.9
beta_two = 0.95
adam_floor = 1e-08
highest = lax.Precision.HIGHEST
f32 = jnp.float32
bf16 = jnp.bfloat16
MESH = pl.DeviceIdType.MESH
VM = pl.BlockSpec(memory_space=pltpu.VMEM)
LIMIT = 61 * 1024 * 1024

NN = (((1,), (0,)), ((), ()))
NT_ = (((1,), (1,)), ((), ()))
TN = (((0,), (0,)), ((), ()))


def mm(a, b, dims=NN):
    return lax.dot_general(a, b, dims, preferred_element_type=f32)


def spot(index, n_model):
    return (index // n_model, lax.rem(index, n_model))


def cross(rows):
    lane = lax.broadcasted_iota(jnp.int32, (LANES, LANES), 1)
    eye = lax.broadcasted_iota(jnp.int32, (LANES, LANES), 0) == lane
    spread = jnp.broadcast_to(rows, (LANES, LANES))
    return jnp.sum(jnp.where(eye, spread, 0.0), axis=1, keepdims=True)


def remote(src, dst, send_sem, recv_sem, to):
    return pltpu.make_async_remote_copy(
        src_ref=src,
        dst_ref=dst,
        send_sem=send_sem,
        recv_sem=recv_sem,
        device_id=to,
        device_id_type=MESH,
    )


class Sizes:
    def __init__(self, n_data, n_model, heads_dev, rows_dev, negs):
        self.n_data, self.n_model, self.heads_dev, self.rows_dev = n_data, n_model, heads_dev, rows_dev
        self.n_every = n_data * n_model
        self.copies = n_model // MB
        look = LEN // n_model
        cap = max(2, 2 * look // self.n_every)
        self.group_len = look * max(1, CH // cap)
        self.groups = LEN // self.group_len
        self.slots = self.n_every * CH
        self.fw = heads_dev * DH
        self.half = n_data // 2
        self.r1 = 4 * self.fw // n_data
        self.r2 = self.fw // n_data
        self.r2p = -(-self.r2 // 16) * 16
        self.rw = self.r1 + self.r2p
        self.rn = negs // n_data
        self.ra = n_model * self.r2p + self.rn
        self.npp = n_model // PAIRS

    def order(self, d):
        return (d % 2) * self.half + d // 2

    def block(self, d):
        flat = d * self.r1
        return flat // (4 * DH), flat % (4 * DH) // DH, flat % DH


def silu_parts(values):
    sigma = 0.5 + 0.5 * jnp.tanh(0.5 * values)
    return sigma, sigma * (1.0 + values * (1.0 - sigma))


def halves(tile):
    low = lax.broadcasted_iota(jnp.int32, tile.shape, 1) < DH
    zero = jnp.zeros_like(tile)
    return jnp.concatenate([jnp.where(low, tile, zero), jnp.where(low, zero, tile)], axis=0)


def beside(tile):
    half = tile.shape[0] // 2
    return jnp.concatenate([tile[:half], tile[half:]], axis=1)


def row_sum(values):
    return jnp.sum(values, axis=0, keepdims=True)


def place_weights(z, w_ref, w1_ref, w2_ref):
    for d in range(z.n_data):
        head, part, first = z.block(d)
        for k in range(z.n_model):
            at = k * z.fw + head * DH + first
            w1_ref[part, at : at + z.r1, :] = w_ref[z.order(d), k, 0 : z.r1, :]
            if w2_ref is not None:
                at = k * z.fw + d * z.r2
                w2_ref[at : at + z.r2, :] = w_ref[z.order(d), k, z.r1 : z.r1 + z.r2, :]


def key_bias(bias_ref, bucket, length):
    table = jnp.sum(bias_ref[...], axis=0)
    hot = jnp.where(
        lax.broadcasted_iota(jnp.int32, (NB, LEN), 0) == bucket, 1.0, 0.0
    )
    rows = lax.dot_general(table, hot, NN, precision=highest, preferred_element_type=f32)
    inside = lax.broadcasted_iota(jnp.int32, (8, LEN), 1) < length
    return jnp.where(inside, 0.5 * rows, -1e30)


def front_kernel(
    z, len_ref, table_ref, f1_ref, f2_ref, bias_ref, owner_ref, local_ref, ids_ref, bucket_ref, gains_ref,
    wanted_ref, slot_ref, w_ref, bias_all_ref,
    x_ref, n1o_ref, q_ref, k_ref, v_ref, do_ref, ghu_ref, gres_ref, ga_ref, stat_ref,
    low_ref, req_ref, asked_ref, send_ref, got_ref, t2_ref, n1_ref, n2_ref, n3_ref, acc_ref, plane_ref, neg_ref,
    xf_ref, hu_ref, o_ref, carry_ref, kb_ref, w1_ref, w2_ref, gw2_ref, gneg_ref,
    ask_send, ask_recv, row_send, row_recv,
    wz_send, wz_recv, wc_send, wc_recv, wp_send, wp_recv, bz_send, bz_recv,
    n1_send, n1_recv, n2_send, n2_recv, n3_send, n3_recv, n4_send, n4_recv, n5_send, n5_recv,
):
    n_every, n_model, half = z.n_every, z.n_model, z.half
    mine = z.groups * CH
    d = lax.axis_index("dp")
    k = lax.axis_index("mp")
    me = d * n_model + k
    side = lax.rem(d, 2)
    chip = d // 2
    here = side * half + chip
    other = d + 1 - 2 * side
    barrier = pltpu.get_barrier_semaphore()

    def signal(i, carry):
        to = spot(lax.rem(me + i, n_every), n_model)
        pl.semaphore_signal(barrier, inc=1, device_id=to, device_id_type=MESH)
        return carry

    lax.fori_loop(1, n_every, signal, 0)

    micro = k // z.copies
    owner_row = owner_ref[micro].astype(f32)
    value_row = local_ref[micro].astype(f32) + 1.0
    high_row = jnp.floor(value_row * (1.0 / 32.0))
    low_row = value_row - 32.0 * high_row
    length = z.group_len
    earlier = jnp.where(
        lax.broadcasted_iota(jnp.int32, (length, length), 0)
        < lax.broadcasted_iota(jnp.int32, (length, length), 1), 1.0, 0.0
    ).astype(bf16)
    pieces = []
    for g in range(z.groups):
        lanes = slice(g * length, (g + 1) * length)
        own = owner_row[:, lanes]
        owner_at = lax.broadcasted_iota(jnp.int32, (n_every, length), 0).astype(f32)
        hot = jnp.where(owner_at == own, 1.0, 0.0)
        rank = row_sum(mm(hot.astype(bf16), earlier) * hot)
        place = own * CH + rank
        for b in range(length // TB):
            slot_ref[g * (length // TB) + b] = place[:, b * TB : (b + 1) * TB]
        ranks = lax.broadcasted_iota(jnp.int32, (CH, length), 0).astype(f32)
        rank_hot = jnp.where(ranks == rank, 1.0, 0.0).astype(bf16)
        high = mm((hot * high_row[:, lanes]).astype(bf16), rank_hot, NT_)
        lower = mm((hot * low_row[:, lanes]).astype(bf16), rank_hot, NT_)
        pieces.append(high * 32.0 + lower - 1.0)
    pieces.append(jnp.full((n_every, LANES - mine), -1.0, f32))
    wanted = jnp.concatenate(pieces, axis=1)
    for o in range(n_every):
        req_ref[o] = wanted[o : o + 1]

    pl.semaphore_wait(barrier, n_every - 1)

    def ask_copy(src, dst, to):
        return remote(
            req_ref.at[to], asked_ref.at[dst], ask_send.at[to], ask_recv.at[src], spot(to, n_model)
        )

    def ask(i, carry):
        to = lax.rem(me + i, n_every)
        ask_copy(me, me, to).start()
        return carry

    lax.fori_loop(1, n_every, ask, 0)
    asked_ref[me] = req_ref[me]

    take = (
        lax.broadcasted_iota(jnp.int32, (z.r1, 4 * z.fw), 1)
        == lax.broadcasted_iota(jnp.int32, (z.r1, 4 * z.fw), 0) + d * z.r1
    )
    w_ref[here, k, 0 : z.r1, :] = mm(
        jnp.where(take, 1.0, 0.0).astype(bf16), f1_ref[...].astype(bf16), NT_
    ).astype(bf16)
    take = (
        lax.broadcasted_iota(jnp.int32, (z.r2p, z.fw), 1)
        == lax.broadcasted_iota(jnp.int32, (z.r2p, z.fw), 0) + d * z.r2
    )
    w_ref[here, k, z.r1 :, :] = mm(
        jnp.where(take, 1.0, 0.0).astype(bf16), f2_ref[...].astype(bf16)
    ).astype(bf16)
    head = lax.broadcasted_iota(jnp.int32, (HEADS, NB), 0)
    bias_tile = jnp.zeros((HEADS, NB), f32)
    for r in range(z.heads_dev):
        bias_tile += jnp.where(head == k * z.heads_dev + r, bias_ref[r : r + 1, :], 0.0)
    bias_all_ref[k] = bias_tile

    def wz_copy(i, at, to):
        return remote(
            w_ref.at[here, at], w_ref.at[here, at], wz_send.at[i], wz_recv.at[at], (d, to)
        )

    def bz_copy(i, at, to):
        return remote(
            bias_all_ref.at[k], bias_all_ref.at[at], bz_send.at[i], bz_recv.at[at], (d, to)
        )

    for i in range(1, n_model):
        to = lax.rem(k + i, n_model)
        wz_copy(i, k, to).start()
        bz_copy(i, k, to).start()
    low_ref[...] = table_ref[...].astype(bf16)

    def row_copy(g, src, dst, to):
        return remote(
            send_ref.at[g, to], got_ref.at[g, dst], row_send.at[g, to], row_recv.at[g, src],
            spot(to, n_model),
        )

    def asked_all(i, carry):
        src = lax.rem(me + i, n_every)
        ask_copy(src, src, src).wait_recv()
        return carry

    lax.fori_loop(1, n_every, asked_all, 0)
    asked = asked_ref[...].reshape(n_every, LANES) + 1.0
    asked_high = jnp.floor(asked * (1.0 / 32.0))
    asked_low = (asked - 32.0 * asked_high).astype(bf16)
    asked_high = asked_high.astype(bf16)
    per = min(TB // CH, n_every)
    spread = jnp.where(
        lax.broadcasted_iota(jnp.int32, (per * CH, CH), 1)
        == lax.rem(lax.broadcasted_iota(jnp.int32, (per * CH, CH), 0), CH), 1.0, 0.0
    ).astype(bf16)
    turn = lax.broadcasted_iota(jnp.int32, (per * CH, n_every), 0) // CH
    asker = lax.broadcasted_iota(jnp.int32, (per * CH, n_every), 1)
    lane = lax.broadcasted_iota(jnp.int32, (per * CH, z.rows_dev), 1).astype(f32)
    turn_row = lax.broadcasted_iota(jnp.int32, (n_every, per * CH), 1) // CH
    asker_row = lax.broadcasted_iota(jnp.int32, (n_every, per * CH), 0)

    def serve(g):
        lanes = slice(g * CH, (g + 1) * CH)
        for b in range(n_every // per):
            at = mm(spread, asked_high[:, lanes], NT_) * 32.0 + mm(spread, asked_low[:, lanes], NT_)
            at = jnp.where(asker == turn + b * per, at, 0.0)
            column = jnp.sum(at, axis=1, keepdims=True) - 1.0
            row = mm(asked_high[:, lanes], spread, NT_) * 32.0 + mm(asked_low[:, lanes], spread, NT_)
            row = row_sum(jnp.where(asker_row == turn_row + b * per, row, 0.0)) - 1.0
            wanted_ref[g, :, b * per * CH : (b + 1) * per * CH] = row
            hot = jnp.where(lane == column, 1.0, 0.0).astype(bf16)
            found = mm(hot, low_ref[...]).astype(bf16)
            send_ref[g, b * per : (b + 1) * per] = found.reshape(per, CH, D)
        got_ref[g, me] = send_ref[g, me]

    def send_group(g):
        def send(i, carry):
            row_copy(g, me, me, lax.rem(me + i, n_every)).start()
            return carry

        lax.fori_loop(1, n_every, send, 0)

    def release(g):
        def follow(i, carry):
            at = lax.rem(me + i, n_every)
            row_copy(g - 2, at, at, at).wait_send()
            row_copy(g, me, me, at).start()
            return carry

        lax.fori_loop(1, n_every, follow, 0)

    serve(0)
    send_group(0)

    per_side = half * MB * z.rn
    span = MB * z.rn
    n_lane = lax.broadcasted_iota(jnp.int32, (TB, z.rows_dev), 1).astype(f32)

    def negatives(i, carry, first):
        at = first * (per_side // TB) + i
        columns = [cross(ids_ref[at * (TB // LANES) + j]) for j in range(TB // LANES)]
        column = jnp.concatenate(columns, axis=0) - (me * z.rows_dev).astype(f32)
        hot = jnp.where(n_lane == column, 1.0, 0.0).astype(bf16)
        t2_ref[first, pl.ds(pl.multiple_of(i * TB, TB), TB), :] = mm(hot, low_ref[...]).astype(bf16)
        return carry

    def wc_copy(i, at, to):
        return remote(
            w_ref.at[at], w_ref.at[at], wc_send.at[i], wc_recv.at[at], (2 * to + side, k)
        )

    def wp_copy(at):
        return remote(w_ref.at[at], w_ref.at[at], wp_send.at[at], wp_recv.at[at], (other, k))

    n1_copy = remote(t2_ref.at[1 - side], n1_ref, n1_send, n1_recv, (other, k))

    def n2_copy(i, at, to):
        return remote(
            acc_ref.at[pl.ds(pl.multiple_of(to * span, 16), span)], n2_ref.at[at],
            n2_send.at[i], n2_recv.at[at], (2 * to + side, k),
        )

    def n3_copy(i, at, to):
        return remote(
            plane_ref.at[to // z.copies], n3_ref.at[at], n3_send.at[i], n3_recv.at[at], (d, to)
        )

    def n4_copy(i, at, to):
        return remote(
            neg_ref.at[at], neg_ref.at[at], n4_send.at[i], n4_recv.at[at], (2 * to + side, k)
        )

    def n5_copy(at):
        return remote(neg_ref.at[at], neg_ref.at[at], n5_send.at[at], n5_recv.at[at], (other, k))

    for i in range(1, n_model):
        wz_copy(i, lax.rem(k + i, n_model), k).wait_recv()
    for i in range(1, half):
        wc_copy(i, here, lax.rem(chip + i, half)).start()
    wp_copy(here).start()
    lax.fori_loop(0, per_side // TB, functools.partial(negatives, first=1 - side), 0)
    n1_copy.start()
    lax.fori_loop(0, per_side // TB, functools.partial(negatives, first=side), 0)
    if z.groups > 1:
        serve(1)
        send_group(1)
    n1_copy.wait_recv()
    acc_ref[...] = t2_ref[side] + n1_ref[...]
    for i in range(1, half):
        n2_copy(i, chip, lax.rem(chip + i, half)).start()
    for g in range(2, z.groups):
        serve(g)

    length = len_ref[micro, 0]
    lead = (lax.rem(k, z.copies) == 0).astype(jnp.int32)
    gain_in = gains_ref[0:1, :]
    gain_attn = gains_ref[1:2, :]
    gain_out = gains_ref[2:3, :]
    for i in range(1, n_model):
        at = lax.rem(k + i, n_model)
        bz_copy(i, at, k).wait_recv()
    kb = key_bias(bias_all_ref, bucket_ref[micro], length)
    for j in range(NT):
        kb_ref[j] = kb[:, j * TB : (j + 1) * TB]
    xf_ref[LEN:, :] = jnp.zeros((8, D), f32)
    carry_ref[...] = jnp.zeros_like(carry_ref)
    stat_ref[...] = jnp.zeros_like(stat_ref)
    gw2_ref[...] = jnp.zeros_like(gw2_ref)
    gneg_ref[...] = jnp.zeros_like(gneg_ref)
    for i in range(1, half):
        from_chip = lax.rem(chip + i, half)
        wc_copy(i, side * half + from_chip, chip).wait_recv()
        wp_copy(side * half + from_chip).start()
    for i in range(half):
        wp_copy((1 - side) * half + i).wait_recv()
    place_weights(z, w_ref, w1_ref, w2_ref)

    def neg_one():
        total = acc_ref[pl.ds(pl.multiple_of(chip * span, 16), span), :]
        for i in range(1, half):
            from_chip = lax.rem(chip + i, half)
            n2_copy(i, from_chip, chip).wait_recv()
            total = total + n2_ref[from_chip]
        plane_ref[...] = total.reshape(MB, z.rn, D)
        for i in range(1, n_model):
            n3_copy(i, k, lax.rem(k + i, n_model)).start()

    def neg_two():
        total = plane_ref[micro]
        for i in range(1, n_model):
            at = lax.rem(k + i, n_model)
            n3_copy(i, at, k).wait_recv()
            total = total + n3_ref[at]
        neg_ref[here] = total
        for i in range(1, half):
            n4_copy(i, here, lax.rem(chip + i, half)).start()
        n5_copy(here).start()

    def neg_three():
        for i in range(1, half):
            at = side * half + lax.rem(chip + i, half)
            n4_copy(i, at, chip).wait_recv()
            n5_copy(at).start()

    def neg_four():
        for i in range(half):
            n5_copy((1 - side) * half + i).wait_recv()

    slots = z.slots

    def arrive(g):
        def wait(i, carry):
            at = lax.rem(me + i, n_every)
            row_copy(g, at, at, at).wait_recv()
            return carry

        lax.fori_loop(1, n_every, wait, 0)

    def inputs(i):
        rows = pl.ds(pl.multiple_of(i * TB, TB), TB)
        hot = lax.broadcasted_iota(jnp.int32, (slots, TB), 0).astype(f32) == slot_ref[i]
        found = got_ref[i * TB // z.group_len]
        x = mm(jnp.where(hot, 1.0, 0.0).astype(bf16), found.reshape(slots, D), TN)
        x_ref[rows, :] = x.astype(bf16)
        xf_ref[rows, :] = x
        factor = lax.rsqrt(jnp.mean(x * x, -1, keepdims=True) + epsilon)
        n1 = (x * factor * gain_in).astype(bf16)
        n1o_ref[rows, :] = n1
        hu_ref[rows, :] = mm(n1, w1_ref[0], NT_)
        for c, ref in ((1, v_ref), (2, q_ref), (3, k_ref)):
            hidden = mm(n1, w1_ref[c], NT_)
            act = (hidden * silu_parts(hidden)[0]).astype(bf16)
            if c == 2:
                act = act * jnp.asarray(0.5 * DH ** (-0.5), bf16)
            for p in range(PAIRS):
                ref[p, rows, :] = act[:, p * WIDE : (p + 1) * WIDE]

    scale = 2.0 * D ** (-0.5)
    in_row = lax.broadcasted_iota(jnp.int32, (2 * TB, TB), 0)
    in_col = lax.broadcasted_iota(jnp.int32, (2 * TB, TB), 1)
    causal = in_col <= lax.rem(in_row, TB)
    first_half = in_row < TB

    def attend(i):
        rows = pl.ds(pl.multiple_of(i * TB, TB), TB)
        place = lax.broadcasted_iota(jnp.int32, (TB, 1), 0) + i * TB
        inv = 1.0 / (place.astype(f32) + 1.0)
        inv2 = jnp.concatenate([inv, inv], axis=0)
        o_ref[:, rows, :] = jnp.zeros((PAIRS, TB, WIDE), f32)

        def part(j, masked):
            keys = pl.ds(pl.multiple_of(j * TB, TB), TB)
            kb = kb_ref[j]
            for p in range(PAIRS):
                kb2 = jnp.where(first_half, kb[2 * p : 2 * p + 1, :], kb[2 * p + 1 : 2 * p + 2, :])
                h = mm(halves(q_ref[p, rows, :]), k_ref[p, keys, :], NT_) + kb2
                w = (h + h * jnp.tanh(h)) * inv2
                if masked:
                    w = jnp.where(causal, w, 0.0)
                o_ref[p, rows, :] += mm(beside(w.astype(bf16)), halves(v_ref[p, keys, :]))

        def before(j, carry):
            part(j, False)
            return carry

        lax.fori_loop(0, i, before, 0)
        part(i, True)

    def lose(i):
        rows = pl.ds(pl.multiple_of(i * TB, TB), TB)
        place = lax.broadcasted_iota(jnp.int32, (TB, 1), 0) + i * TB
        o = jnp.concatenate([o_ref[p, rows, :] for p in range(PAIRS)], axis=1)
        factor_attn = lax.rsqrt(jnp.mean(o * o, -1, keepdims=True) + epsilon)
        na = o * factor_attn * gain_attn
        hu = hu_ref[rows, :]
        sigma, slope = silu_parts(hu)
        upper = hu * sigma
        gated = (na * upper).astype(bf16)
        y = xf_ref[rows, :] + mm(gated, w2_ref[...])
        factor_out = lax.rsqrt(jnp.mean(y * y, -1, keepdims=True) + epsilon)
        out = (y * factor_out * gain_out).astype(bf16)
        zf = out.astype(f32)
        after = xf_ref[pl.ds(pl.multiple_of(i * TB + TB, 8), 8), :]
        last = lax.broadcasted_iota(jnp.int32, (TB, 1), 0) == TB - 1
        target = jnp.where(last, after[0:1, :], pltpu.roll(xf_ref[rows, :], TB - 1, 0))
        neg_logits = mm(out, neg_ref[...].reshape(half * 2 * z.rn, D), NT_) * scale
        pos = jnp.sum(zf * target, -1, keepdims=True) * scale
        top = jnp.maximum(jnp.max(neg_logits, -1, keepdims=True), pos)
        neg_exp = jnp.exp(neg_logits - top)
        pos_exp = jnp.exp(pos - top)
        total = pos_exp + jnp.sum(neg_exp, -1, keepdims=True)
        live = jnp.where(place + 1 < length, 1.0, 0.0) * lead.astype(f32)
        per = (top + jnp.log(total) - pos) * live
        share = 1.0 / total
        gneg = (neg_exp * (share * live)).astype(bf16)
        gpos = (pos_exp * share - 1.0) * live
        gz = mm(gneg, neg_ref[...].reshape(half * 2 * z.rn, D)) * scale + gpos * target * scale
        gneg_ref[...] += mm(gneg, out, TN) * scale
        target_grad = gpos * zf * scale
        first = lax.broadcasted_iota(jnp.int32, (TB, 1), 0) == 0
        shifted = jnp.where(first, carry_ref[0:1, :], pltpu.roll(target_grad, 1, 0))
        carry_ref[0:1, :] = target_grad[TB - 1 : TB, :]
        scaled = gz * gain_out
        gy = factor_out * (
            scaled - y * factor_out * factor_out * jnp.mean(y * scaled, -1, keepdims=True)
        )
        gres_ref[rows, :] = gy + shifted
        low = gy.astype(bf16)
        gg = mm(low, w2_ref[...], NT_)
        gw2_ref[...] += mm(gated, low, TN)
        gnorm = gg * upper
        gup = gg * na
        og = gain_attn * gnorm
        inner = jnp.sum(o * og, -1, keepdims=True)
        go = factor_attn * (og - o * factor_attn * factor_attn * (inner / D))
        go = go.astype(bf16)
        for p in range(PAIRS):
            do_ref[p, rows, :] = go[:, p * WIDE : (p + 1) * WIDE]
        ghu_ref[rows, :] = (gup * slope).astype(bf16)
        stat_ref[1:2, :] += row_sum(gnorm * o * factor_attn)
        stat_ref[2:3, :] += row_sum(gz * y * factor_out)
        stat_ref[3:4, :] += jnp.broadcast_to(row_sum(per), (1, D))
        stat_ref[4:5, :] += jnp.broadcast_to(row_sum(live), (1, D))


    per_group = z.group_len // TB
    arrive(0)

    def last(i, carry):
        lose(i)
        return carry

    def after_one():
        neg_one()
        for g in range(3, z.groups):
            release(g)

    def after_two():
        neg_three()
        neg_four()
        lax.fori_loop(0, NT - 2, last, 0)

    def step(i, carry):
        if per_group == 1:
            pl.when(i > 0)(lambda: arrive(i))
        pl.when(i == NT - 2)(neg_two)
        inputs(i)
        attend(i)
        if z.groups > 2:
            pl.when(i == 0)(lambda: release(2))
        pl.when(i == 1)(after_one)
        pl.when(i == NT - 2)(after_two)
        return carry

    lax.fori_loop(0, NT, step, 0)
    lax.fori_loop(NT - 2, NT, last, 0)
    for dd in range(z.n_data):
        at = z.order(dd)
        for kk in range(z.n_model):
            piece = gw2_ref[kk * z.fw + dd * z.r2 : kk * z.fw + (dd + 1) * z.r2, :]
            if z.r2p > z.r2:
                piece = jnp.concatenate([piece, jnp.zeros((z.r2p - z.r2, D), f32)], axis=0)
            ga_ref[at, kk * z.r2p : (kk + 1) * z.r2p, :] = piece
        ga_ref[at, z.n_model * z.r2p :, :] = gneg_ref[at * z.rn : (at + 1) * z.rn, :]

    for i in range(half):
        wp_copy(side * half + i).wait_send()
        n5_copy(side * half + i).wait_send()
    for i in range(1, half):
        to = lax.rem(chip + i, half)
        wc_copy(i, here, to).wait_send()
        n2_copy(i, chip, to).wait_send()
        n4_copy(i, here, to).wait_send()
    for i in range(1, n_model):
        at = lax.rem(k + i, n_model)
        wz_copy(i, k, at).wait_send()
        n3_copy(i, k, at).wait_send()
        bz_copy(i, k, at).wait_send()
    n1_copy.wait_send()

    def finish(i, carry):
        at = lax.rem(me + i, n_every)
        ask_copy(at, at, at).wait_send()
        for g in range(max(0, z.groups - 2), z.groups):
            row_copy(g, at, at, at).wait_send()
        return carry

    lax.fori_loop(1, n_every, finish, 0)


def front(z, scalars, table, w_f1, w_f2, bias_tile, owner, local, ids, bucket, gains):
    sds = jax.ShapeDtypeStruct
    dma = pltpu.SemaphoreType.DMA
    vm = pltpu.VMEM
    per_side = z.half * MB * z.rn
    every, model, half, data = (z.n_every,), (z.n_model,), (z.half,), (z.n_data,)
    groups_every = (z.groups, z.n_every)
    pairs_shape = sds((PAIRS, LEN, WIDE), bf16)
    return pl.pallas_call(
        functools.partial(front_kernel, z),
        out_shape=(
            sds((z.groups, 1, z.slots), f32),
            sds((NT, 1, TB), f32),
            sds((z.n_data, z.n_model, z.rw, D), bf16),
            sds((z.n_model, 8, LANES), f32),
            sds((LEN, D), bf16), sds((LEN, D), bf16),
            pairs_shape, pairs_shape, pairs_shape, pairs_shape,
            sds((LEN, D), bf16), sds((LEN, D), f32),
            sds((z.n_data, z.ra, D), f32), sds((8, D), f32),
        ),
        in_specs=[pl.BlockSpec(memory_space=pltpu.SMEM)] + [VM] * 9,
        out_specs=(VM,) * 14,
        scratch_shapes=[
            vm(table.shape, bf16),
            vm((z.n_every, 1, LANES), f32),
            vm((z.n_every, 1, LANES), f32),
            vm((z.groups, z.n_every, CH, D), bf16),
            vm((z.groups, z.n_every, CH, D), bf16),
            vm((2, per_side, D), bf16),
            vm((per_side, D), bf16),
            vm((z.half, MB * z.rn, D), bf16),
            vm((z.n_model, z.rn, D), bf16),
            vm((per_side, D), bf16),
            vm((MB, z.rn, D), bf16),
            vm((z.n_data, z.rn, D), bf16),
            vm((LEN + 8, D), f32),
            vm((LEN, D), f32),
            vm((PAIRS, LEN, WIDE), f32),
            vm((8, D), f32),
            vm((NT, 8, TB), f32),
            vm((4, D, D), bf16),
            vm((D, D), bf16),
            vm((D, D), f32),
            vm((z.n_data * z.rn, D), f32),
            dma(every), dma(every), dma(groups_every), dma(groups_every),
            dma(model), dma(model), dma(half), dma(data), dma(data), dma(data), dma(model), dma(model),
            dma, dma, dma(half), dma(half), dma(model), dma(model), dma(half), dma(data), dma(data), dma(data),
        ],
        compiler_params=pltpu.CompilerParams(
            collective_id=0, has_side_effects=True, vmem_limit_bytes=LIMIT
        ),
        cost_estimate=pl.CostEstimate(
            flops=60_000_000_000, bytes_accessed=30_000_000, transcendentals=6_000_000
        ),
        name="front",
    )(scalars, table, w_f1, w_f2, bias_tile, owner, local, ids, bucket, gains)


def rear_kernel(
    z, len_ref, x_ref, n1_ref, q_ref, k_ref, v_ref, do_ref, ghu_ref, gres_ref, w_ref, bias_ref, bucket_ref,
    gains_ref, slot_ref, stat_in_ref, ga_ref, asked_ref, ids_ref,
    tg_ref, wg_ref, packs_ref, squares_ref,
    gh_ref, hid_ref, kb_ref, dq_ref, dk_ref, dv_ref, kt_ref, bs_ref, w1_ref, stat_ref, pack_ref, out_ref, gb_ref,
    got_ref, pa_ref, pb_ref, sa_ref, sb_ref, ca_ref, cb_ref, zs_ref, zr_ref, ng_ref, sq_ref,
    row_send, row_recv, pack_send, pack_recv,
    pa_send, pa_recv, pb_send, pb_recv, ca_send, ca_recv, cb_send, cb_recv,
    zw_send, zw_recv, zf_send, zf_recv, zn_send, zn_recv, gw_send, gw_recv, gn_send, gn_recv,
    hw_send, hw_recv, hn_send, hn_recv, sq_send, sq_recv,
):
    n_every, n_model, half = z.n_every, z.n_model, z.half
    slots = z.slots
    d = lax.axis_index("dp")
    k = lax.axis_index("mp")
    me = d * n_model + k
    side = lax.rem(d, 2)
    chip = d // 2
    here = side * half + chip
    other = d + 1 - 2 * side
    micro = k // z.copies
    barrier = pltpu.get_barrier_semaphore()

    def signal(i, carry):
        to = spot(lax.rem(me + i, n_every), n_model)
        pl.semaphore_signal(barrier, inc=1, device_id=to, device_id_type=MESH)
        return carry

    lax.fori_loop(1, n_every, signal, 0)

    pa_copy = remote(ga_ref.at[1 - side], pa_ref, pa_send, pa_recv, (other, k))

    def pb_copy(p):
        return remote(gb_ref.at[1 - side, p], pb_ref.at[p], pb_send.at[p], pb_recv.at[p], (other, k))

    def row_copy(g, src, dst, to):
        return remote(
            out_ref.at[g, to], got_ref.at[g, dst], row_send.at[g, to], row_recv.at[g, src],
            spot(to, n_model),
        )

    def pack_copy(src, dst, to):
        return remote(
            pack_ref, packs_ref.at[dst], pack_send.at[to], pack_recv.at[src], spot(to, n_model)
        )

    def ca_copy(i, at, to):
        return remote(
            sa_ref.at[to], ca_ref.at[at], ca_send.at[i], ca_recv.at[at], (2 * to + side, k)
        )

    def cb_copy(p, i, at, to):
        return remote(
            sb_ref.at[p, to], cb_ref.at[p, at], cb_send.at[p, i], cb_recv.at[p, at], (2 * to + side, k)
        )

    def zn_copy(i, at, to):
        return remote(
            ng_ref.at[here, at], ng_ref.at[here, at], zn_send.at[i], zn_recv.at[at], (d, to)
        )

    def zw_copy(at, to):
        part = pl.ds(0, z.r1)
        return remote(
            zs_ref.at[to, part], zr_ref.at[at, part], zw_send.at[to], zw_recv.at[at], (d, to)
        )

    def zf_copy(at, to):
        part = pl.ds(z.r1, z.r2p)
        return remote(
            zs_ref.at[to, part], zr_ref.at[at, part], zf_send.at[to], zf_recv.at[at], (d, to)
        )

    def gw_copy(i, at, to):
        return remote(
            wg_ref.at[at], wg_ref.at[at], gw_send.at[i], gw_recv.at[at], (2 * to + side, k)
        )

    def gn_copy(i, at, to):
        return remote(
            ng_ref.at[at], ng_ref.at[at], gn_send.at[i], gn_recv.at[at], (2 * to + side, k)
        )

    def hw_copy(at):
        return remote(wg_ref.at[at], wg_ref.at[at], hw_send.at[at], hw_recv.at[at], (other, k))

    def hn_copy(at):
        return remote(ng_ref.at[at], ng_ref.at[at], hn_send.at[at], hn_recv.at[at], (other, k))

    def sq_copy(src, dst, to):
        return remote(
            sq_ref, squares_ref.at[dst], sq_send.at[to], sq_recv.at[src], spot(to, n_model)
        )

    def chips_a():
        pa_copy.wait_recv()
        sa_ref[...] = (ga_ref[side] + pa_ref[...]).astype(bf16)
        for i in range(1, half):
            ca_copy(i, chip, lax.rem(chip + i, half)).start()

    def chips_b(p):
        pb_copy(p).wait_recv()
        sb_ref[p] = (gb_ref[side, p] + pb_ref[p]).astype(bf16)
        for i in range(1, half):
            cb_copy(p, i, chip, lax.rem(chip + i, half)).start()

    def planes_a():
        total = sa_ref[chip].astype(f32)
        for i in range(1, half):
            at = lax.rem(chip + i, half)
            ca_copy(i, at, chip).wait_recv()
            total = total + ca_ref[at].astype(f32)
        ng_ref[here, k] = total[n_model * z.r2p :].astype(bf16)
        zs_ref[:, z.r1 :, :] = total[: n_model * z.r2p].reshape(n_model, z.r2p, D)
        for i in range(1, n_model):
            to = lax.rem(k + i, n_model)
            zn_copy(i, k, to).start()
            zf_copy(k, to).start()

    def planes_b(p):
        total = sb_ref[p, chip].astype(f32)
        for i in range(1, half):
            at = lax.rem(chip + i, half)
            cb_copy(p, i, at, chip).wait_recv()
            total = total + cb_ref[p, at].astype(f32)
        for i in range(z.npp):
            to = p * z.npp + i
            zs_ref[to, : z.r1, :] = total[i * z.r1 : (i + 1) * z.r1]
            pl.when(k != to)(lambda to=to: zw_copy(k, to).start())

    def spread_a():
        for i in range(1, n_model):
            zn_copy(i, lax.rem(k + i, n_model), k).wait_recv()
        for i in range(1, half):
            gn_copy(i, here, lax.rem(chip + i, half)).start()
        hn_copy(here).start()

    def swap_a():
        for i in range(1, half):
            at = side * half + lax.rem(chip + i, half)
            gn_copy(i, at, chip).wait_recv()
            hn_copy(at).start()

    gain_in = gains_ref[0:1, :]
    place_weights(z, w_ref, w1_ref, None)
    kb_ref[...] = key_bias(bias_ref, bucket_ref[micro], len_ref[micro, 0]).T

    def inputs(i, carry):
        rows = pl.ds(pl.multiple_of(i * TB, TB), TB)
        for c in (1, 2, 3):
            hid_ref[c - 1, rows, :] = mm(n1_ref[rows, :], w1_ref[c], NT_)
        return carry

    lax.fori_loop(0, NT, inputs, 0)
    bs_ref[...] = jnp.zeros_like(bs_ref)
    in_row = lax.broadcasted_iota(jnp.int32, (2 * TB, TB), 0)
    in_col = lax.broadcasted_iota(jnp.int32, (2 * TB, TB), 1)
    causal = lax.rem(in_row, TB) <= in_col
    ones_lane = lax.broadcasted_iota(jnp.int32, (2 * TB, LANES), 1)
    ones_half = lax.broadcasted_iota(jnp.int32, (2 * TB, LANES), 0) >= TB
    stat_ref[...] = jnp.zeros_like(stat_ref)
    per_group = z.group_len // TB

    def outputs(i):
        rows = pl.ds(pl.multiple_of(i * TB, TB), TB)
        gn = mm(ghu_ref[rows, :], w1_ref[0])
        for c in (1, 2, 3):
            gn += mm(gh_ref[c - 1, rows, :], w1_ref[c])
        x = x_ref[rows, :].astype(f32)
        factor = lax.rsqrt(jnp.mean(x * x, -1, keepdims=True) + epsilon)
        scaled = gn * gain_in
        gx = factor * (scaled - x * factor * factor * jnp.mean(x * scaled, -1, keepdims=True))
        gx = (gx + gres_ref[rows, :]).astype(bf16)
        stat_ref[0:1, :] += row_sum(gn * x * factor)
        group = i // per_group
        hot = lax.broadcasted_iota(jnp.int32, (slots, TB), 0).astype(f32) == slot_ref[i]
        mine = mm(jnp.where(hot, 1.0, 0.0).astype(bf16), gx).astype(bf16)
        mine = mine.reshape(z.n_every, CH, D)
        if per_group == 1:
            out_ref[group] = mine
        else:
            out_ref[group] = jnp.where(lax.rem(i, per_group) == 0, mine, out_ref[group] + mine)

    def send_group(g):
        def send(i, carry):
            row_copy(g, me, me, lax.rem(me + i, n_every)).start()
            return carry

        lax.fori_loop(1, n_every, send, 0)
        got_ref[g, me] = out_ref[g, me]

    def weights_grad(p):
        lanes = slice(p * WIDE, (p + 1) * WIDE)
        for c in range(4):
            left = ghu_ref[:, lanes] if c == 0 else gh_ref[c - 1, :, lanes]
            grads = mm(left, n1_ref[...], TN)
            for side_head in range(2):
                head = 2 * p + side_head
                for dd in range(z.n_data):
                    own_head, part, first = z.block(dd)
                    if part == c and own_head == head % z.heads_dev:
                        at = head // z.heads_dev - p * z.npp
                        gb_ref[dd % 2, p, dd // 2, at * z.r1 : (at + 1) * z.r1, :] = grads[
                            side_head * DH + first : side_head * DH + first + z.r1
                        ]
        pb_copy(p).start()

    early = range(PAIRS - SPAN)
    late = range(PAIRS - SPAN, PAIRS)

    def first_hook():
        for p in early:
            chips_b(p)
        spread_a()

    def second_hook():
        for p in early:
            planes_b(p)

    def late_weights():
        for p in late:
            weights_grad(p)

    pl.semaphore_wait(barrier, n_every - 1)
    pa_copy.start()

    def keys_of(p, j):
        keys = pl.ds(pl.multiple_of(j * TB, TB), TB)
        at = p % SPAN
        kt = k_ref[p, keys, :].astype(f32).T
        low = lax.broadcasted_iota(jnp.int32, kt.shape, 0) < DH
        kt_ref[at] = jnp.concatenate(
            [jnp.where(low, kt, 0.0), jnp.where(low, 0.0, kt)], axis=1
        ).astype(bf16)
        dk_ref[at] = jnp.zeros((TB, WIDE + LANES), f32)
        dv_ref[at] = jnp.zeros((TB, WIDE), f32)

    def part(p, i, j, masked):
        keys = pl.ds(pl.multiple_of(j * TB, TB), TB)
        rows = pl.ds(pl.multiple_of(i * TB, TB), TB)
        at = p % SPAN
        q = q_ref[p, rows, :]
        do = do_ref[p, rows, :]
        kb = jnp.concatenate(
            [kb_ref[keys, 2 * p : 2 * p + 1], kb_ref[keys, 2 * p + 1 : 2 * p + 2]], axis=0
        )
        mark = jnp.where(
            ones_lane == jnp.where(ones_half, 2 * p + 1, 2 * p), 1.0, 0.0
        ).astype(bf16)
        place = lax.broadcasted_iota(jnp.int32, (1, TB), 1) + i * TB
        inv = 1.0 / (place.astype(f32) + 1.0)
        h = mm(halves(k_ref[p, keys, :]), q, NT_) + kb
        t = jnp.tanh(h)
        m = h * t
        w = (h + m) * inv
        ds = mm(halves(v_ref[p, keys, :]), do, NT_) * ((1.0 + t) * (0.5 * inv)) * (1.0 + h - m)
        if masked:
            w = jnp.where(causal, w, 0.0)
            ds = jnp.where(causal, ds, 0.0)
        ds = ds.astype(bf16)
        dv_ref[at] += mm(beside(w.astype(bf16)), halves(do))
        dk_ref[at] += mm(beside(ds), jnp.concatenate([halves(q), mark], axis=1))
        dq_ref[at, i] += mm(kt_ref[at], ds)

    def keys_end(p, j):
        keys = pl.ds(pl.multiple_of(j * TB, TB), TB)
        lanes = slice(p * WIDE, (p + 1) * WIDE)
        at = p % SPAN
        slope_v = silu_parts(hid_ref[0, keys, lanes])[1]
        slope_k = silu_parts(hid_ref[2, keys, lanes])[1]
        slope_q = silu_parts(hid_ref[1, keys, lanes])[1]
        gh_ref[0, keys, lanes] = (dv_ref[at] * slope_v).astype(bf16)
        gh_ref[2, keys, lanes] = (dk_ref[at, :, :WIDE] * 2.0 * slope_k).astype(bf16)
        gh_ref[1, keys, lanes] = (dq_ref[at, j].T * DH ** (-0.5) * slope_q).astype(bf16)
        bs_ref[keys, :] += dk_ref[at, :, WIDE:]

    for phase in range(PAIRS // SPAN):
        pairs = range(phase * SPAN, (phase + 1) * SPAN)
        final = phase == PAIRS // SPAN - 1
        dq_ref[...] = jnp.zeros_like(dq_ref)

        def keys_step(j, carry, pairs=pairs, final=final, phase=phase):
            for p in pairs:
                keys_of(p, j)
            for p in pairs:
                part(p, j, j, True)

            def later(i, inner):
                for p in pairs:
                    part(p, i, j, False)
                return inner

            lax.fori_loop(j + 1, NT, later, 0)
            for p in pairs:
                keys_end(p, j)
            if phase == 0:
                pl.when(j == 0)(chips_a)
                pl.when(j == 2)(planes_a)
            if final:
                pl.when(j == NT - 1)(late_weights)
                pl.when(j == 0)(first_hook)
                outputs(j)
                if per_group == 1:
                    send_group(j)
                pl.when(j == 1)(second_hook)
                pl.when(j == 2)(swap_a)
            return carry

        lax.fori_loop(0, NT, keys_step, 0)
        if not final:
            for p in pairs:
                weights_grad(p)

    if per_group > 1:
        for g in range(z.groups):
            send_group(g)
    hot = jnp.where(
        lax.broadcasted_iota(jnp.int32, (NB, LEN), 0) == bucket_ref[micro], 1.0, 0.0
    )
    bias_grad = lax.dot_general(hot, bs_ref[...], NN, precision=highest, preferred_element_type=f32)
    for i in range(D // LANES):
        lanes = slice(i * LANES, (i + 1) * LANES)
        pack_ref[i : i + 1] = stat_ref[0:1, lanes]
        pack_ref[4 + i : 5 + i] = stat_in_ref[1:2, lanes]
        pack_ref[8 + i : 9 + i] = stat_in_ref[2:3, lanes]
    pack_ref[12:14] = stat_in_ref[3:5, :LANES]
    pack_ref[14:16] = jnp.zeros((2, LANES), f32)
    pack_ref[16:24] = bias_grad.T[0:8, :]
    packs_ref[me] = pack_ref[...]

    def pack_all(i, carry):
        pack_copy(me, me, lax.rem(me + i, n_every)).start()
        return carry

    lax.fori_loop(1, n_every, pack_all, 0)

    tg_ref[...] = jnp.zeros_like(tg_ref)
    wide = min(TB, slots)
    ask_at = lax.broadcasted_iota(jnp.int32, (z.rows_dev, wide), 0).astype(f32)

    def collect(g):
        def wait(i, carry):
            at = lax.rem(me + i, n_every)
            row_copy(g, at, at, at).wait_recv()
            return carry

        lax.fori_loop(1, n_every, wait, 0)
        for b in range(slots // wide):
            asked = asked_ref[g][:, b * wide : (b + 1) * wide]
            hot = jnp.where(ask_at == asked, 1.0, 0.0).astype(bf16)
            rows = got_ref[g, b * (wide // CH) : (b + 1) * (wide // CH)].reshape(wide, D)
            tg_ref[...] += mm(hot, rows)

    neg_rows = n_model * z.rn
    row_at = lax.broadcasted_iota(jnp.int32, (z.rows_dev, neg_rows), 0).astype(f32)
    base = (me * z.rows_dev).astype(f32)

    def negatives(at):
        hot = jnp.where(row_at == ids_ref[at] - base, 1.0, 0.0).astype(bf16)
        tg_ref[...] += mm(hot, ng_ref[at].reshape(neg_rows, D))

    for p in late:
        chips_b(p)
    collect(0)
    for p in late:
        planes_b(p)
    for i in range(half):
        negatives(side * half + i)
    for i in range(half):
        hn_copy((1 - side) * half + i).wait_recv()
        negatives((1 - side) * half + i)
    for g in range(1, max(1, z.groups - 1)):
        collect(g)
    total = zs_ref[k]
    for i in range(1, n_model):
        at = lax.rem(k + i, n_model)
        zw_copy(at, k).wait_recv()
        zf_copy(at, k).wait_recv()
        total = total + zr_ref[at]
    wg_ref[here] = total
    for i in range(1, half):
        gw_copy(i, here, lax.rem(chip + i, half)).start()
    hw_copy(here).start()
    if z.groups > 1:
        collect(z.groups - 1)

    table_grad = tg_ref[...]
    slice_grad = wg_ref[here]
    squares = row_sum(table_grad * table_grad) + row_sum(slice_grad * slice_grad)
    sq_ref[...] = sum(squares[:, i * LANES : (i + 1) * LANES] for i in range(D // LANES))
    squares_ref[me] = sq_ref[...]

    def share(i, carry):
        to = lax.rem(me + i, n_every)
        sq_copy(me, me, to).start()
        return carry

    lax.fori_loop(1, n_every, share, 0)
    for i in range(1, half):
        at = side * half + lax.rem(chip + i, half)
        gw_copy(i, at, chip).wait_recv()
        hw_copy(at).start()
    for i in range(half):
        hw_copy((1 - side) * half + i).wait_recv()
        hw_copy(side * half + i).wait_send()
        hn_copy(side * half + i).wait_send()
    for i in range(1, half):
        to = lax.rem(chip + i, half)
        ca_copy(i, chip, to).wait_send()
        for p in range(PAIRS):
            cb_copy(p, i, chip, to).wait_send()
        gn_copy(i, here, to).wait_send()
        gw_copy(i, here, to).wait_send()
    for i in range(1, n_model):
        to = lax.rem(k + i, n_model)
        zn_copy(i, k, to).wait_send()
        zw_copy(k, to).wait_send()
        zf_copy(k, to).wait_send()
    pa_copy.wait_send()
    for p in range(PAIRS):
        pb_copy(p).wait_send()

    def finish(i, carry):
        at = lax.rem(me + i, n_every)
        for g in range(z.groups):
            row_copy(g, at, at, at).wait_send()
        pack_copy(at, at, at).wait_send()
        pack_copy(at, at, at).wait_recv()
        sq_copy(at, at, at).wait_send()
        sq_copy(at, at, at).wait_recv()
        return carry

    lax.fori_loop(1, n_every, finish, 0)


def rear(
    z, scalars, x, n1, q, k, v, do, ghu, gres, w, bias, bucket, gains, slot, stat, ga, asked, ids
):
    sds = jax.ShapeDtypeStruct
    dma = pltpu.SemaphoreType.DMA
    vm = pltpu.VMEM
    every, model, half, data = (z.n_every,), (z.n_model,), (z.half,), (z.n_data,)
    groups_every = (z.groups, z.n_every)
    pairs, pairs_half = (PAIRS,), (PAIRS, z.half)
    rows_b = z.npp * z.r1
    return pl.pallas_call(
        functools.partial(rear_kernel, z),
        out_shape=(
            sds((z.rows_dev, D), f32),
            sds((z.n_data, z.rw, D), f32),
            sds((z.n_every, 24, LANES), f32),
            sds((z.n_every, 1, LANES), f32),
        ),
        in_specs=[pl.BlockSpec(memory_space=pltpu.SMEM)] + [VM] * 17,
        out_specs=(VM,) * 4,
        scratch_shapes=[
            vm((3, LEN, D), bf16),
            vm((3, LEN, D), f32),
            vm((LEN, 8), f32),
            vm((SPAN, NT, WIDE, TB), f32),
            vm((SPAN, TB, WIDE + LANES), f32),
            vm((SPAN, TB, WIDE), f32),
            vm((SPAN, WIDE, 2 * TB), bf16),
            vm((LEN, LANES), f32),
            vm((4, D, D), bf16),
            vm((8, D), f32),
            vm((24, LANES), f32),
            vm((z.groups, z.n_every, CH, D), bf16),
            vm((2, PAIRS, z.half, rows_b, D), f32),
            vm((z.groups, z.n_every, CH, D), bf16),
            vm((z.half, z.ra, D), f32),
            vm((PAIRS, z.half, rows_b, D), f32),
            vm((z.half, z.ra, D), bf16),
            vm((PAIRS, z.half, rows_b, D), bf16),
            vm((z.half, z.ra, D), bf16),
            vm((PAIRS, z.half, rows_b, D), bf16),
            vm((z.n_model, z.rw, D), f32),
            vm((z.n_model, z.rw, D), f32),
            vm((z.n_data, z.n_model, z.rn, D), bf16),
            vm((1, LANES), f32),
            dma(groups_every), dma(groups_every), dma(every), dma(every),
            dma, dma, dma(pairs), dma(pairs), dma(half), dma(half), dma(pairs_half), dma(pairs_half),
            dma(model), dma(model), dma(model), dma(model), dma(model), dma(model),
            dma(half), dma(data), dma(half), dma(data),
            dma(data), dma(data), dma(data), dma(data), dma(every), dma(every),
        ],
        compiler_params=pltpu.CompilerParams(
            collective_id=1, has_side_effects=True, vmem_limit_bytes=LIMIT
        ),
        cost_estimate=pl.CostEstimate(
            flops=60_000_000_000, bytes_accessed=30_000_000, transcendentals=6_000_000
        ),
        name="rear",
    )(scalars, x, n1, q, k, v, do, ghu, gres, w, bias, bucket, gains, slot, stat, ga, asked, ids)


def adam_step(weight, grad, first, second, rate, decay):
    first_new = beta_one * first + (1.0 - beta_one) * grad
    second_new = beta_two * second + (1.0 - beta_two) * grad * grad
    fix_one = 1.0 / (1.0 - beta_one**STEP)
    fix_two = 1.0 / (1.0 - beta_two**STEP)
    move = first_new * fix_one / (jnp.sqrt(second_new * fix_two) + adam_floor) + decay * weight
    return (weight - rate * move, first_new, second_new)


def settle_kernel(
    z, squares_ref, packs_ref, wg_ref, tg_ref, t_ref, tm_ref, tv_ref, a_ref, am_ref, av_ref,
    b_ref, bm_ref, bv_ref, c_ref, cm_ref, cv_ref, e_ref, em_ref, ev_ref,
    t_out, tm_out, tv_out, tl_out, a_out, am_out, av_out, al_out, b_out, bm_out, bv_out, bl_out,
    c_out, cm_out, cv_out, e_out, em_out, ev_out, loss_out, count_out, norm_out, factor_ref, one_ref,
):
    def update(grad, refs, outs, rate, decay):
        new, first, second = adam_step(refs[0][...], grad, refs[1][...], refs[2][...], rate, decay)
        outs[0][...] = new
        outs[1][...] = first
        outs[2][...] = second
        if len(outs) > 3:
            outs[3][...] = new.astype(bf16)

    @pl.when(pl.program_id(0) == 0)
    def _():
        packs = jnp.sum(packs_ref[...], axis=0)
        gain_grad = jnp.concatenate(
            [
                jnp.concatenate([packs[4 * r + i : 4 * r + i + 1] for i in range(D // LANES)], axis=1)
                for r in range(3)
            ],
            axis=0,
        )
        bias_all = packs[16:24]
        squares = jnp.sum(squares_ref[...], axis=0) + row_sum(packs[0:12] * packs[0:12])
        squares = squares + row_sum(bias_all * bias_all)
        norm = jnp.sqrt(jnp.sum(squares, axis=1, keepdims=True))
        factor = jnp.minimum(1.0, clip_at / norm)
        factor_ref[...] = jnp.broadcast_to(factor, factor_ref.shape)
        loss_out[...] = packs[12:13, 0:1]
        count_out[...] = packs[13:14, 0:1]
        norm_out[...] = norm
        one = jnp.concatenate([wg_ref[z.order(d), 0 : z.r1] for d in range(z.n_data)], axis=0)
        two = jnp.concatenate(
            [wg_ref[z.order(d), z.r1 : z.r1 + z.r2] for d in range(z.n_data)], axis=0
        )
        one_ref[...] = one.T * factor
        update(two * factor, (b_ref, bm_ref, bv_ref), (b_out, bm_out, bv_out, bl_out), 0.04, 0.1)
        update(gain_grad * factor, (c_ref, cm_ref, cv_ref), (c_out, cm_out, cv_out), 0.5, 0.0)
        head = lax.broadcasted_iota(jnp.int32, bias_all.shape, 0)
        first_head = lax.axis_index("mp") * z.heads_dev
        mine = [
            row_sum(jnp.where(head == first_head + r, bias_all, 0.0)) for r in range(z.heads_dev)
        ]
        bias_grad = jnp.concatenate(mine, axis=0)
        update(bias_grad * factor, (e_ref, em_ref, ev_ref), (e_out, em_out, ev_out), 1.0, 0.0)

    size = a_ref.shape[0]
    rows = pl.ds(pl.multiple_of(pl.program_id(0) * size, size), size)
    update(one_ref[rows, :], (a_ref, am_ref, av_ref), (a_out, am_out, av_out, al_out), 0.04, 0.1)
    update(
        tg_ref[...] * factor_ref[0:1, 0:1], (t_ref, tm_ref, tv_ref), (t_out, tm_out, tv_out, tl_out), 0.5, 0.1
    )


def settle(z, squares, packs, wg, tg, table, f1, f2, gains, bias):
    sds = jax.ShapeDtypeStruct
    rows = next(r for r in range(112, 0, -16) if z.rows_dev % r == 0)
    blocks = z.rows_dev // rows
    steps = next(n for n in range(blocks, 512) if D % n == 0 and D // n % 16 == 0)
    block = pl.BlockSpec((rows, D), lambda i: (jnp.minimum(i, blocks - 1), 0))
    part = pl.BlockSpec((D // steps, 4 * z.fw), lambda i: (i, 0))

    def like(array, dtype=f32):
        return sds(array.shape, dtype)

    return pl.pallas_call(
        functools.partial(settle_kernel, z),
        grid=(steps,),
        out_shape=(
            like(tg), like(tg), like(tg), like(tg, bf16),
            like(f1[0]), like(f1[0]), like(f1[0]), like(f1[0], bf16),
            like(f2[0]), like(f2[0]), like(f2[0]), like(f2[0], bf16),
            like(gains[0]), like(gains[0]), like(gains[0]),
            like(bias[0]), like(bias[0]), like(bias[0]),
            sds((1, 1), f32), sds((1, 1), f32), sds((1, 1), f32),
        ),
        in_specs=[VM] * 3 + [block] * 4 + [part] * 3 + [VM] * 9,
        out_specs=(block,) * 4 + (part,) * 4 + (VM,) * 13,
        scratch_shapes=[pltpu.VMEM((8, LANES), f32), pltpu.VMEM((D, 4 * z.fw), f32)],
        compiler_params=pltpu.CompilerParams(vmem_limit_bytes=LIMIT),
        cost_estimate=pl.CostEstimate(
            flops=20 * z.rows_dev * D, bytes_accessed=20_000_000, transcendentals=1_000_000
        ),
        name="settle",
    )(squares, packs, wg, tg, *table, *f1, *f2, *gains, *bias)


def pick(array, index):
    return lax.dynamic_index_in_dim(array, index, 0, keepdims=False)


def per_device(
    lengths, owners, item_rows, buckets, negatives, table, table_m, table_v, w_f1, f1_m, f1_v,
    w_f2, f2_m, f2_v, gains, gains_m, gains_v, bias, bias_m, bias_v,
):
    n_model = lax.axis_size("mp")
    n_data = lax.axis_size("dp")
    z = Sizes(n_data, n_model, bias.shape[0], table.shape[0], negatives.shape[1])
    ids = negatives.astype(f32).reshape(MB, n_data, z.rn).transpose(1, 0, 2)
    ids_rows = ids.reshape(-1, 1, LANES)
    ids_cols = jnp.repeat(ids, z.copies, axis=1).reshape(n_data, 1, n_model * z.rn)

    asked, slot, w, bias_all, x, n1, q, k, v, do, ghu, gres, ga, stat_a = front(
        z, lengths, table, w_f1, w_f2, bias, owners.reshape(MB, 1, LEN), item_rows, ids_rows,
        buckets, gains,
    )
    table_grad, wg, packs, squares = rear(
        z, lengths, x, n1, q, k, v, do, ghu, gres, w, bias_all, buckets, gains, slot, stat_a,
        ga.reshape(2, z.half, z.ra, D), asked, ids_cols,
    )
    *new, loss_sum, loss_count, grad_norm = settle(
        z, squares, packs, wg, table_grad, (table, table_m, table_v), (w_f1, f1_m, f1_v),
        (w_f2, f2_m, f2_v), (gains, gains_m, gains_v), (bias, bias_m, bias_v),
    )
    return (loss_sum.reshape(()), loss_count.reshape(()), grad_norm.reshape(()), *new)


def solution(mesh):
    rows, cols = P(("dp", "mp"), None), P(None, "mp")
    heads = P("mp", None)
    in_specs = (
        P(None, "dp"), P(None, "dp", None, None), P(None, "dp", None), P(None, "dp", None), P(),
        rows, rows, rows, cols, cols, cols, heads, heads, heads, P(), P(), P(), heads, heads, heads,
    )
    out_specs = (
        P(), P(), P(), rows, rows, rows, rows, cols, cols, cols, cols,
        heads, heads, heads, heads, P(), P(), P(), heads, heads, heads,
    )
    return jax.shard_map(
        per_device, mesh=mesh, in_specs=in_specs, out_specs=out_specs, check_vma=False
    )
```
